128 devices in a mesh: segment: 4 (over z_lo, core), lon: 8 (over z_hi, y), lat: 4 (over x).
Axes of the slice: x: 4, y: 4, z: 4 (z_hi: 2, z_lo: 2; z = z_hi * 2 + z_lo), core: 2. Of those that a mesh axis runs over, the one named last changes fastest.
Arguments:
- latents: bfloat16 [4, 2, 24, 192, 512], P(None, None, 'lat', 'lon'), may hold values from -6 to 6
- segment_depth: int32 [4], replicated, may hold values from 1 to 2, as said below
- shift_flags: int32 [8, 2], P('segment'), may hold values from 0 to 1
- w_qkv: bfloat16 [8, 512, 1536], P('segment'), may hold values from -0.25 to 0.25
- w_out: bfloat16 [8, 512, 512], P('segment'), may hold values from -0.25 to 0.25
- w_up: bfloat16 [8, 512, 2048], P('segment'), may hold values from -0.25 to 0.25
- w_down: bfloat16 [8, 2048, 512], P('segment'), may hold values from -0.125 to 0.125
- gains: float32 [8, 2, 512], P('segment'), may hold values from 0.25 to 1.75
- logit_scale: float32 [8, 8], P('segment'), may hold values from 2 to 100
Outputs:
- sections: float32 [4, 4, 2, 24, 192, 512], P('segment', None, None, 'lat', 'lon')
The draws below stay inside these ranges and needn't reach their ends.
Inputs may be any that keep to these rules, and one draw needn't show every extreme that they name: `segment_depth`: at least one section applies 2 layers and at least one applies a single layer.
All inputs are finite; a program needn't handle non-finite values.
Results may differ from the reference program's by a relative error of at most 0.035.
The reference program's roundings to bfloat16 on the way count: a program that leaves them out, or rounds other values in their place, can miss the bound.
Values may be sent and summed in bfloat16 or wider, within the bound.
A program may use at most 192 MiB of HBM per device.

```python
import jax
import jax.numpy as jnp
from jax import lax

D = 512
HEADS = 8
FF = 2048
HD = 64
W_LAT = 6
W_LON = 12
LEV = 2
MAXD = 2
M = 4
NLAT = 24
NLON = 192
LAYERS = 8
N_SEGMENT = 4


def draw_segment_depth(key, part):
    key = jax.random.fold_in(key, 1)
    first, second = jax.random.split(key)
    depth = jax.random.randint(first, (N_SEGMENT,), 1, MAXD + 1)
    order = jax.random.permutation(second, jnp.arange(N_SEGMENT, dtype=jnp.int32))
    places = jnp.arange(N_SEGMENT, dtype=jnp.int32)
    depth = jnp.where(places == order[0], MAXD, depth)
    depth = jnp.where(places == order[1], 1, depth)
    return depth.astype(jnp.int32)


def draw_logit_scale(key, part):
    key = jax.random.fold_in(key, 2)
    first = jax.random.fold_in(key, 0)
    spread = jax.random.uniform(first, (LAYERS, HEADS), jnp.float32)
    scale = 2.0 * jnp.exp(spread * jnp.log(6.0))
    return scale.astype(jnp.float32)


def with_ends(entries, stream_key, smallest, top_value):
    longest = entries.shape.index(max(entries.shape))
    spots = []
    for shift in (0, 1):
        where = [jax.random.randint(jax.random.fold_in(stream_key, axis), (), 0, length) for axis, length in enumerate(entries.shape)]
        where[longest] = (where[longest] + shift) % entries.shape[longest]
        spots.append(tuple(where))
    return entries.at[spots[0]].set(smallest).at[spots[1]].set(top_value)


def level_of(key, extent, cuts, least, largest):
    def one(dim, parts):
        heights = jax.random.uniform(jax.random.fold_in(jax.random.fold_in(key, 6), dim), (parts,), jnp.float32, least / len(cuts), largest / len(cuts))
        return jnp.repeat(jnp.exp(heights), extent[dim] // parts).reshape((-1,) + (1,) * (len(extent) - dim - 1))

    loudness = one(*cuts[0])
    for cut in cuts[1:]:
        loudness = loudness * one(*cut)
    return loudness


def scatter_about(stream_key, shape, width, reach, cuts=(), held_as=jnp.bfloat16):
    level = level_of(stream_key, shape, cuts, -0.22, 0.18) if cuts else 1.0
    values = jax.random.normal(stream_key, shape, jnp.float32) * width * level
    return jnp.minimum(jnp.maximum(values, -reach), reach).astype(held_as)


def setup_inputs(seed: int = 0) -> dict:
    seeds = jax.random.split(jax.random.key(seed), 10)
    latents = scatter_about(seeds[0], (M, LEV, NLAT, NLON, D), 1.0, 6.0, ((2, 4), (3, 8)))
    segment_depth = draw_segment_depth(jax.random.fold_in(seeds[9], 71), 0)
    shift_flags = with_ends(jax.random.randint(seeds[2], (LAYERS, 2), 0, 2), jax.random.fold_in(seeds[2], 1), 0, 1).astype(jnp.int32)
    w_qkv = scatter_about(seeds[3], (LAYERS, D, 3 * D), D ** -0.5, 0.25, ((0, 4),))
    w_out = scatter_about(seeds[4], (LAYERS, D, D), D ** -0.5, 0.25, ((0, 4),))
    w_up = scatter_about(seeds[5], (LAYERS, D, FF), D ** -0.5, 0.25, ((0, 4),))
    w_down = scatter_about(seeds[6], (LAYERS, FF, D), FF ** -0.5, 0.125, ((0, 4),))
    gains = jnp.clip(1.0 + 0.15 * jax.random.normal(seeds[7], (LAYERS, 2, D), jnp.float32), 0.25, 1.75)
    logit_scale = draw_logit_scale(jax.random.fold_in(seeds[9], 71), 0)
    return {"latents": latents, "segment_depth": segment_depth, "shift_flags": shift_flags, "w_qkv": w_qkv, "w_out": w_out, "w_up": w_up, "w_down": w_down, "gains": gains, "logit_scale": logit_scale}


def unit_heads(block):
    return block * lax.rsqrt(lax.optimization_barrier(jnp.sum(block * block, axis=-1, keepdims=True)) + 1e-06)

def layer_norm(values, gain):
    mean = lax.optimization_barrier(jnp.mean(values, axis=-1, keepdims=True))
    centred = values - mean
    var = lax.optimization_barrier(jnp.mean(centred * centred, axis=-1, keepdims=True))
    return centred * lax.rsqrt(var + 1e-05) * gain

def to_windows(field):
    lead = field.shape[3:]
    shaped = field.reshape((LEV, NLAT // W_LAT, W_LAT, NLON // W_LON, W_LON) + lead)
    order = (1, 3, 0, 2, 4) + tuple(range(5, 5 + len(lead)))
    return shaped.transpose(order).reshape((-1, LEV * W_LAT * W_LON) + lead)

def from_windows(field):
    shaped = field.reshape(NLAT // W_LAT, NLON // W_LON, LEV, W_LAT, W_LON, D)
    return shaped.transpose(2, 0, 3, 1, 4, 5).reshape(LEV, NLAT, NLON, D)

def one_layer(state, wqkv, wout, wup, wdown, gain, scale, flags):
    rounded = state.astype(jnp.bfloat16)
    proj = jnp.dot(rounded.reshape(-1, D), wqkv, preferred_element_type=jnp.float32)
    proj = proj.reshape(LEV, NLAT, NLON, 3, HEADS, HD)
    query = unit_heads(proj[:, :, :, 0]).astype(jnp.bfloat16)
    keys = unit_heads(proj[:, :, :, 1]).astype(jnp.bfloat16)
    values = proj[:, :, :, 2].astype(jnp.bfloat16)
    s_lat = flags[0] * (W_LAT // 2)
    s_lon = flags[1] * (W_LON // 2)
    rows = jnp.arange(NLAT, dtype=jnp.int32)
    labels = jnp.floor_divide(rows - s_lat, W_LAT).astype(jnp.int32)
    labels = jnp.roll(labels, -s_lat)
    labels = jnp.broadcast_to(labels[None, :, None], (LEV, NLAT, NLON))
    query = jnp.roll(query, (-s_lat, -s_lon), axis=(1, 2))
    keys = jnp.roll(keys, (-s_lat, -s_lon), axis=(1, 2))
    values = jnp.roll(values, (-s_lat, -s_lon), axis=(1, 2))
    qw = to_windows(query).astype(jnp.float32)
    kw = to_windows(keys).astype(jnp.float32)
    vw = to_windows(values).astype(jnp.float32)
    lw = to_windows(labels)
    scores = jnp.einsum('wqhd,wkhd->whqk', qw, kw) * scale[None, :, None, None]
    same = lw[:, :, None] == lw[:, None, :]
    scores = jnp.where(same[:, None], scores, -1e+30)
    top = lax.optimization_barrier(jnp.max(scores, axis=-1, keepdims=True))
    expo = jnp.exp(scores - top)
    weights = (expo / lax.optimization_barrier(jnp.sum(expo, axis=-1, keepdims=True))).astype(jnp.bfloat16)
    mixed = jnp.einsum('whqk,wkhd->wqhd', weights.astype(jnp.float32), vw).astype(jnp.bfloat16)
    mixed = from_windows(mixed.reshape(mixed.shape[0], mixed.shape[1], D))
    mixed = jnp.roll(mixed, (s_lat, s_lon), axis=(1, 2))
    out = jnp.dot(mixed.reshape(-1, D), wout, preferred_element_type=jnp.float32)
    flat = state.reshape(-1, D)
    first = flat + layer_norm(out, gain[0])
    hidden = jax.nn.gelu(jnp.dot(first.astype(jnp.bfloat16), wup, preferred_element_type=jnp.float32)).astype(jnp.bfloat16)
    down = jnp.dot(hidden, wdown, preferred_element_type=jnp.float32)
    second = first + layer_norm(down, gain[1])
    return second.reshape(LEV, NLAT, NLON, D)

def reference(latents, segment_depth, shift_flags, w_qkv, w_out, w_up, w_down, gains, logit_scale):
    results = []
    for micro in range(M):
        state = latents[micro].astype(jnp.float32)
        outputs = []
        for section in range(N_SEGMENT):
            for inner in range(MAXD):
                slot = section * MAXD + inner
                fresh = one_layer(state, w_qkv[slot], w_out[slot], w_up[slot], w_down[slot], gains[slot], logit_scale[slot], shift_flags[slot])
                state = jnp.where(inner < segment_depth[section], fresh, state)
            outputs.append(state)
        results.append(jnp.stack(outputs))
    return jnp.stack(results, axis=1)
```

```python
import functools

import jax
import jax.numpy as jnp
import numpy as np
from jax import lax
from jax.experimental import pallas as pl
from jax.experimental.pallas import tpu as pltpu
from jax.sharding import PartitionSpec as P

MESH = pl.DeviceIdType.MESH
HEADS = 8
GROUPS = 4
BLOCK = 36
HALF = GROUPS * BLOCK
CELLS = 2 * HALF
EDGE = 48
WIDE = CELLS + HALF + 3 * EDGE
PART = HALF // 2
SLOTS = 4
LOG2E = 1.4426950408889634
BIG = 1e30


def moves():
    table = np.zeros((CELLS, 128), np.float32)
    row = np.arange(CELLS)
    half, group, cell = row // HALF, row % HALF // BLOCK, row % BLOCK
    for lat in range(2):
        for lon in range(2):
            which = lat * 2 + lon
            for r in range(CELLS):
                h, g, t = half[r], group[r], cell[r]
                south, source = (h == 1, 1 - h) if lat else (False, h)
                east, column = (g == 3, (g + 1) % 4) if lon else (False, g)
                if south and east:
                    at = CELLS + HALF + 2 * EDGE + t
                elif south:
                    at = CELLS + column * BLOCK + t
                elif east:
                    at = CELLS + HALF + source * EDGE + t
                else:
                    at = source * HALF + column * BLOCK + t
                table[r, which] = at
                north, source = (h == 0, 1 - h) if lat else (False, h)
                west, column = (g == 0, (g + 3) % 4) if lon else (False, g)
                last = EDGE - BLOCK + t
                if north and west:
                    at = CELLS + HALF + 2 * EDGE + last
                elif north:
                    at = CELLS + column * BLOCK + t
                elif west:
                    at = CELLS + HALF + source * EDGE + last
                else:
                    at = source * HALF + column * BLOCK + t
                table[r, 4 + which] = at
    return table


def normed(values, gain):
    mean = jnp.mean(values, axis=-1, keepdims=True)
    centred = values - mean
    var = jnp.mean(centred * centred, axis=-1, keepdims=True)
    return centred * lax.rsqrt(var + 1e-05) * gain


def gelu(u):
    inner = u * (0.7978845608028654 + 0.035677408136300125 * (u * u))
    half = 0.5 * u
    return half + half * jnp.tanh(inner)


def dot(a, b):
    return jnp.dot(a, b, preferred_element_type=jnp.float32)


def kernel(
    lon_n, lat_n, depth_ref, latents, params, table, w_qkv, w_out, w_up, w_down, sections,
    wq, wo, wu, wd, par, fwd, bwd, x, src, ret, hid, stage, hand_out, hand_in, cross, ones,
    w_recv, w_send, p_recv, p_send, f_recv, f_send, b_recv, b_send, in_sem, h_recv, h_send,
    o_recv, o_send,
):
    seg = lax.axis_index("segment")
    lon = lax.axis_index("lon")
    lat = lax.axis_index("lat")
    chip = seg // 2
    core = lax.rem(seg, 2)
    mate_core = 1 - core
    north, south = lax.rem(lat + lat_n - 1, lat_n), lax.rem(lat + 1, lat_n)
    west, east = lax.rem(lon + lon_n - 1, lon_n), lax.rem(lon + 1, lon_n)

    def device(s, o, a):
        return {"segment": s, "lon": o, "lat": a}

    to_n, to_s = device(seg, lon, north), device(seg, lon, south)
    to_w, to_e = device(seg, west, lat), device(seg, east, lat)
    to_nw, to_se = device(seg, west, north), device(seg, east, south)
    mate = device(chip * 2 + mate_core, lon, lat)
    other = device(lax.rem(seg + 2, 4), lon, lat)

    weights = ((w_qkv, wq), (w_out, wo), (w_up, wu), (w_down, wd))

    def own_weights(i, k):
        slot = core * 2 + i
        held, kept = weights[k]
        return pltpu.make_async_copy(held.at[i], kept.at[slot], w_recv.at[slot, k])

    def lent_weights(i, k):
        slot = core * 2 + i
        held, kept = weights[k]
        return pltpu.make_async_remote_copy(
            src_ref=held.at[i], dst_ref=kept.at[slot], send_sem=w_send.at[i, k],
            recv_sem=w_recv.at[slot, k], device_id=mate, device_id_type=MESH,
        )

    def weights_here(l, k):
        held, kept = weights[k]
        pltpu.make_async_copy(held.at[0], kept.at[l], w_recv.at[l, k]).wait()

    def own_params():
        return pltpu.make_async_copy(params, par.at[pl.ds(core * 2, 2)], p_recv.at[core])

    def lent_params():
        return pltpu.make_async_remote_copy(
            src_ref=params, dst_ref=par.at[pl.ds(core * 2, 2)], send_sem=p_send.at[0],
            recv_sem=p_recv.at[core], device_id=mate, device_id_type=MESH,
        )

    def edges(b, buf, pieces, send, recv):
        return [
            pltpu.make_async_remote_copy(
                src_ref=buf.at[b, pl.ds(start, size)], dst_ref=buf.at[b, pl.ds(at, size)],
                send_sem=send.at[b, i], recv_sem=recv.at[b, i], device_id=to,
                device_id_type=MESH,
            )
            for i, (start, size, at, to) in enumerate(pieces)
        ]

    at_edge = CELLS + HALF

    def forth(b):
        return edges(
            b, src,
            (
                (0, HALF, CELLS, to_n),
                (0, EDGE, at_edge, to_w),
                (HALF, EDGE, at_edge + EDGE, to_w),
                (0, EDGE, at_edge + 2 * EDGE, to_nw),
            ),
            f_send, f_recv,
        )

    def back(b):
        return edges(
            b, ret,
            (
                (HALF, HALF, CELLS, to_s),
                (HALF - EDGE, EDGE, at_edge, to_e),
                (CELLS - EDGE, EDGE, at_edge + EDGE, to_e),
                (CELLS - EDGE, EDGE, at_edge + 2 * EDGE, to_se),
            ),
            b_send, b_recv,
        )

    def load_input(b):
        return pltpu.make_async_copy(
            latents.at[core + 2 * b], src.at[b, pl.ds(0, CELLS)], in_sem.at[b]
        )

    def hand_on(b):
        return pltpu.make_async_remote_copy(
            src_ref=hand_out.at[b], dst_ref=hand_in.at[b], send_sem=h_send.at[b],
            recv_sem=h_recv.at[b], device_id=other, device_id_type=MESH,
        )

    def keep_output(b, s):
        return pltpu.make_async_copy(
            stage.at[b, s], sections.at[core + 2 * b], o_recv.at[b, 0]
        )

    def give_output(b, s):
        return pltpu.make_async_remote_copy(
            src_ref=stage.at[b, s], dst_ref=sections.at[core + 2 * b], send_sem=o_send.at[b],
            recv_sem=o_recv.at[b, 1], device_id=mate, device_id_type=MESH,
        )

    barrier = pltpu.get_barrier_semaphore()
    for k in range(4):
        own_weights(0, k).start()
    own_params().start()

    @pl.when(chip == 0)
    def _():
        for b in range(2):
            load_input(b).start()

    for to in (to_n, to_s, to_w, to_e, to_nw, to_se, mate, other):
        pl.semaphore_signal(barrier, inc=1, device_id=to, device_id_type=MESH)
    pl.semaphore_wait(barrier, 8)

    lent_params().start()
    for i in range(2):
        for k in range(4):
            lent_weights(i, k).start()
            if i == 1:
                own_weights(i, k).start()

    @pl.when(chip == 0)
    def _():
        for b in range(2):
            load_input(b).wait()
            x[b] = src[b, 0:CELLS].astype(jnp.float32)
            for copy in forth(b):
                copy.start()

    @pl.when(chip == 1)
    def _():
        for b in range(2):
            hand_on(b).wait_recv()
            entry = hand_in[b]
            src[b, 0:CELLS] = entry
            x[b] = entry.astype(jnp.float32)
            for copy in forth(b):
                copy.start()

    own_params().wait()
    pltpu.make_async_copy(params, par.at[pl.ds(mate_core * 2, 2)], p_recv.at[mate_core]).wait()

    rows = lax.broadcasted_iota(jnp.int32, (HALF, HALF), 0)
    cols = lax.broadcasted_iota(jnp.int32, (HALF, HALF), 1)
    split = (rows < PART) != (cols < PART)
    is_last = jnp.where(lat == lat_n - 1, 1.0, 0.0)
    cross[...] = jnp.where(split, -BIG, 0.0) * is_last
    r256 = lax.broadcasted_iota(jnp.int32, (256, 256), 0)
    c256 = lax.broadcasted_iota(jnp.int32, (256, 256), 1)
    ones[...] = jnp.where(r256 // 64 == c256 // 64, 1.0, 0.0).astype(jnp.bfloat16)

    place = lax.broadcasted_iota(jnp.int32, (CELLS, WIDE), 1).astype(jnp.float32)

    def choose(l, carry):
        f_lat = par[l, 2:3, 0:1]
        f_lon = par[l, 3:4, 0:1]
        picks = (
            (1.0 - f_lat) * (1.0 - f_lon), (1.0 - f_lat) * f_lon,
            f_lat * (1.0 - f_lon), f_lat * f_lon,
        )
        for first, kept in ((0, fwd), (4, bwd)):
            at = sum(table[:, first + i : first + i + 1] * picks[i] for i in range(4))
            kept[l] = jnp.where(place == at, 1.0, 0.0).astype(jnp.bfloat16)
        return carry

    lax.fori_loop(0, SLOTS, choose, 0)

    lane = lax.broadcasted_iota(jnp.int32, (1, 256), 1)
    masks = [jnp.where(lane // 64 == h, 1.0, 0.0).astype(jnp.bfloat16) for h in range(4)]

    def unit(block):
        square = block * block
        high = square.astype(jnp.bfloat16)
        low = (square - high.astype(jnp.float32)).astype(jnp.bfloat16)
        total = dot(high, ones[...]) + dot(low, ones[...])
        return block * lax.rsqrt(total + 1e-06)

    def window(values, w):
        a = w * PART
        return jnp.concatenate(
            [values[a : a + PART], values[HALF + a : HALF + a + PART]], axis=0
        ).astype(jnp.bfloat16)

    def attend(b, l):
        for copy in forth(b):
            copy.wait()
        cells = dot(fwd[l], src[b]).astype(jnp.bfloat16)
        bias = par[l, 2:3, 0:HALF] * cross[...]
        for g in range(2):
            lanes = [slice(p * 512 + g * 256, p * 512 + g * 256 + 256) for p in range(3)]
            q = unit(dot(cells, wq[l, :, lanes[0]]))
            k = unit(dot(cells, wq[l, :, lanes[1]]))
            v = dot(cells, wq[l, :, lanes[2]])
            outs = []
            for w in range(2):
                qw, kw, vw = window(q, w), window(k, w), window(v, w)
                total = jnp.zeros((HALF, 256), jnp.float32)
                for h in range(4):
                    scale = par[l, 4 + g * 4 + h : 5 + g * 4 + h, 0:HALF]
                    score = lax.dot_general(
                        qw, kw * masks[h], (((1,), (1,)), ((), ())),
                        preferred_element_type=jnp.float32,
                    )
                    score = score * scale + bias
                    top = jnp.max(score, axis=-1, keepdims=True)
                    expo = jnp.exp2(score - top)
                    share = 1.0 / jnp.sum(expo, axis=-1, keepdims=True)
                    weight = (expo * share).astype(jnp.bfloat16)
                    total = total + dot(weight, vw * masks[h])
                outs.append(total)
            for h in range(2):
                part = slice(h * PART, h * PART + PART)
                ret[b, h * HALF : h * HALF + HALF, g * 256 : g * 256 + 256] = jnp.concatenate(
                    [outs[0][part], outs[1][part]], axis=0
                ).astype(jnp.bfloat16)
        for copy in back(b):
            copy.start()

    def feed(b, l):
        for copy in back(b):
            copy.wait()
        mixed = dot(bwd[l], ret[b]).astype(jnp.bfloat16)
        state = x[b]
        first = state + normed(dot(mixed, wo[l]), par[l, 0:1])
        firstb = first.astype(jnp.bfloat16)
        for c in range(4):
            part = slice(c * 512, c * 512 + 512)
            hid[:, part] = gelu(dot(firstb, wu[l, :, part])).astype(jnp.bfloat16)
        second = first + normed(dot(hid[...], wd[l]), par[l, 1:2])
        s = l // 2
        applied = lax.rem(l, 2) < depth_ref[chip * 2 + s]
        fresh = jnp.where(applied, second, state)
        x[b] = fresh
        freshb = fresh.astype(jnp.bfloat16)

        @pl.when(l < SLOTS - 1)
        def _():
            src[b, 0:CELLS] = freshb
            for copy in forth(b):
                copy.start()

        @pl.when(lax.rem(l, 2) == 1)
        def _():
            stage[b, s] = fresh

            @pl.when(s == core)
            def _():
                keep_output(b, s).start()

            @pl.when(s != core)
            def _():
                give_output(b, s).start()

        @pl.when((l == SLOTS - 1) & (chip == 0))
        def _():
            hand_out[b] = freshb
            hand_on(b).start()

    def layer(l, carry):
        weights_here(l, 0)

        def one(b, c):
            attend(b, l)
            return c

        lax.fori_loop(0, 2, one, 0)
        for k in range(1, 4):
            weights_here(l, k)

        def two(b, c):
            feed(b, l)
            return c

        lax.fori_loop(0, 2, two, 0)
        return carry

    lax.fori_loop(0, SLOTS, layer, 0)

    for i in range(2):
        for k in range(4):
            lent_weights(i, k).wait_send()
    lent_params().wait_send()

    @pl.when(chip == 0)
    def _():
        for b in range(2):
            hand_on(b).wait_send()

    for b in range(2):
        keep_output(b, core).wait()
        give_output(b, mate_core).wait()


def shards(latents, segment_depth, shift_flags, w_qkv, w_out, w_up, w_down, gains, logit_scale,
           lon_n, lat_n):
    micro, levels, clat, clon, width = latents.shape
    cells = latents.reshape(micro, levels, 2, 3, GROUPS, 6, width)
    cells = cells.transpose(0, 2, 4, 1, 3, 5, 6).reshape(micro, CELLS, width)
    small = jnp.concatenate(
        [shift_flags.astype(jnp.float32), logit_scale * LOG2E, jnp.zeros((2, 4), jnp.float32)],
        axis=1,
    )
    params = jnp.concatenate(
        [gains, jnp.broadcast_to(small[:, :, None], (2, 14, width))], axis=1
    )
    table = jnp.asarray(moves())
    hbm = pl.BlockSpec(memory_space=pl.ANY)
    bf16, f32 = jnp.bfloat16, jnp.float32
    dma = pltpu.SemaphoreType.DMA
    out = pl.pallas_call(
        functools.partial(kernel, lon_n, lat_n),
        out_shape=jax.ShapeDtypeStruct((micro, CELLS, width), f32),
        in_specs=[
            pl.BlockSpec(memory_space=pltpu.SMEM), hbm, hbm,
            pl.BlockSpec(memory_space=pltpu.VMEM), hbm, hbm, hbm, hbm,
        ],
        out_specs=hbm,
        scratch_shapes=[
            pltpu.VMEM((SLOTS, width, 3 * width), bf16),
            pltpu.VMEM((SLOTS, width, width), bf16),
            pltpu.VMEM((SLOTS, width, 4 * width), bf16),
            pltpu.VMEM((SLOTS, 4 * width, width), bf16),
            pltpu.VMEM((SLOTS, 16, width), f32),
            pltpu.VMEM((SLOTS, CELLS, WIDE), bf16),
            pltpu.VMEM((SLOTS, CELLS, WIDE), bf16),
            pltpu.VMEM((2, CELLS, width), f32),
            pltpu.VMEM((2, WIDE, width), bf16),
            pltpu.VMEM((2, WIDE, width), bf16),
            pltpu.VMEM((CELLS, 4 * width), bf16),
            pltpu.VMEM((2, 2, CELLS, width), f32),
            pltpu.VMEM((2, CELLS, width), bf16),
            pltpu.VMEM((2, CELLS, width), bf16),
            pltpu.VMEM((HALF, HALF), f32),
            pltpu.VMEM((256, 256), bf16),
            dma((SLOTS, 4)), dma((2, 4)), dma((2,)), dma((1,)),
            dma((2, 4)), dma((2, 4)), dma((2, 4)), dma((2, 4)),
            dma((2,)), dma((2,)), dma((2,)), dma((2, 2)), dma((2,)),
        ],
        compiler_params=pltpu.CompilerParams(
            collective_id=0, has_side_effects=True, vmem_limit_bytes=60 * 1024 * 1024
        ),
        cost_estimate=pl.CostEstimate(
            flops=16 * 2 * 10**9, bytes_accessed=20 * 10**6, transcendentals=10**7
        ),
    )(segment_depth, cells, params, table, w_qkv, w_out, w_up, w_down)
    out = out.reshape(micro, 2, GROUPS, levels, 3, 6, width).transpose(0, 3, 1, 4, 2, 5, 6)
    return out.reshape(1, micro, levels, clat, clon, width)


def solution(mesh):
    placed = (
        P(None, None, "lat", "lon", None),
        P(),
        P("segment", None),
        P("segment", None, None),
        P("segment", None, None),
        P("segment", None, None),
        P("segment", None, None),
        P("segment", None, None),
        P("segment", None),
    )
    return jax.shard_map(
        functools.partial(shards, lon_n=mesh.shape["lon"], lat_n=mesh.shape["lat"]),
        mesh=mesh,
        in_specs=placed,
        out_specs=P("segment", None, None, "lat", "lon", None),
        check_vma=False,
    )
```

```python
import functools

import jax
import jax.numpy as jnp
import numpy as np
from jax import lax
from jax.experimental import pallas as pl
from jax.experimental.pallas import tpu as pltpu
from jax.sharding import PartitionSpec as P

MESH = pl.DeviceIdType.MESH
HALF = 144
CELLS = 2 * HALF
PART = HALF // 2
REACH = 80
EDGE = 48
AT_LAT = CELLS
AT_LON = AT_LAT + 2 * REACH
AT_BOTH = AT_LON + 2 * EDGE
WIDE = AT_BOTH + EDGE
SLOTS = 4
LOG2E = 1.4426950408889634
BIG = 1e30


def moves():
    table = np.zeros((CELLS, 128), np.float32)
    for core in range(2):
        far_half = 1 - core
        for lat in range(2):
            for lon in range(2):
                which = core * 8 + lat * 2 + lon
                for at in range(CELLS):
                    window, half, pair, cell = at // 144, at % 144 // 72, at % 72 // 36, at % 36
                    level, row, column = cell // 18, cell % 18 // 6, cell % 6
                    column += (2 * window + pair) * 6 + lon * (6 - 12 * core)
                    across = column >= 24 or column < 0
                    edge_column = column - 24 if core == 0 else column + 24 - 16
                    along = lat == 1 and half == far_half
                    source = 1 - half if lat else half
                    edge = (level * 3 + row) * 8 + edge_column
                    if along and across:
                        take = AT_BOTH + edge
                    elif along:
                        take = AT_LAT + level * REACH + core * 8 + row * 24 + column
                    elif across:
                        take = AT_LON + source * EDGE + edge
                    else:
                        take = level * 144 + (source * 3 + row) * 24 + column
                    table[at, which] = take

                    level, row, column = at // 144, at % 144 // 24, at % 24
                    half, row = row // 3, row % 3
                    along = lat == 1 and half == core
                    source = 1 - half if lat else half
                    column -= lon * (6 - 12 * core)
                    across = column >= 24 or column < 0
                    column %= 24
                    window, pair = column // 12, column % 12 // 6
                    inside = source * 72 + pair * 36 + level * 18 + row * 6 + column % 6
                    if along and across:
                        take = AT_BOTH + inside - (0 if core else 96)
                    elif along:
                        take = AT_LAT + window * REACH + inside - (0 if core else 64)
                    elif across:
                        take = AT_LON + source * EDGE + inside - source * 64 - (0 if core else 32)
                    else:
                        take = window * 144 + inside
                    table[at, which + 4] = take
    return table


def normed(values, gain):
    mean = jnp.mean(values, axis=-1, keepdims=True)
    centred = values - mean
    var = jnp.mean(centred * centred, axis=-1, keepdims=True)
    return centred * lax.rsqrt(var + 1e-05) * gain


def gelu(u):
    inner = u * (0.7978845608028654 + 0.035677408136300125 * (u * u))
    half = 0.5 * u
    return half + half * jnp.tanh(inner)


def dot(a, b):
    return jnp.dot(a, b, preferred_element_type=jnp.float32)


def kernel(
    lon_n, lat_n, depth_ref, latents, small_in, gains_in, table, w_qkv, w_out, w_up, w_down, sections,
    wq, wo, wu, wd, small, gains, fwd, bwd, x, src, packed, ret, hid, stage, hand_out, hand_in, cross, ones,
    w_recv, w_send, p_recv, p_send, f_recv, f_send, b_recv, b_send, in_sem, h_recv, h_send,
    o_recv, o_send,
):
    seg = lax.axis_index("segment")
    lon = lax.axis_index("lon")
    lat = lax.axis_index("lat")
    chip = seg // 2
    core = lax.rem(seg, 2)
    mate_core = 1 - core
    north, south = lax.rem(lat + lat_n - 1, lat_n), lax.rem(lat + 1, lat_n)
    west, east = lax.rem(lon + lon_n - 1, lon_n), lax.rem(lon + 1, lon_n)

    def device(s, o, a):
        return {"segment": s, "lon": o, "lat": a}

    out_lat, home_lat = north + core * (south - north), south + core * (north - south)
    out_lon, home_lon = west + core * (east - west), east + core * (west - east)
    to_n, to_s = device(seg, lon, out_lat), device(seg, lon, home_lat)
    to_w, to_e = device(seg, out_lon, lat), device(seg, home_lon, lat)
    to_nw, to_se = device(seg, out_lon, out_lat), device(seg, home_lon, home_lat)
    mate = device(chip * 2 + mate_core, lon, lat)
    other = device(lax.rem(seg + 2, 4), lon, lat)

    weights = ((w_qkv, wq), (w_out, wo), (w_up, wu), (w_down, wd))

    def own_weights(i, k):
        slot = core * 2 + i
        held, kept = weights[k]
        return pltpu.make_async_copy(held.at[i], kept.at[slot], w_recv.at[slot, k])

    def lent_weights(i, k):
        slot = core * 2 + i
        held, kept = weights[k]
        return pltpu.make_async_remote_copy(
            src_ref=held.at[i], dst_ref=kept.at[slot], send_sem=w_send.at[i, k],
            recv_sem=w_recv.at[slot, k], device_id=mate, device_id_type=MESH,
        )

    def weights_here(l, k):
        held, kept = weights[k]
        pltpu.make_async_copy(held.at[0], kept.at[l], w_recv.at[l, k]).wait()

    tiny = ((small_in, small), (gains_in, gains))

    def own_params(k):
        held, kept = tiny[k]
        return pltpu.make_async_copy(held, kept.at[pl.ds(core * 2, 2)], p_recv.at[core, k])

    def lent_params(k):
        held, kept = tiny[k]
        return pltpu.make_async_remote_copy(
            src_ref=held, dst_ref=kept.at[pl.ds(core * 2, 2)], send_sem=p_send.at[k],
            recv_sem=p_recv.at[core, k], device_id=mate, device_id_type=MESH,
        )

    def edges(pieces, send, recv):
        return [
            pltpu.make_async_remote_copy(
                src_ref=source, dst_ref=target, send_sem=send.at[i], recv_sem=recv.at[i],
                device_id=to, device_id_type=MESH,
            )
            for i, (source, target, to) in enumerate(pieces)
        ]

    def rows_from(start, size):
        return pl.ds(pl.multiple_of(start, 16), size)

    def forth(b):
        return edges(
            (
                (src.at[b, rows_from(64 * core, REACH)], src.at[b, pl.ds(AT_LAT, REACH)], to_n),
                (
                    src.at[b, rows_from(HALF + 64 * core, REACH)],
                    src.at[b, pl.ds(AT_LAT + REACH, REACH)], to_n,
                ),
                (packed.at[b], src.at[b, pl.ds(AT_LON, 2 * EDGE)], to_w),
                (packed.at[b, rows_from(EDGE * core, EDGE)], src.at[b, pl.ds(AT_BOTH, EDGE)], to_nw),
            ),
            f_send.at[b], f_recv.at[b],
        )

    def back(b):
        return edges(
            (
                (ret.at[b, rows_from(64 - 64 * core, REACH)], ret.at[b, pl.ds(AT_LAT, REACH)], to_s),
                (
                    ret.at[b, rows_from(208 - 64 * core, REACH)],
                    ret.at[b, pl.ds(AT_LAT + REACH, REACH)], to_s,
                ),
                (ret.at[b, rows_from(176 - 176 * core, EDGE)], ret.at[b, pl.ds(AT_LON, EDGE)], to_e),
                (
                    ret.at[b, rows_from(240 - 176 * core, EDGE)],
                    ret.at[b, pl.ds(AT_LON + EDGE, EDGE)], to_e,
                ),
                (ret.at[b, rows_from(240 - 240 * core, EDGE)], ret.at[b, pl.ds(AT_BOTH, EDGE)], to_se),
            ),
            b_send.at[b], b_recv.at[b],
        )

    def edge_of(values, column):
        rows = [
            level * 144 + row * 24 + column
            for half in ((0, 1, 2), (3, 4, 5)) for level in (0, 1) for row in half
        ]
        return jnp.concatenate([values[r : r + 8] for r in rows], axis=0)

    def far_edge(values):
        return jnp.where(core == 0, edge_of(values, 0), edge_of(values, 16)).astype(jnp.bfloat16)

    def load_input(b):
        return pltpu.make_async_copy(
            latents.at[core + 2 * b], src.at[b, pl.ds(0, CELLS)], in_sem.at[b]
        )

    def hand_on(b):
        return pltpu.make_async_remote_copy(
            src_ref=hand_out.at[b], dst_ref=hand_in.at[b], send_sem=h_send.at[b],
            recv_sem=h_recv.at[b], device_id=other, device_id_type=MESH,
        )

    def keep_output(b, s):
        return pltpu.make_async_copy(
            stage.at[b, s], sections.at[core + 2 * b], o_recv.at[b, 0]
        )

    def give_output(b, s):
        return pltpu.make_async_remote_copy(
            src_ref=stage.at[b, s], dst_ref=sections.at[core + 2 * b], send_sem=o_send.at[b],
            recv_sem=o_recv.at[b, 1], device_id=mate, device_id_type=MESH,
        )

    barrier = pltpu.get_barrier_semaphore()
    for k in range(4):
        own_weights(0, k).start()
    for k in range(2):
        own_params(k).start()

    @pl.when(chip == 0)
    def _():
        for b in range(2):
            load_input(b).start()

    for to in (to_n, to_s, to_w, to_e, to_nw, to_se, mate, other):
        pl.semaphore_signal(barrier, inc=1, device_id=to, device_id_type=MESH)
    pl.semaphore_wait(barrier, 8)

    for k in range(2):
        lent_params(k).start()
    for i in range(2):
        for k in range(4):
            lent_weights(i, k).start()
            if i == 1:
                own_weights(i, k).start()

    @pl.when(chip == 0)
    def _():
        for b in range(2):
            load_input(b).wait()
            entry = src[b, 0:CELLS].astype(jnp.float32)
            x[b] = entry
            packed[b] = far_edge(entry)
            for copy in forth(b):
                copy.start()

    @pl.when(chip == 1)
    def _():
        for b in range(2):
            hand_on(b).wait_recv()
            src[b, 0:CELLS] = hand_in[b]
            entry = hand_in[b].astype(jnp.float32)
            x[b] = entry
            packed[b] = far_edge(entry)
            for copy in forth(b):
                copy.start()

    for k, (held, kept) in enumerate(tiny):
        own_params(k).wait()
        pltpu.make_async_copy(
            held, kept.at[pl.ds(mate_core * 2, 2)], p_recv.at[mate_core, k]
        ).wait()

    rows = lax.broadcasted_iota(jnp.int32, (HALF, HALF), 0)
    cols = lax.broadcasted_iota(jnp.int32, (HALF, HALF), 1)
    split = (rows < PART) != (cols < PART)
    is_last = jnp.where(lat == (lat_n - 1) * (1 - core), 1.0, 0.0)
    cross[...] = jnp.where(split, -BIG, 0.0) * is_last
    r256 = lax.broadcasted_iota(jnp.int32, (256, 256), 0)
    c256 = lax.broadcasted_iota(jnp.int32, (256, 256), 1)
    ones[...] = jnp.where(r256 // 64 == c256 // 64, 1.0, 0.0).astype(jnp.bfloat16)

    place = lax.broadcasted_iota(jnp.int32, (CELLS, WIDE), 1).astype(jnp.float32)

    def choose(l, carry):
        f_lat = small[l, 0:1, 0:1]
        f_lon = small[l, 0:1, 1:2]
        picks = (
            (1.0 - f_lat) * (1.0 - f_lon), (1.0 - f_lat) * f_lon,
            f_lat * (1.0 - f_lon), f_lat * f_lon,
        )
        for first, kept in ((0, fwd), (4, bwd)):
            at = sum(
                jnp.where(
                    core == 0, table[:, first + i : first + i + 1],
                    table[:, first + i + 8 : first + i + 9],
                ) * picks[i]
                for i in range(4)
            )
            kept[l] = jnp.where(place == at, 1.0, 0.0).astype(jnp.bfloat16)
        return carry

    lax.fori_loop(0, SLOTS, choose, 0)

    lane = lax.broadcasted_iota(jnp.int32, (1, 256), 1)
    masks = [jnp.where(lane // 64 == h, 1.0, 0.0).astype(jnp.bfloat16) for h in range(4)]
    first_of_pair = lax.broadcasted_iota(jnp.int32, (HALF, 128), 1) < 64

    def unit(block):
        total = dot((block * block).astype(jnp.bfloat16), ones[...])
        return (block * lax.rsqrt(total + 1e-06)).astype(jnp.bfloat16)

    def attend(b, l):
        for copy in forth(b):
            copy.wait()
        cells = dot(fwd[l], src[b]).astype(jnp.bfloat16)
        bias = small[l, 0:1, 0:1] * cross[...]
        for g in range(2):
            lanes = [slice(p * 512 + g * 256, p * 512 + g * 256 + 256) for p in range(3)]
            q = unit(dot(cells, wq[l, :, lanes[0]]))
            k = unit(dot(cells, wq[l, :, lanes[1]]))
            v = dot(cells, wq[l, :, lanes[2]]).astype(jnp.bfloat16)
            for w in range(2):
                part = slice(w * HALF, w * HALF + HALF)
                heads = jnp.concatenate([q[part] * masks[h] for h in range(4)], axis=0)
                scores = lax.dot_general(
                    heads, k[part], (((1,), (1,)), ((), ())), preferred_element_type=jnp.float32
                )
                expos, shares = [], []
                for h in range(4):
                    scale = small[l, 0:1, 2 + g * 4 + h : 3 + g * 4 + h]
                    score = scores[h * HALF : h * HALF + HALF] * scale + bias
                    expo = jnp.exp2(score - jnp.max(score, axis=-1, keepdims=True))
                    shares.append(1.0 / jnp.sum(expo, axis=-1, keepdims=True))
                    expos.append(expo.astype(jnp.bfloat16))
                mixed = dot(jnp.concatenate(expos, axis=0), v[part])
                for p in range(2):
                    at = slice(p * 128, p * 128 + 128)
                    one = mixed[2 * p * HALF : (2 * p + 1) * HALF, at] * shares[2 * p]
                    two = mixed[(2 * p + 1) * HALF : (2 * p + 2) * HALF, at] * shares[2 * p + 1]
                    ret[b, part, g * 256 + p * 128 : g * 256 + p * 128 + 128] = jnp.where(
                        first_of_pair, one, two
                    ).astype(jnp.bfloat16)
        for copy in back(b):
            copy.start()

    def feed(b, l):
        for copy in back(b):
            copy.wait()
        mixed = dot(bwd[l], ret[b]).astype(jnp.bfloat16)
        state = x[b]
        first = state + normed(dot(mixed, wo[l]), gains[l, 0:1])
        firstb = first.astype(jnp.bfloat16)
        for c in range(4):
            part = slice(c * 512, c * 512 + 512)
            hid[:, part] = gelu(dot(firstb, wu[l, :, part])).astype(jnp.bfloat16)
        second = first + normed(dot(hid[...], wd[l]), gains[l, 1:2])
        s = l // 2
        applied = lax.rem(l, 2) < depth_ref[chip * 2 + s]
        fresh = jnp.where(applied, second, state)
        x[b] = fresh
        freshb = fresh.astype(jnp.bfloat16)

        @pl.when(l < SLOTS - 1)
        def _():
            src[b, 0:CELLS] = freshb
            packed[b] = far_edge(fresh)
            for copy in forth(b):
                copy.start()

        @pl.when(lax.rem(l, 2) == 1)
        def _():
            stage[b, s] = fresh

            @pl.when(s == core)
            def _():
                keep_output(b, s).start()

            @pl.when(s != core)
            def _():
                give_output(b, s).start()

        @pl.when((l == SLOTS - 1) & (chip == 0))
        def _():
            hand_out[b] = freshb
            hand_on(b).start()

    def layer(l, carry):
        weights_here(l, 0)

        def one(b, c):
            attend(b, l)
            return c

        lax.fori_loop(0, 2, one, 0)
        for k in range(1, 4):
            weights_here(l, k)

        def two(b, c):
            feed(b, l)
            return c

        lax.fori_loop(0, 2, two, 0)
        return carry

    lax.fori_loop(0, SLOTS, layer, 0)

    for i in range(2):
        for k in range(4):
            lent_weights(i, k).wait_send()
    for k in range(2):
        lent_params(k).wait_send()

    @pl.when(chip == 0)
    def _():
        for b in range(2):
            hand_on(b).wait_send()

    for b in range(2):
        keep_output(b, core).wait()
        give_output(b, mate_core).wait()


def shards(latents, segment_depth, shift_flags, w_qkv, w_out, w_up, w_down, gains, logit_scale,
           lon_n, lat_n):
    micro, levels, clat, clon, width = latents.shape
    cells = latents.reshape(micro, CELLS, width)
    small = jnp.concatenate(
        [shift_flags.astype(jnp.float32), logit_scale * LOG2E, jnp.zeros((2, 118), jnp.float32)],
        axis=1,
    ).reshape(2, 1, 128)
    table = jnp.asarray(moves())
    hbm = pl.BlockSpec(memory_space=pl.ANY)
    bf16, f32 = jnp.bfloat16, jnp.float32
    dma = pltpu.SemaphoreType.DMA
    out = pl.pallas_call(
        functools.partial(kernel, lon_n, lat_n),
        out_shape=jax.ShapeDtypeStruct((micro, CELLS, width), f32),
        in_specs=[
            pl.BlockSpec(memory_space=pltpu.SMEM), hbm, hbm, hbm,
            pl.BlockSpec(memory_space=pltpu.VMEM), hbm, hbm, hbm, hbm,
        ],
        out_specs=hbm,
        scratch_shapes=[
            pltpu.VMEM((SLOTS, width, 3 * width), bf16),
            pltpu.VMEM((SLOTS, width, width), bf16),
            pltpu.VMEM((SLOTS, width, 4 * width), bf16),
            pltpu.VMEM((SLOTS, 4 * width, width), bf16),
            pltpu.VMEM((SLOTS, 1, 128), f32),
            pltpu.VMEM((SLOTS, 2, width), f32),
            pltpu.VMEM((SLOTS, CELLS, WIDE), bf16),
            pltpu.VMEM((SLOTS, CELLS, WIDE), bf16),
            pltpu.VMEM((2, CELLS, width), f32),
            pltpu.VMEM((2, WIDE, width), bf16),
            pltpu.VMEM((2, 2 * EDGE, width), bf16),
            pltpu.VMEM((2, WIDE, width), bf16),
            pltpu.VMEM((CELLS, 4 * width), bf16),
            pltpu.VMEM((2, 2, CELLS, width), f32),
            pltpu.VMEM((2, CELLS, width), bf16),
            pltpu.VMEM((2, CELLS, width), bf16),
            pltpu.VMEM((HALF, HALF), f32),
            pltpu.VMEM((256, 256), bf16),
            dma((SLOTS, 4)), dma((2, 4)), dma((2, 2)), dma((2,)),
            dma((2, 4)), dma((2, 4)), dma((2, 5)), dma((2, 5)),
            dma((2,)), dma((2,)), dma((2,)), dma((2, 2)), dma((2,)),
        ],
        compiler_params=pltpu.CompilerParams(
            collective_id=0, has_side_effects=True, vmem_limit_bytes=60 * 1024 * 1024
        ),
        cost_estimate=pl.CostEstimate(
            flops=16 * 2 * 10**9, bytes_accessed=20 * 10**6, transcendentals=10**7
        ),
    )(segment_depth, cells, small, gains, table, w_qkv, w_out, w_up, w_down)
    return out.reshape(1, micro, levels, clat, clon, width)


def solution(mesh):
    placed = (
        P(None, None, "lat", "lon", None),
        P(),
        P("segment", None),
        P("segment", None, None),
        P("segment", None, None),
        P("segment", None, None),
        P("segment", None, None),
        P("segment", None, None),
        P("segment", None),
    )
    return jax.shard_map(
        functools.partial(shards, lon_n=mesh.shape["lon"], lat_n=mesh.shape["lat"]),
        mesh=mesh,
        in_specs=placed,
        out_specs=P("segment", None, None, "lat", "lon", None),
        check_vma=False,
    )
```

```python
import functools

import jax
import jax.numpy as jnp
import numpy as np
from jax import lax
from jax.experimental import pallas as pl
from jax.experimental.pallas import tpu as pltpu
from jax.sharding import PartitionSpec as P

MESH = pl.DeviceIdType.MESH
HALF = 144
CELLS = 2 * HALF
PART = HALF // 2
REACH = 80
EDGE = 48
AT_LAT = CELLS
AT_LON = AT_LAT + 2 * REACH
AT_BOTH = AT_LON + 2 * EDGE
WIDE = AT_BOTH + EDGE
SLOTS = 4
LOG2E = 1.4426950408889634
BIG = 1e30


def moves():
    table = np.zeros((CELLS, 128), np.float32)
    for core in range(2):
        far_half = 1 - core
        for lat in range(2):
            for lon in range(2):
                which = core * 8 + lat * 2 + lon
                for at in range(CELLS):
                    window, half, pair, cell = at // 144, at % 144 // 72, at % 72 // 36, at % 36
                    level, row, column = cell // 18, cell % 18 // 6, cell % 6
                    column += (2 * window + pair) * 6 + lon * (6 - 12 * core)
                    across = column >= 24 or column < 0
                    edge_column = column - 24 if core == 0 else column + 24 - 16
                    along = lat == 1 and half == far_half
                    source = 1 - half if lat else half
                    edge = (level * 3 + row) * 8 + edge_column
                    if along and across:
                        take = AT_BOTH + edge
                    elif along:
                        take = AT_LAT + level * REACH + core * 8 + row * 24 + column
                    elif across:
                        take = AT_LON + source * EDGE + edge
                    else:
                        take = level * 144 + (source * 3 + row) * 24 + column
                    table[at, which] = take

                    level, row, column = at // 144, at % 144 // 24, at % 24
                    half, row = row // 3, row % 3
                    along = lat == 1 and half == core
                    source = 1 - half if lat else half
                    column -= lon * (6 - 12 * core)
                    across = column >= 24 or column < 0
                    column %= 24
                    window, pair = column // 12, column % 12 // 6
                    inside = source * 72 + pair * 36 + level * 18 + row * 6 + column % 6
                    if along and across:
                        take = AT_BOTH + inside - (0 if core else 96)
                    elif along:
                        take = AT_LAT + window * REACH + inside - (0 if core else 64)
                    elif across:
                        take = AT_LON + source * EDGE + inside - source * 64 - (0 if core else 32)
                    else:
                        take = window * 144 + inside
                    table[at, which + 4] = take
    return table


def normed(values, gain):
    mean = jnp.mean(values, axis=-1, keepdims=True)
    centred = values - mean
    var = jnp.mean(centred * centred, axis=-1, keepdims=True)
    return centred * lax.rsqrt(var + 1e-05) * gain


def gelu(u):
    inner = u * (0.7978845608028654 + 0.035677408136300125 * (u * u))
    half = 0.5 * u
    return half + half * jnp.tanh(inner)


def dot(a, b):
    return jnp.dot(a, b, preferred_element_type=jnp.float32)


def kernel(
    lon_n, lat_n, depth_ref, latents, small_in, gains_in, table, w_qkv, w_out, w_up, w_down, sections,
    wq, wo, wu, wd, small, gains, fwd, bwd, x, src, packed, ret, stage, hand_out, hand_in, cross, ones,
    w_recv, w_send, p_recv, p_send, f_recv, f_send, b_recv, b_send, in_sem, h_recv, h_send,
    o_recv, o_send,
):
    seg = lax.axis_index("segment")
    lon = lax.axis_index("lon")
    lat = lax.axis_index("lat")
    chip = seg // 2
    core = lax.rem(seg, 2)
    mate_core = 1 - core
    north, south = lax.rem(lat + lat_n - 1, lat_n), lax.rem(lat + 1, lat_n)
    west, east = lax.rem(lon + lon_n - 1, lon_n), lax.rem(lon + 1, lon_n)

    def device(s, o, a):
        return {"segment": s, "lon": o, "lat": a}

    out_lat, home_lat = north + core * (south - north), south + core * (north - south)
    out_lon, home_lon = west + core * (east - west), east + core * (west - east)
    to_n, to_s = device(seg, lon, out_lat), device(seg, lon, home_lat)
    to_w, to_e = device(seg, out_lon, lat), device(seg, home_lon, lat)
    to_nw, to_se = device(seg, out_lon, out_lat), device(seg, home_lon, home_lat)
    mate = device(chip * 2 + mate_core, lon, lat)
    other = device(lax.rem(seg + 2, 4), lon, lat)

    weights = ((w_qkv, wq), (w_out, wo), (w_up, wu), (w_down, wd))

    def own_weights(i, k):
        slot = core * 2 + i
        held, kept = weights[k]
        return pltpu.make_async_copy(held.at[i], kept.at[slot], w_recv.at[slot, k])

    def lent_weights(i, k):
        slot = core * 2 + i
        held, kept = weights[k]
        return pltpu.make_async_remote_copy(
            src_ref=held.at[i], dst_ref=kept.at[slot], send_sem=w_send.at[i, k],
            recv_sem=w_recv.at[slot, k], device_id=mate, device_id_type=MESH,
        )

    def weights_here(l, k):
        held, kept = weights[k]
        pltpu.make_async_copy(held.at[0], kept.at[l], w_recv.at[l, k]).wait()

    tiny = ((small_in, small), (gains_in, gains))

    def own_params(k):
        held, kept = tiny[k]
        return pltpu.make_async_copy(held, kept.at[pl.ds(core * 2, 2)], p_recv.at[core, k])

    def lent_params(k):
        held, kept = tiny[k]
        return pltpu.make_async_remote_copy(
            src_ref=held, dst_ref=kept.at[pl.ds(core * 2, 2)], send_sem=p_send.at[k],
            recv_sem=p_recv.at[core, k], device_id=mate, device_id_type=MESH,
        )

    def edges(pieces, send, recv):
        return [
            pltpu.make_async_remote_copy(
                src_ref=source, dst_ref=target, send_sem=send.at[i], recv_sem=recv.at[i],
                device_id=to, device_id_type=MESH,
            )
            for i, (source, target, to) in enumerate(pieces)
        ]

    def rows_from(start, size):
        return pl.ds(pl.multiple_of(start, 16), size)

    def forth(b):
        return edges(
            (
                (src.at[b, rows_from(64 * core, REACH)], src.at[b, pl.ds(AT_LAT, REACH)], to_n),
                (
                    src.at[b, rows_from(HALF + 64 * core, REACH)],
                    src.at[b, pl.ds(AT_LAT + REACH, REACH)], to_n,
                ),
                (packed.at[b], src.at[b, pl.ds(AT_LON, 2 * EDGE)], to_w),
                (packed.at[b, rows_from(EDGE * core, EDGE)], src.at[b, pl.ds(AT_BOTH, EDGE)], to_nw),
            ),
            f_send.at[b], f_recv.at[b],
        )

    def back(b):
        return edges(
            (
                (ret.at[b, rows_from(64 - 64 * core, REACH)], ret.at[b, pl.ds(AT_LAT, REACH)], to_s),
                (
                    ret.at[b, rows_from(208 - 64 * core, REACH)],
                    ret.at[b, pl.ds(AT_LAT + REACH, REACH)], to_s,
                ),
                (ret.at[b, rows_from(176 - 176 * core, EDGE)], ret.at[b, pl.ds(AT_LON, EDGE)], to_e),
                (
                    ret.at[b, rows_from(240 - 176 * core, EDGE)],
                    ret.at[b, pl.ds(AT_LON + EDGE, EDGE)], to_e,
                ),
                (ret.at[b, rows_from(240 - 240 * core, EDGE)], ret.at[b, pl.ds(AT_BOTH, EDGE)], to_se),
            ),
            b_send.at[b], b_recv.at[b],
        )

    def edge_of(values, column):
        rows = [
            level * 144 + row * 24 + column
            for half in ((0, 1, 2), (3, 4, 5)) for level in (0, 1) for row in half
        ]
        return jnp.concatenate([values[r : r + 8] for r in rows], axis=0)

    def far_edge(values):
        return jnp.where(core == 0, edge_of(values, 0), edge_of(values, 16)).astype(jnp.bfloat16)

    def load_input(b):
        return pltpu.make_async_copy(
            latents.at[core + 2 * b], src.at[b, pl.ds(0, CELLS)], in_sem.at[b]
        )

    def hand_on(b):
        return pltpu.make_async_remote_copy(
            src_ref=hand_out.at[b], dst_ref=hand_in.at[b], send_sem=h_send.at[b],
            recv_sem=h_recv.at[b], device_id=other, device_id_type=MESH,
        )

    def keep_output(b, s):
        return pltpu.make_async_copy(
            stage.at[b, s], sections.at[core + 2 * b], o_recv.at[b, 0]
        )

    def give_output(b, s):
        return pltpu.make_async_remote_copy(
            src_ref=stage.at[b, s], dst_ref=sections.at[core + 2 * b], send_sem=o_send.at[b],
            recv_sem=o_recv.at[b, 1], device_id=mate, device_id_type=MESH,
        )

    barrier = pltpu.get_barrier_semaphore()
    for k in range(4):
        own_weights(0, k).start()
    for k in range(2):
        own_params(k).start()

    @pl.when(chip == 0)
    def _():
        for b in range(2):
            load_input(b).start()

    for to in (to_n, to_s, to_w, to_e, to_nw, to_se, mate, other):
        pl.semaphore_signal(barrier, inc=1, device_id=to, device_id_type=MESH)
    pl.semaphore_wait(barrier, 8)

    for k in range(2):
        lent_params(k).start()
    for i in range(2):
        for k in range(4):
            lent_weights(i, k).start()
            if i == 1:
                own_weights(i, k).start()

    @pl.when(chip == 0)
    def _():
        for b in range(2):
            load_input(b).wait()
            entry = src[b, 0:CELLS].astype(jnp.float32)
            x[b] = entry
            packed[b] = far_edge(entry)
            for copy in forth(b):
                copy.start()

    @pl.when(chip == 1)
    def _():
        for b in range(2):
            hand_on(b).wait_recv()
            src[b, 0:CELLS] = hand_in[b]
            entry = hand_in[b].astype(jnp.float32)
            x[b] = entry
            packed[b] = far_edge(entry)
            for copy in forth(b):
                copy.start()

    for k, (held, kept) in enumerate(tiny):
        own_params(k).wait()
        pltpu.make_async_copy(
            held, kept.at[pl.ds(mate_core * 2, 2)], p_recv.at[mate_core, k]
        ).wait()

    rows = lax.broadcasted_iota(jnp.int32, (HALF, HALF), 0)
    cols = lax.broadcasted_iota(jnp.int32, (HALF, HALF), 1)
    split = (rows < PART) != (cols < PART)
    is_last = jnp.where(lat == (lat_n - 1) * (1 - core), 1.0, 0.0)
    cross[...] = jnp.where(split, -BIG, 0.0) * is_last
    r256 = lax.broadcasted_iota(jnp.int32, (256, 256), 0)
    c256 = lax.broadcasted_iota(jnp.int32, (256, 256), 1)
    ones[...] = jnp.where(r256 // 64 == c256 // 64, 1.0, 0.0).astype(jnp.bfloat16)

    place = lax.broadcasted_iota(jnp.int32, (CELLS, WIDE), 1).astype(jnp.float32)

    def choose(l, carry):
        f_lat = small[l, 0:1, 0:1]
        f_lon = small[l, 0:1, 1:2]
        picks = (
            (1.0 - f_lat) * (1.0 - f_lon), (1.0 - f_lat) * f_lon,
            f_lat * (1.0 - f_lon), f_lat * f_lon,
        )
        for first, kept in ((0, fwd), (4, bwd)):
            at = sum(
                jnp.where(
                    core == 0, table[:, first + i : first + i + 1],
                    table[:, first + i + 8 : first + i + 9],
                ) * picks[i]
                for i in range(4)
            )
            kept[l] = jnp.where(place == at, 1.0, 0.0).astype(jnp.bfloat16)
        return carry

    lax.fori_loop(0, SLOTS, choose, 0)

    lane = lax.broadcasted_iota(jnp.int32, (1, 256), 1)
    masks = [jnp.where(lane // 64 == h, 1.0, 0.0).astype(jnp.bfloat16) for h in range(4)]
    first_of_pair = lax.broadcasted_iota(jnp.int32, (HALF, 128), 1) < 64

    def unit(block):
        total = dot((block * block).astype(jnp.bfloat16), ones[...])
        return (block * lax.rsqrt(total + 1e-06)).astype(jnp.bfloat16)

    def attend(b, l):
        for copy in forth(b):
            copy.wait()
        cells = dot(fwd[l], src[b]).astype(jnp.bfloat16)
        bias = small[l, 0:1, 0:1] * cross[...]
        done = [[], []]
        for g in range(2):
            lanes = [slice(p * 512 + g * 256, p * 512 + g * 256 + 256) for p in range(3)]
            q = unit(dot(cells, wq[l, :, lanes[0]]))
            k = unit(dot(cells, wq[l, :, lanes[1]]))
            v = dot(cells, wq[l, :, lanes[2]]).astype(jnp.bfloat16)
            for w in range(2):
                part = slice(w * HALF, w * HALF + HALF)
                heads = jnp.concatenate([q[part] * masks[h] for h in range(4)], axis=0)
                scores = lax.dot_general(
                    heads, k[part], (((1,), (1,)), ((), ())), preferred_element_type=jnp.float32
                )
                expos, shares = [], []
                for h in range(4):
                    scale = small[l, 0:1, 2 + g * 4 + h : 3 + g * 4 + h]
                    score = scores[h * HALF : h * HALF + HALF] * scale + bias
                    expo = jnp.exp2(score - jnp.max(score, axis=-1, keepdims=True))
                    shares.append(1.0 / jnp.sum(expo, axis=-1, keepdims=True))
                    expos.append(expo.astype(jnp.bfloat16))
                mixed = dot(jnp.concatenate(expos, axis=0), v[part])
                for p in range(2):
                    at = slice(p * 128, p * 128 + 128)
                    one = mixed[2 * p * HALF : (2 * p + 1) * HALF, at] * shares[2 * p]
                    two = mixed[(2 * p + 1) * HALF : (2 * p + 2) * HALF, at] * shares[2 * p + 1]
                    done[w].append(jnp.where(first_of_pair, one, two).astype(jnp.bfloat16))
        for w in range(2):
            ret[b, w * HALF : w * HALF + HALF] = jnp.concatenate(done[w], axis=1)
        for copy in back(b):
            copy.start()

    def feed(b, l):
        for copy in back(b):
            copy.wait()
        mixed = dot(bwd[l], ret[b]).astype(jnp.bfloat16)
        state = x[b]
        first = state + normed(dot(mixed, wo[l]), gains[l, 0:1])
        firstb = first.astype(jnp.bfloat16)
        hidden = jnp.concatenate(
            [
                gelu(dot(firstb, wu[l, :, c : c + 256])).astype(jnp.bfloat16)
                for c in range(0, 2048, 256)
            ],
            axis=1,
        )
        second = first + normed(dot(hidden, wd[l]), gains[l, 1:2])
        s = l // 2
        applied = lax.rem(l, 2) < depth_ref[chip * 2 + s]
        fresh = jnp.where(applied, second, state)
        x[b] = fresh
        freshb = fresh.astype(jnp.bfloat16)

        @pl.when(l < SLOTS - 1)
        def _():
            src[b, 0:CELLS] = freshb
            packed[b] = far_edge(fresh)
            for copy in forth(b):
                copy.start()

        @pl.when(lax.rem(l, 2) == 1)
        def _():
            stage[b, s] = fresh

            @pl.when(s == core)
            def _():
                keep_output(b, s).start()

            @pl.when(s != core)
            def _():
                give_output(b, s).start()

        @pl.when((l == SLOTS - 1) & (chip == 0))
        def _():
            hand_out[b] = freshb
            hand_on(b).start()

    def layer(l, carry):
        weights_here(l, 0)

        def one(b, c):
            attend(b, l)
            return c

        lax.fori_loop(0, 2, one, 0)
        for k in range(1, 4):
            weights_here(l, k)

        def two(b, c):
            feed(b, l)
            return c

        lax.fori_loop(0, 2, two, 0)
        return carry

    lax.fori_loop(0, SLOTS, layer, 0)

    for i in range(2):
        for k in range(4):
            lent_weights(i, k).wait_send()
    for k in range(2):
        lent_params(k).wait_send()

    @pl.when(chip == 0)
    def _():
        for b in range(2):
            hand_on(b).wait_send()

    for b in range(2):
        keep_output(b, core).wait()
        give_output(b, mate_core).wait()


def shards(latents, segment_depth, shift_flags, w_qkv, w_out, w_up, w_down, gains, logit_scale,
           lon_n, lat_n):
    micro, levels, clat, clon, width = latents.shape
    cells = latents.reshape(micro, CELLS, width)
    small = jnp.concatenate(
        [shift_flags.astype(jnp.float32), logit_scale * LOG2E, jnp.zeros((2, 118), jnp.float32)],
        axis=1,
    ).reshape(2, 1, 128)
    table = jnp.asarray(moves())
    hbm = pl.BlockSpec(memory_space=pl.ANY)
    bf16, f32 = jnp.bfloat16, jnp.float32
    dma = pltpu.SemaphoreType.DMA
    out = pl.pallas_call(
        functools.partial(kernel, lon_n, lat_n),
        out_shape=jax.ShapeDtypeStruct((micro, CELLS, width), f32),
        in_specs=[
            pl.BlockSpec(memory_space=pltpu.SMEM), hbm, hbm, hbm,
            pl.BlockSpec(memory_space=pltpu.VMEM), hbm, hbm, hbm, hbm,
        ],
        out_specs=hbm,
        scratch_shapes=[
            pltpu.VMEM((SLOTS, width, 3 * width), bf16),
            pltpu.VMEM((SLOTS, width, width), bf16),
            pltpu.VMEM((SLOTS, width, 4 * width), bf16),
            pltpu.VMEM((SLOTS, 4 * width, width), bf16),
            pltpu.VMEM((SLOTS, 1, 128), f32),
            pltpu.VMEM((SLOTS, 2, width), f32),
            pltpu.VMEM((SLOTS, CELLS, WIDE), bf16),
            pltpu.VMEM((SLOTS, CELLS, WIDE), bf16),
            pltpu.VMEM((2, CELLS, width), f32),
            pltpu.VMEM((2, WIDE, width), bf16),
            pltpu.VMEM((2, 2 * EDGE, width), bf16),
            pltpu.VMEM((2, WIDE, width), bf16),
            pltpu.VMEM((2, 2, CELLS, width), f32),
            pltpu.VMEM((2, CELLS, width), bf16),
            pltpu.VMEM((2, CELLS, width), bf16),
            pltpu.VMEM((HALF, HALF), f32),
            pltpu.VMEM((256, 256), bf16),
            dma((SLOTS, 4)), dma((2, 4)), dma((2, 2)), dma((2,)),
            dma((2, 4)), dma((2, 4)), dma((2, 5)), dma((2, 5)),
            dma((2,)), dma((2,)), dma((2,)), dma((2, 2)), dma((2,)),
        ],
        compiler_params=pltpu.CompilerParams(
            collective_id=0, has_side_effects=True, vmem_limit_bytes=60 * 1024 * 1024
        ),
        cost_estimate=pl.CostEstimate(
            flops=16 * 2 * 10**9, bytes_accessed=20 * 10**6, transcendentals=10**7
        ),
    )(segment_depth, cells, small, gains, table, w_qkv, w_out, w_up, w_down)
    return out.reshape(1, micro, levels, clat, clon, width)


def solution(mesh):
    placed = (
        P(None, None, "lat", "lon", None),
        P(),
        P("segment", None),
        P("segment", None, None),
        P("segment", None, None),
        P("segment", None, None),
        P("segment", None, None),
        P("segment", None, None),
        P("segment", None),
    )
    return jax.shard_map(
        functools.partial(shards, lon_n=mesh.shape["lon"], lat_n=mesh.shape["lat"]),
        mesh=mesh,
        in_specs=placed,
        out_specs=P("segment", None, None, "lat", "lon", None),
        check_vma=False,
    )
```

```python
import functools

import jax
import jax.numpy as jnp
import numpy as np
from jax import lax
from jax.experimental import pallas as pl
from jax.experimental.pallas import tpu as pltpu
from jax.sharding import PartitionSpec as P

MESH = pl.DeviceIdType.MESH
HALF = 144
CELLS = 2 * HALF
PART = HALF // 2
REACH = 80
EDGE = 48
AT_LAT = CELLS
AT_LON = AT_LAT + 2 * REACH
AT_BOTH = AT_LON + 2 * EDGE
WIDE = AT_BOTH + EDGE
SLOTS = 4
LENGTHS = ((2, 3), (2, 4), (3, 2), (3, 3), (3, 4), (4, 2), (4, 3))
LOG2E = 1.4426950408889634
BIG = 1e30


def moves():
    table = np.zeros((CELLS, 128), np.float32)
    for core in range(2):
        far_half = 1 - core
        for lat in range(2):
            for lon in range(2):
                which = core * 8 + lat * 2 + lon
                for at in range(CELLS):
                    window, half, pair, cell = at // 144, at % 144 // 72, at % 72 // 36, at % 36
                    level, row, column = cell // 18, cell % 18 // 6, cell % 6
                    column += (2 * window + pair) * 6 + lon * (6 - 12 * core)
                    across = column >= 24 or column < 0
                    edge_column = column - 24 if core == 0 else column + 24 - 16
                    along = lat == 1 and half == far_half
                    source = 1 - half if lat else half
                    edge = (level * 3 + row) * 8 + edge_column
                    if along and across:
                        take = AT_BOTH + edge
                    elif along:
                        take = AT_LAT + level * REACH + core * 8 + row * 24 + column
                    elif across:
                        take = AT_LON + source * EDGE + edge
                    else:
                        take = level * 144 + (source * 3 + row) * 24 + column
                    table[at, which] = take

                    level, row, column = at // 144, at % 144 // 24, at % 24
                    half, row = row // 3, row % 3
                    along = lat == 1 and half == core
                    source = 1 - half if lat else half
                    column -= lon * (6 - 12 * core)
                    across = column >= 24 or column < 0
                    column %= 24
                    window, pair = column // 12, column % 12 // 6
                    inside = source * 72 + pair * 36 + level * 18 + row * 6 + column % 6
                    if along and across:
                        take = AT_BOTH + inside - (0 if core else 96)
                    elif along:
                        take = AT_LAT + window * REACH + inside - (0 if core else 64)
                    elif across:
                        take = AT_LON + source * EDGE + inside - source * 64 - (0 if core else 32)
                    else:
                        take = window * 144 + inside
                    table[at, which + 4] = take
    return table


def normed(values, gain):
    mean = jnp.mean(values, axis=-1, keepdims=True)
    centred = values - mean
    var = jnp.mean(centred * centred, axis=-1, keepdims=True)
    return centred * lax.rsqrt(var + 1e-05) * gain


def gelu(u):
    inner = u * (0.7978845608028654 + 0.035677408136300125 * (u * u))
    half = 0.5 * u
    return half + half * jnp.tanh(inner)


def dot(a, b):
    return jnp.dot(a, b, preferred_element_type=jnp.float32)


def kernel(
    lon_n, lat_n, lengths, depth_ref, latents, small_in, gains_in, table, w_qkv, w_out, w_up, w_down, sections,
    wq_a, wo_a, wu_a, wd_a, wq_b, wo_b, wu_b, wd_b, small, gains, fwd, bwd, x, src, packed, ret, stage, hand_out, hand_in, cross, ones,
    w_recv, w_send, p_recv, p_send, f_recv, f_send, b_recv, b_send, in_sem, h_recv, h_send,
    o_recv, o_send,
):
    seg = lax.axis_index("segment")
    lon = lax.axis_index("lon")
    lat = lax.axis_index("lat")
    chip = seg // 2
    core = lax.rem(seg, 2)
    mate_core = 1 - core
    north, south = lax.rem(lat + lat_n - 1, lat_n), lax.rem(lat + 1, lat_n)
    west, east = lax.rem(lon + lon_n - 1, lon_n), lax.rem(lon + 1, lon_n)

    def device(s, o, a):
        return {"segment": s, "lon": o, "lat": a}

    out_lat, home_lat = north + core * (south - north), south + core * (north - south)
    out_lon, home_lon = west + core * (east - west), east + core * (west - east)
    to_n, to_s = device(seg, lon, out_lat), device(seg, lon, home_lat)
    to_w, to_e = device(seg, out_lon, lat), device(seg, home_lon, lat)
    to_nw, to_se = device(seg, out_lon, out_lat), device(seg, home_lon, home_lat)
    mate = device(chip * 2 + mate_core, lon, lat)
    other = device(lax.rem(seg + 2, 4), lon, lat)

    steps = lengths[0] + chip * (lengths[1] - lengths[0])
    depth = depth_ref[2 * chip]

    first_weights = (wq_a, wo_a, wu_a, wd_a)
    later_weights = (wq_b, wo_b, wu_b, wd_b)
    held_weights = (w_qkv, w_out, w_up, w_down)

    def each_weight(i, k, act):
        if i == 1:
            act(held_weights[k].at[1], later_weights[k].at[2 * core])
            return

        @pl.when(core == 0)
        def _():
            act(held_weights[k].at[0], first_weights[k])

        @pl.when(core == 1)
        def _():
            act(held_weights[k].at[0], later_weights[k].at[1])

    def own_weights(i, k):
        slot = core * 2 + i
        each_weight(
            i, k,
            lambda held, kept: pltpu.make_async_copy(held, kept, w_recv.at[slot, k]).start(),
        )

    def lent_weights(i, k, act):
        slot = core * 2 + i
        each_weight(
            i, k,
            lambda held, kept: act(
                pltpu.make_async_remote_copy(
                    src_ref=held, dst_ref=kept, send_sem=w_send.at[i, k],
                    recv_sem=w_recv.at[slot, k], device_id=mate, device_id_type=MESH,
                )
            ),
        )

    def weights_here(slot, k):
        kept = first_weights[k] if slot == 0 else later_weights[k].at[slot - 1]
        pltpu.make_async_copy(held_weights[k].at[0], kept, w_recv.at[slot, k]).wait()

    tiny = ((small_in, small), (gains_in, gains))

    def own_params(k):
        held, kept = tiny[k]
        return pltpu.make_async_copy(held, kept.at[pl.ds(core * 2, 2)], p_recv.at[core, k])

    def lent_params(k):
        held, kept = tiny[k]
        return pltpu.make_async_remote_copy(
            src_ref=held, dst_ref=kept.at[pl.ds(core * 2, 2)], send_sem=p_send.at[k],
            recv_sem=p_recv.at[core, k], device_id=mate, device_id_type=MESH,
        )

    def edges(pieces, send, recv):
        return [
            pltpu.make_async_remote_copy(
                src_ref=source, dst_ref=target, send_sem=send.at[i], recv_sem=recv.at[i],
                device_id=to, device_id_type=MESH,
            )
            for i, (source, target, to) in enumerate(pieces)
        ]

    def rows_from(start, size):
        return pl.ds(pl.multiple_of(start, 16), size)

    def forth(b):
        return edges(
            (
                (src.at[b, rows_from(64 * core, REACH)], src.at[b, pl.ds(AT_LAT, REACH)], to_n),
                (
                    src.at[b, rows_from(HALF + 64 * core, REACH)],
                    src.at[b, pl.ds(AT_LAT + REACH, REACH)], to_n,
                ),
                (packed.at[b], src.at[b, pl.ds(AT_LON, 2 * EDGE)], to_w),
                (packed.at[b, rows_from(EDGE * core, EDGE)], src.at[b, pl.ds(AT_BOTH, EDGE)], to_nw),
            ),
            f_send.at[b], f_recv.at[b],
        )

    def back(b):
        return edges(
            (
                (ret.at[b, rows_from(64 - 64 * core, REACH)], ret.at[b, pl.ds(AT_LAT, REACH)], to_s),
                (
                    ret.at[b, rows_from(208 - 64 * core, REACH)],
                    ret.at[b, pl.ds(AT_LAT + REACH, REACH)], to_s,
                ),
                (ret.at[b, rows_from(176 - 176 * core, EDGE)], ret.at[b, pl.ds(AT_LON, EDGE)], to_e),
                (
                    ret.at[b, rows_from(240 - 176 * core, EDGE)],
                    ret.at[b, pl.ds(AT_LON + EDGE, EDGE)], to_e,
                ),
                (ret.at[b, rows_from(240 - 240 * core, EDGE)], ret.at[b, pl.ds(AT_BOTH, EDGE)], to_se),
            ),
            b_send.at[b], b_recv.at[b],
        )

    def edge_of(values, column):
        rows = [
            level * 144 + row * 24 + column
            for half in ((0, 1, 2), (3, 4, 5)) for level in (0, 1) for row in half
        ]
        return jnp.concatenate([values[r : r + 8] for r in rows], axis=0)

    def far_edge(values):
        return jnp.where(core == 0, edge_of(values, 0), edge_of(values, 16)).astype(jnp.bfloat16)

    def load_input(b):
        return pltpu.make_async_copy(
            latents.at[core + 2 * b], src.at[b, pl.ds(0, CELLS)], in_sem.at[b]
        )

    def hand_on(b):
        return pltpu.make_async_remote_copy(
            src_ref=hand_out.at[b], dst_ref=hand_in.at[b], send_sem=h_send.at[b],
            recv_sem=h_recv.at[b], device_id=other, device_id_type=MESH,
        )

    def keep_output(b, s):
        return pltpu.make_async_copy(
            stage.at[b, s], sections.at[core + 2 * b], o_recv.at[b, 0]
        )

    def give_output(b, s):
        return pltpu.make_async_remote_copy(
            src_ref=stage.at[b, s], dst_ref=sections.at[core + 2 * b], send_sem=o_send.at[b],
            recv_sem=o_recv.at[b, 1], device_id=mate, device_id_type=MESH,
        )

    barrier = pltpu.get_barrier_semaphore()
    for k in range(4):
        own_weights(0, k)
    for k in range(2):
        own_params(k).start()

    @pl.when(chip == 0)
    def _():
        for b in range(2):
            load_input(b).start()

    for to in (to_n, to_s, to_w, to_e, to_nw, to_se, mate, other):
        pl.semaphore_signal(barrier, inc=1, device_id=to, device_id_type=MESH)
    pl.semaphore_wait(barrier, 8)

    for k in range(2):
        lent_params(k).start()
    for i in range(2):
        for k in range(4):
            lent_weights(i, k, lambda copy: copy.start())
            if i == 1:
                own_weights(i, k)

    @pl.when(chip == 0)
    def _():
        for b in range(2):
            load_input(b).wait()
            entry = src[b, 0:CELLS].astype(jnp.float32)
            x[b] = entry
            packed[b] = far_edge(entry)
            for copy in forth(b):
                copy.start()

    @pl.when(chip == 1)
    def _():
        for b in range(2):
            hand_on(b).wait_recv()
            src[b, 0:CELLS] = hand_in[b]
            entry = hand_in[b].astype(jnp.float32)
            x[b] = entry
            packed[b] = far_edge(entry)
            for copy in forth(b):
                copy.start()

    for k, (held, kept) in enumerate(tiny):
        own_params(k).wait()
        pltpu.make_async_copy(
            held, kept.at[pl.ds(mate_core * 2, 2)], p_recv.at[mate_core, k]
        ).wait()

    rows = lax.broadcasted_iota(jnp.int32, (HALF, HALF), 0)
    cols = lax.broadcasted_iota(jnp.int32, (HALF, HALF), 1)
    split = (rows < PART) != (cols < PART)
    is_last = jnp.where(lat == (lat_n - 1) * (1 - core), 1.0, 0.0)
    cross[...] = jnp.where(split, -BIG, 0.0) * is_last
    r256 = lax.broadcasted_iota(jnp.int32, (256, 256), 0)
    c256 = lax.broadcasted_iota(jnp.int32, (256, 256), 1)
    ones[...] = jnp.where(r256 // 64 == c256 // 64, 1.0, 0.0).astype(jnp.bfloat16)

    place = lax.broadcasted_iota(jnp.int32, (CELLS, WIDE), 1).astype(jnp.float32)

    def slot_of(step):
        return jnp.clip(step + jnp.where(step == 0, 0, 2 - depth), 0, SLOTS - 1)

    def choose(step, carry):
        f_lat = small[slot_of(step), 0:1, 0:1]
        f_lon = small[slot_of(step), 0:1, 1:2]
        picks = (
            (1.0 - f_lat) * (1.0 - f_lon), (1.0 - f_lat) * f_lon,
            f_lat * (1.0 - f_lon), f_lat * f_lon,
        )
        for first, kept in ((0, fwd), (4, bwd)):
            at = sum(
                jnp.where(
                    core == 0, table[:, first + i : first + i + 1],
                    table[:, first + i + 8 : first + i + 9],
                ) * picks[i]
                for i in range(4)
            )
            kept[step] = jnp.where(place == at, 1.0, 0.0).astype(jnp.bfloat16)
        return carry

    lax.fori_loop(0, steps, choose, 0)

    lane = lax.broadcasted_iota(jnp.int32, (1, 256), 1)
    masks = [jnp.where(lane // 64 == h, 1.0, 0.0).astype(jnp.bfloat16) for h in range(4)]
    first_of_pair = lax.broadcasted_iota(jnp.int32, (HALF, 128), 1) < 64

    def unit(block):
        total = dot((block * block).astype(jnp.bfloat16), ones[...])
        return (block * lax.rsqrt(total + 1e-06)).astype(jnp.bfloat16)

    def attend(b, step, l, weight):
        for copy in forth(b):
            copy.wait()
        cells = dot(fwd[step], src[b]).astype(jnp.bfloat16)
        bias = small[l, 0:1, 0:1] * cross[...]
        done = [[], []]
        for g in range(2):
            lanes = [slice(p * 512 + g * 256, p * 512 + g * 256 + 256) for p in range(3)]
            q = unit(dot(cells, weight(0, lanes[0])))
            k = unit(dot(cells, weight(0, lanes[1])))
            v = dot(cells, weight(0, lanes[2])).astype(jnp.bfloat16)
            for w in range(2):
                part = slice(w * HALF, w * HALF + HALF)
                heads = jnp.concatenate([q[part] * masks[h] for h in range(4)], axis=0)
                scores = lax.dot_general(
                    heads, k[part], (((1,), (1,)), ((), ())), preferred_element_type=jnp.float32
                )
                expos, shares = [], []
                for h in range(4):
                    scale = small[l, 0:1, 2 + g * 4 + h : 3 + g * 4 + h]
                    score = scores[h * HALF : h * HALF + HALF] * scale + bias
                    expo = jnp.exp2(score - jnp.max(score, axis=-1, keepdims=True))
                    shares.append(1.0 / jnp.sum(expo, axis=-1, keepdims=True))
                    expos.append(expo.astype(jnp.bfloat16))
                mixed = dot(jnp.concatenate(expos, axis=0), v[part])
                for p in range(2):
                    at = slice(p * 128, p * 128 + 128)
                    one = mixed[2 * p * HALF : (2 * p + 1) * HALF, at] * shares[2 * p]
                    two = mixed[(2 * p + 1) * HALF : (2 * p + 2) * HALF, at] * shares[2 * p + 1]
                    done[w].append(jnp.where(first_of_pair, one, two).astype(jnp.bfloat16))
        for w in range(2):
            ret[b, w * HALF : w * HALF + HALF] = jnp.concatenate(done[w], axis=1)
        for copy in back(b):
            copy.start()

    def feed(b, step, l, weight):
        for copy in back(b):
            copy.wait()
        mixed = dot(bwd[step], ret[b]).astype(jnp.bfloat16)
        state = x[b]
        first = state + normed(dot(mixed, weight(1)), gains[l, 0:1])
        firstb = first.astype(jnp.bfloat16)
        hidden = jnp.concatenate(
            [
                gelu(dot(firstb, weight(2, slice(c, c + 256)))).astype(jnp.bfloat16)
                for c in range(0, 2048, 256)
            ],
            axis=1,
        )
        fresh = first + normed(dot(hidden, weight(3)), gains[l, 1:2])
        x[b] = fresh

        @pl.when(step < steps - 1)
        def _():
            src[b, 0:CELLS] = fresh.astype(jnp.bfloat16)
            packed[b] = far_edge(fresh)
            for copy in forth(b):
                copy.start()

        def emit(s, value):
            stage[b, s] = value

            @pl.when(s == core)
            def _():
                keep_output(b, s).start()

            @pl.when(s != core)
            def _():
                give_output(b, s).start()

        @pl.when(step == 1)
        def _():
            emit(0, jnp.where(depth == 1, state, fresh))

        @pl.when(step == steps - 1)
        def _():
            emit(1, fresh)

            @pl.when(chip == 0)
            def _():
                hand_out[b] = fresh.astype(jnp.bfloat16)
                hand_on(b).start()

    def layer(step, l, weight):
        def one(b, c):
            attend(b, step, l, weight)
            return c

        def two(b, c):
            feed(b, step, l, weight)
            return c

        return one, two

    def weight_a(k, lanes=slice(None)):
        return first_weights[k][:, lanes]

    weights_here(0, 0)
    one, two = layer(0, 0, weight_a)
    lax.fori_loop(0, 2, one, 0)
    for k in range(1, 4):
        weights_here(0, k)
    lax.fori_loop(0, 2, two, 0)

    for slot in range(1, SLOTS):
        for k in range(4):
            weights_here(slot, k)

    def later(step, carry):
        l = slot_of(step)

        def weight_b(k, lanes=slice(None)):
            return later_weights[k][jnp.maximum(l, 1) - 1, :, lanes]

        one, two = layer(step, l, weight_b)
        lax.fori_loop(0, 2, one, 0)
        lax.fori_loop(0, 2, two, 0)
        return carry

    lax.fori_loop(1, steps, later, 0)

    for i in range(2):
        for k in range(4):
            lent_weights(i, k, lambda copy: copy.wait_send())
    for k in range(2):
        lent_params(k).wait_send()

    @pl.when(chip == 0)
    def _():
        for b in range(2):
            hand_on(b).wait_send()

    for b in range(2):
        keep_output(b, core).wait()
        give_output(b, mate_core).wait()


def shards(latents, segment_depth, shift_flags, w_qkv, w_out, w_up, w_down, gains, logit_scale,
           lon_n, lat_n):
    micro, levels, clat, clon, width = latents.shape
    cells = latents.reshape(micro, CELLS, width)
    small = jnp.concatenate(
        [shift_flags.astype(jnp.float32), logit_scale * LOG2E, jnp.zeros((2, 118), jnp.float32)],
        axis=1,
    ).reshape(2, 1, 128)
    table = jnp.asarray(moves())
    hbm = pl.BlockSpec(memory_space=pl.ANY)
    bf16, f32 = jnp.bfloat16, jnp.float32
    dma = pltpu.SemaphoreType.DMA
    def run(which):
        lengths = LENGTHS[which]
        return pl.pallas_call(
            functools.partial(kernel, lon_n, lat_n, lengths),
            out_shape=jax.ShapeDtypeStruct((micro, CELLS, width), f32),
            in_specs=[
                pl.BlockSpec(memory_space=pltpu.SMEM), hbm, hbm, hbm,
                pl.BlockSpec(memory_space=pltpu.VMEM), hbm, hbm, hbm, hbm,
            ],
            out_specs=hbm,
            scratch_shapes=[
                pltpu.VMEM((width, 3 * width), bf16),
                pltpu.VMEM((width, width), bf16),
                pltpu.VMEM((width, 4 * width), bf16),
                pltpu.VMEM((4 * width, width), bf16),
                pltpu.VMEM((SLOTS - 1, width, 3 * width), bf16),
                pltpu.VMEM((SLOTS - 1, width, width), bf16),
                pltpu.VMEM((SLOTS - 1, width, 4 * width), bf16),
                pltpu.VMEM((SLOTS - 1, 4 * width, width), bf16),
                pltpu.VMEM((SLOTS, 1, 128), f32),
                pltpu.VMEM((SLOTS, 2, width), f32),
                pltpu.VMEM((SLOTS, CELLS, WIDE), bf16),
                pltpu.VMEM((SLOTS, CELLS, WIDE), bf16),
                pltpu.VMEM((2, CELLS, width), f32),
                pltpu.VMEM((2, WIDE, width), bf16),
                pltpu.VMEM((2, 2 * EDGE, width), bf16),
                pltpu.VMEM((2, WIDE, width), bf16),
                pltpu.VMEM((2, 2, CELLS, width), f32),
                pltpu.VMEM((2, CELLS, width), bf16),
                pltpu.VMEM((2, CELLS, width), bf16),
                pltpu.VMEM((HALF, HALF), f32),
                pltpu.VMEM((256, 256), bf16),
                dma((SLOTS, 4)), dma((2, 4)), dma((2, 2)), dma((2,)),
                dma((2, 4)), dma((2, 4)), dma((2, 5)), dma((2, 5)),
                dma((2,)), dma((2,)), dma((2,)), dma((2, 2)), dma((2,)),
            ],
            compiler_params=pltpu.CompilerParams(
                collective_id=which, has_side_effects=True, vmem_limit_bytes=60 * 1024 * 1024
            ),
            cost_estimate=pl.CostEstimate(
                flops=16 * 2 * 10**9, bytes_accessed=20 * 10**6, transcendentals=10**7
            ),
        )

    operands = (segment_depth, cells, small, gains, table, w_qkv, w_out, w_up, w_down)
    lengths = segment_depth[0:2].sum(), segment_depth[2:4].sum()
    out = lax.switch(
        (lengths[0] - 2) * 3 + lengths[1] - 3,
        [run(which) for which in range(len(LENGTHS))],
        *operands,
    )
    return out.reshape(1, micro, levels, clat, clon, width)


def solution(mesh):
    placed = (
        P(None, None, "lat", "lon", None),
        P(),
        P("segment", None),
        P("segment", None, None),
        P("segment", None, None),
        P("segment", None, None),
        P("segment", None, None),
        P("segment", None, None),
        P("segment", None),
    )
    return jax.shard_map(
        functools.partial(shards, lon_n=mesh.shape["lon"], lat_n=mesh.shape["lat"]),
        mesh=mesh,
        in_specs=placed,
        out_specs=P("segment", None, None, "lat", "lon", None),
        check_vma=False,
    )
```

```python
import functools

import jax
import jax.numpy as jnp
import numpy as np
from jax import lax
from jax.experimental import pallas as pl
from jax.experimental.pallas import tpu as pltpu
from jax.sharding import PartitionSpec as P

MESH = pl.DeviceIdType.MESH
HALF = 144
CELLS = 2 * HALF
PART = HALF // 2
REACH = 80
EDGE = 48
AT_LAT = CELLS
AT_LON = AT_LAT + 2 * REACH
AT_BOTH = AT_LON + 2 * EDGE
WIDE = AT_BOTH + EDGE
SLOTS = 4
LENGTHS = ((3, 3), (4, 3), (3, 4))
LOG2E = 1.4426950408889634
BIG = 1e30


def moves():
    table = np.zeros((CELLS, 128), np.float32)
    for core in range(2):
        far_half = 1 - core
        for lat in range(2):
            for lon in range(2):
                which = core * 8 + lat * 2 + lon
                for at in range(CELLS):
                    window, half, pair, cell = at // 144, at % 144 // 72, at % 72 // 36, at % 36
                    level, row, column = cell // 18, cell % 18 // 6, cell % 6
                    column += (2 * window + pair) * 6 + lon * (6 - 12 * core)
                    across = column >= 24 or column < 0
                    edge_column = column - 24 if core == 0 else column + 24 - 16
                    along = lat == 1 and half == far_half
                    source = 1 - half if lat else half
                    edge = (level * 3 + row) * 8 + edge_column
                    if along and across:
                        take = AT_BOTH + edge
                    elif along:
                        take = AT_LAT + level * REACH + core * 8 + row * 24 + column
                    elif across:
                        take = AT_LON + source * EDGE + edge
                    else:
                        take = level * 144 + (source * 3 + row) * 24 + column
                    table[at, which] = take

                    level, row, column = at // 144, at % 144 // 24, at % 24
                    half, row = row // 3, row % 3
                    along = lat == 1 and half == core
                    source = 1 - half if lat else half
                    column -= lon * (6 - 12 * core)
                    across = column >= 24 or column < 0
                    column %= 24
                    window, pair = column // 12, column % 12 // 6
                    inside = source * 72 + pair * 36 + level * 18 + row * 6 + column % 6
                    if along and across:
                        take = AT_BOTH + inside - (0 if core else 96)
                    elif along:
                        take = AT_LAT + window * REACH + inside - (0 if core else 64)
                    elif across:
                        take = AT_LON + source * EDGE + inside - source * 64 - (0 if core else 32)
                    else:
                        take = window * 144 + inside
                    table[at, which + 4] = take
    return table


def normed(values, gain):
    mean = jnp.mean(values, axis=-1, keepdims=True)
    centred = values - mean
    var = jnp.mean(centred * centred, axis=-1, keepdims=True)
    return centred * lax.rsqrt(var + 1e-05) * gain


def gelu(u):
    inner = u * (0.7978845608028654 + 0.035677408136300125 * (u * u))
    half = 0.5 * u
    return half + half * jnp.tanh(inner)


def dot(a, b):
    return jnp.dot(a, b, preferred_element_type=jnp.float32)


def kernel(
    lon_n, lat_n, lengths, depth_ref, latents, small_in, gains_in, table, w_qkv, w_out, w_up, w_down, sections,
    wq_a, wo_a, wu_a, wd_a, wq_b, wo_b, wu_b, wd_b, small, gains, fwd, bwd, x, src, packed, ret, stage, hand_out, hand_in, cross, ones,
    w_recv, w_send, p_recv, p_send, f_recv, f_send, b_recv, b_send, in_sem, h_recv, h_send,
    o_recv, o_send,
):
    seg = lax.axis_index("segment")
    lon = lax.axis_index("lon")
    lat = lax.axis_index("lat")
    chip = seg // 2
    core = lax.rem(seg, 2)
    mate_core = 1 - core
    north, south = lax.rem(lat + lat_n - 1, lat_n), lax.rem(lat + 1, lat_n)
    west, east = lax.rem(lon + lon_n - 1, lon_n), lax.rem(lon + 1, lon_n)

    def device(s, o, a):
        return {"segment": s, "lon": o, "lat": a}

    out_lat, home_lat = north + core * (south - north), south + core * (north - south)
    out_lon, home_lon = west + core * (east - west), east + core * (west - east)
    to_n, to_s = device(seg, lon, out_lat), device(seg, lon, home_lat)
    to_w, to_e = device(seg, out_lon, lat), device(seg, home_lon, lat)
    to_nw, to_se = device(seg, out_lon, out_lat), device(seg, home_lon, home_lat)
    mate = device(chip * 2 + mate_core, lon, lat)
    other = device(lax.rem(seg + 2, 4), lon, lat)

    steps = lengths[0] + chip * (lengths[1] - lengths[0])
    depth = depth_ref[2 * chip]
    layers = depth + depth_ref[2 * chip + 1]

    first_weights = (wq_a, wo_a, wu_a, wd_a)
    later_weights = (wq_b, wo_b, wu_b, wd_b)
    held_weights = (w_qkv, w_out, w_up, w_down)

    def each_weight(i, k, act):
        if i == 1:
            act(held_weights[k].at[1], later_weights[k].at[2 * core])
            return

        @pl.when(core == 0)
        def _():
            act(held_weights[k].at[0], first_weights[k])

        @pl.when(core == 1)
        def _():
            act(held_weights[k].at[0], later_weights[k].at[1])

    def own_weights(i, k):
        slot = core * 2 + i
        each_weight(
            i, k,
            lambda held, kept: pltpu.make_async_copy(held, kept, w_recv.at[slot, k]).start(),
        )

    def lent_weights(i, k, act):
        slot = core * 2 + i
        each_weight(
            i, k,
            lambda held, kept: act(
                pltpu.make_async_remote_copy(
                    src_ref=held, dst_ref=kept, send_sem=w_send.at[i, k],
                    recv_sem=w_recv.at[slot, k], device_id=mate, device_id_type=MESH,
                )
            ),
        )

    def weights_here(slot, k):
        kept = first_weights[k] if slot == 0 else later_weights[k].at[slot - 1]
        pltpu.make_async_copy(held_weights[k].at[0], kept, w_recv.at[slot, k]).wait()

    tiny = ((small_in, small), (gains_in, gains))

    def own_params(k):
        held, kept = tiny[k]
        return pltpu.make_async_copy(held, kept.at[pl.ds(core * 2, 2)], p_recv.at[core, k])

    def lent_params(k):
        held, kept = tiny[k]
        return pltpu.make_async_remote_copy(
            src_ref=held, dst_ref=kept.at[pl.ds(core * 2, 2)], send_sem=p_send.at[k],
            recv_sem=p_recv.at[core, k], device_id=mate, device_id_type=MESH,
        )

    def edges(pieces, send, recv):
        return [
            pltpu.make_async_remote_copy(
                src_ref=source, dst_ref=target, send_sem=send.at[i], recv_sem=recv.at[i],
                device_id=to, device_id_type=MESH,
            )
            for i, (source, target, to) in enumerate(pieces)
        ]

    def rows_from(start, size):
        return pl.ds(pl.multiple_of(start, 16), size)

    def forth(b):
        return edges(
            (
                (src.at[b, rows_from(64 * core, REACH)], src.at[b, pl.ds(AT_LAT, REACH)], to_n),
                (
                    src.at[b, rows_from(HALF + 64 * core, REACH)],
                    src.at[b, pl.ds(AT_LAT + REACH, REACH)], to_n,
                ),
                (packed.at[b], src.at[b, pl.ds(AT_LON, 2 * EDGE)], to_w),
                (packed.at[b, rows_from(EDGE * core, EDGE)], src.at[b, pl.ds(AT_BOTH, EDGE)], to_nw),
            ),
            f_send.at[b], f_recv.at[b],
        )

    def back(b):
        return edges(
            (
                (ret.at[b, rows_from(64 - 64 * core, REACH)], ret.at[b, pl.ds(AT_LAT, REACH)], to_s),
                (
                    ret.at[b, rows_from(208 - 64 * core, REACH)],
                    ret.at[b, pl.ds(AT_LAT + REACH, REACH)], to_s,
                ),
                (ret.at[b, rows_from(176 - 176 * core, EDGE)], ret.at[b, pl.ds(AT_LON, EDGE)], to_e),
                (
                    ret.at[b, rows_from(240 - 176 * core, EDGE)],
                    ret.at[b, pl.ds(AT_LON + EDGE, EDGE)], to_e,
                ),
                (ret.at[b, rows_from(240 - 240 * core, EDGE)], ret.at[b, pl.ds(AT_BOTH, EDGE)], to_se),
            ),
            b_send.at[b], b_recv.at[b],
        )

    def edge_of(values, column):
        rows = [
            level * 144 + row * 24 + column
            for half in ((0, 1, 2), (3, 4, 5)) for level in (0, 1) for row in half
        ]
        return jnp.concatenate([values[r : r + 8] for r in rows], axis=0)

    def far_edge(values):
        return jnp.where(core == 0, edge_of(values, 0), edge_of(values, 16)).astype(jnp.bfloat16)

    def load_input(b):
        return pltpu.make_async_copy(
            latents.at[core + 2 * b], src.at[b, pl.ds(0, CELLS)], in_sem.at[b]
        )

    def hand_on(b):
        return pltpu.make_async_remote_copy(
            src_ref=hand_out.at[b], dst_ref=hand_in.at[b], send_sem=h_send.at[b],
            recv_sem=h_recv.at[b], device_id=other, device_id_type=MESH,
        )

    def keep_output(b, s):
        return pltpu.make_async_copy(
            stage.at[b, s], sections.at[core + 2 * b], o_recv.at[b, 0]
        )

    def give_output(b, s):
        return pltpu.make_async_remote_copy(
            src_ref=stage.at[b, s], dst_ref=sections.at[core + 2 * b], send_sem=o_send.at[b],
            recv_sem=o_recv.at[b, 1], device_id=mate, device_id_type=MESH,
        )

    barrier = pltpu.get_barrier_semaphore()
    for k in range(4):
        own_weights(0, k)
    for k in range(2):
        own_params(k).start()

    @pl.when(chip == 0)
    def _():
        for b in range(2):
            load_input(b).start()

    for to in (to_n, to_s, to_w, to_e, to_nw, to_se, mate, other):
        pl.semaphore_signal(barrier, inc=1, device_id=to, device_id_type=MESH)
    pl.semaphore_wait(barrier, 8)

    for k in range(2):
        lent_params(k).start()
    for i in range(2):
        for k in range(4):
            lent_weights(i, k, lambda copy: copy.start())
            if i == 1:
                own_weights(i, k)

    @pl.when(chip == 0)
    def _():
        for b in range(2):
            load_input(b).wait()
            entry = src[b, 0:CELLS].astype(jnp.float32)
            x[b] = entry
            packed[b] = far_edge(entry)
            for copy in forth(b):
                copy.start()

    @pl.when(chip == 1)
    def _():
        for b in range(2):
            hand_on(b).wait_recv()
            src[b, 0:CELLS] = hand_in[b]
            entry = hand_in[b].astype(jnp.float32)
            x[b] = entry
            packed[b] = far_edge(entry)
            for copy in forth(b):
                copy.start()

    for k, (held, kept) in enumerate(tiny):
        own_params(k).wait()
        pltpu.make_async_copy(
            held, kept.at[pl.ds(mate_core * 2, 2)], p_recv.at[mate_core, k]
        ).wait()

    rows = lax.broadcasted_iota(jnp.int32, (HALF, HALF), 0)
    cols = lax.broadcasted_iota(jnp.int32, (HALF, HALF), 1)
    split = (rows < PART) != (cols < PART)
    is_last = jnp.where(lat == (lat_n - 1) * (1 - core), 1.0, 0.0)
    cross[...] = jnp.where(split, -BIG, 0.0) * is_last
    r256 = lax.broadcasted_iota(jnp.int32, (256, 256), 0)
    c256 = lax.broadcasted_iota(jnp.int32, (256, 256), 1)
    ones[...] = jnp.where(r256 // 64 == c256 // 64, 1.0, 0.0).astype(jnp.bfloat16)

    place = lax.broadcasted_iota(jnp.int32, (CELLS, WIDE), 1).astype(jnp.float32)

    def slot_of(step):
        return jnp.clip(step + jnp.where(step == 0, 0, 2 - depth), 0, SLOTS - 1)

    def choose(step, carry):
        f_lat = small[slot_of(step), 0:1, 0:1]
        f_lon = small[slot_of(step), 0:1, 1:2]
        picks = (
            (1.0 - f_lat) * (1.0 - f_lon), (1.0 - f_lat) * f_lon,
            f_lat * (1.0 - f_lon), f_lat * f_lon,
        )
        for first, kept in ((0, fwd), (4, bwd)):
            at = sum(
                jnp.where(
                    core == 0, table[:, first + i : first + i + 1],
                    table[:, first + i + 8 : first + i + 9],
                ) * picks[i]
                for i in range(4)
            )
            kept[step] = jnp.where(place == at, 1.0, 0.0).astype(jnp.bfloat16)
        return carry

    lax.fori_loop(0, steps, choose, 0)

    lane = lax.broadcasted_iota(jnp.int32, (1, 256), 1)
    masks = [jnp.where(lane // 64 == h, 1.0, 0.0).astype(jnp.bfloat16) for h in range(4)]
    first_of_pair = lax.broadcasted_iota(jnp.int32, (HALF, 128), 1) < 64

    def unit(block):
        total = dot((block * block).astype(jnp.bfloat16), ones[...])
        return (block * lax.rsqrt(total + 1e-06)).astype(jnp.bfloat16)

    def attend(b, step, l, weight):
        for copy in forth(b):
            copy.wait()
        cells = dot(fwd[step], src[b]).astype(jnp.bfloat16)
        bias = small[l, 0:1, 0:1] * cross[...]
        done = [[], []]
        for g in range(2):
            lanes = [slice(p * 512 + g * 256, p * 512 + g * 256 + 256) for p in range(3)]
            q = unit(dot(cells, weight(0, lanes[0])))
            k = unit(dot(cells, weight(0, lanes[1])))
            v = dot(cells, weight(0, lanes[2])).astype(jnp.bfloat16)
            for w in range(2):
                part = slice(w * HALF, w * HALF + HALF)
                heads = jnp.concatenate([q[part] * masks[h] for h in range(4)], axis=0)
                scores = lax.dot_general(
                    heads, k[part], (((1,), (1,)), ((), ())), preferred_element_type=jnp.float32
                )
                expos, shares = [], []
                for h in range(4):
                    scale = small[l, 0:1, 2 + g * 4 + h : 3 + g * 4 + h]
                    score = scores[h * HALF : h * HALF + HALF] * scale + bias
                    expo = jnp.exp2(score - jnp.max(score, axis=-1, keepdims=True))
                    shares.append(1.0 / jnp.sum(expo, axis=-1, keepdims=True))
                    expos.append(expo.astype(jnp.bfloat16))
                mixed = dot(jnp.concatenate(expos, axis=0), v[part])
                for p in range(2):
                    at = slice(p * 128, p * 128 + 128)
                    one = mixed[2 * p * HALF : (2 * p + 1) * HALF, at] * shares[2 * p]
                    two = mixed[(2 * p + 1) * HALF : (2 * p + 2) * HALF, at] * shares[2 * p + 1]
                    done[w].append(jnp.where(first_of_pair, one, two).astype(jnp.bfloat16))
        for w in range(2):
            ret[b, w * HALF : w * HALF + HALF] = jnp.concatenate(done[w], axis=1)
        for copy in back(b):
            copy.start()

    def feed(b, step, l, weight):
        for copy in back(b):
            copy.wait()
        mixed = dot(bwd[step], ret[b]).astype(jnp.bfloat16)
        state = x[b]
        first = state + normed(dot(mixed, weight(1)), gains[l, 0:1])
        firstb = first.astype(jnp.bfloat16)
        hidden = jnp.concatenate(
            [
                gelu(dot(firstb, weight(2, slice(c, c + 256)))).astype(jnp.bfloat16)
                for c in range(0, 2048, 256)
            ],
            axis=1,
        )
        fresh = first + normed(dot(hidden, weight(3)), gains[l, 1:2])
        fresh = jnp.where(step < layers, fresh, state)
        x[b] = fresh

        @pl.when(step < steps - 1)
        def _():
            src[b, 0:CELLS] = fresh.astype(jnp.bfloat16)
            packed[b] = far_edge(fresh)
            for copy in forth(b):
                copy.start()

        def emit(s, value):
            stage[b, s] = value

            @pl.when(s == core)
            def _():
                keep_output(b, s).start()

            @pl.when(s != core)
            def _():
                give_output(b, s).start()

        @pl.when(step == 1)
        def _():
            emit(0, jnp.where(depth == 1, state, fresh))

        @pl.when(step == steps - 1)
        def _():
            emit(1, fresh)

            @pl.when(chip == 0)
            def _():
                hand_out[b] = fresh.astype(jnp.bfloat16)
                hand_on(b).start()

    def layer(step, l, weight):
        def one(b, c):
            attend(b, step, l, weight)
            return c

        def two(b, c):
            feed(b, step, l, weight)
            return c

        return one, two

    def weight_a(k, lanes=slice(None)):
        return first_weights[k][:, lanes]

    weights_here(0, 0)
    one, two = layer(0, 0, weight_a)
    lax.fori_loop(0, 2, one, 0)
    for k in range(1, 4):
        weights_here(0, k)
    lax.fori_loop(0, 2, two, 0)

    for slot in range(1, SLOTS):
        for k in range(4):
            weights_here(slot, k)

    def later(step, carry):
        l = slot_of(step)

        def weight_b(k, lanes=slice(None)):
            return later_weights[k][jnp.maximum(l, 1) - 1, :, lanes]

        one, two = layer(step, l, weight_b)
        lax.fori_loop(0, 2, one, 0)
        lax.fori_loop(0, 2, two, 0)
        return carry

    lax.fori_loop(1, steps, later, 0)

    for i in range(2):
        for k in range(4):
            lent_weights(i, k, lambda copy: copy.wait_send())
    for k in range(2):
        lent_params(k).wait_send()

    @pl.when(chip == 0)
    def _():
        for b in range(2):
            hand_on(b).wait_send()

    for b in range(2):
        keep_output(b, core).wait()
        give_output(b, mate_core).wait()


def shards(latents, segment_depth, shift_flags, w_qkv, w_out, w_up, w_down, gains, logit_scale,
           lon_n, lat_n):
    micro, levels, clat, clon, width = latents.shape
    cells = latents.reshape(micro, CELLS, width)
    small = jnp.concatenate(
        [shift_flags.astype(jnp.float32), logit_scale * LOG2E, jnp.zeros((2, 118), jnp.float32)],
        axis=1,
    ).reshape(2, 1, 128)
    table = jnp.asarray(moves())
    hbm = pl.BlockSpec(memory_space=pl.ANY)
    bf16, f32 = jnp.bfloat16, jnp.float32
    dma = pltpu.SemaphoreType.DMA
    def run(which):
        lengths = LENGTHS[which]
        return pl.pallas_call(
            functools.partial(kernel, lon_n, lat_n, lengths),
            out_shape=jax.ShapeDtypeStruct((micro, CELLS, width), f32),
            in_specs=[
                pl.BlockSpec(memory_space=pltpu.SMEM), hbm, hbm, hbm,
                pl.BlockSpec(memory_space=pltpu.VMEM), hbm, hbm, hbm, hbm,
            ],
            out_specs=hbm,
            scratch_shapes=[
                pltpu.VMEM((width, 3 * width), bf16),
                pltpu.VMEM((width, width), bf16),
                pltpu.VMEM((width, 4 * width), bf16),
                pltpu.VMEM((4 * width, width), bf16),
                pltpu.VMEM((SLOTS - 1, width, 3 * width), bf16),
                pltpu.VMEM((SLOTS - 1, width, width), bf16),
                pltpu.VMEM((SLOTS - 1, width, 4 * width), bf16),
                pltpu.VMEM((SLOTS - 1, 4 * width, width), bf16),
                pltpu.VMEM((SLOTS, 1, 128), f32),
                pltpu.VMEM((SLOTS, 2, width), f32),
                pltpu.VMEM((SLOTS, CELLS, WIDE), bf16),
                pltpu.VMEM((SLOTS, CELLS, WIDE), bf16),
                pltpu.VMEM((2, CELLS, width), f32),
                pltpu.VMEM((2, WIDE, width), bf16),
                pltpu.VMEM((2, 2 * EDGE, width), bf16),
                pltpu.VMEM((2, WIDE, width), bf16),
                pltpu.VMEM((2, 2, CELLS, width), f32),
                pltpu.VMEM((2, CELLS, width), bf16),
                pltpu.VMEM((2, CELLS, width), bf16),
                pltpu.VMEM((HALF, HALF), f32),
                pltpu.VMEM((256, 256), bf16),
                dma((SLOTS, 4)), dma((2, 4)), dma((2, 2)), dma((2,)),
                dma((2, 4)), dma((2, 4)), dma((2, 5)), dma((2, 5)),
                dma((2,)), dma((2,)), dma((2,)), dma((2, 2)), dma((2,)),
            ],
            compiler_params=pltpu.CompilerParams(
                collective_id=which, has_side_effects=True, vmem_limit_bytes=60 * 1024 * 1024
            ),
            cost_estimate=pl.CostEstimate(
                flops=16 * 2 * 10**9, bytes_accessed=20 * 10**6, transcendentals=10**7
            ),
        )

    operands = (segment_depth, cells, small, gains, table, w_qkv, w_out, w_up, w_down)
    lengths = segment_depth[0:2].sum(), segment_depth[2:4].sum()
    out = lax.switch(
        lengths[0] // 4 + 2 * (lengths[1] // 4),
        [run(which) for which in range(len(LENGTHS))],
        *operands,
    )
    return out.reshape(1, micro, levels, clat, clon, width)


def solution(mesh):
    placed = (
        P(None, None, "lat", "lon", None),
        P(),
        P("segment", None),
        P("segment", None, None),
        P("segment", None, None),
        P("segment", None, None),
        P("segment", None, None),
        P("segment", None, None),
        P("segment", None),
    )
    return jax.shard_map(
        functools.partial(shards, lon_n=mesh.shape["lon"], lat_n=mesh.shape["lat"]),
        mesh=mesh,
        in_specs=placed,
        out_specs=P("segment", None, None, "lat", "lon", None),
        check_vma=False,
    )
```

```python
import functools

import jax
import jax.numpy as jnp
import numpy as np
from jax import lax
from jax.experimental import pallas as pl
from jax.experimental.pallas import tpu as pltpu
from jax.sharding import PartitionSpec as P

MESH = pl.DeviceIdType.MESH
HALF = 144
CELLS = 2 * HALF
PART = HALF // 2
REACH = 80
EDGE = 48
AT_LON = CELLS
AT_BOTH = AT_LON + 2 * EDGE
TAKEN = AT_BOTH + EDGE
AT_LAT = TAKEN
WIDE = AT_LAT + 2 * REACH
SLOTS = 4
LENGTHS = ((3, 3), (4, 3), (3, 4))
LOG2E = 1.4426950408889634
BIG = 1e30


def moves():
    table = np.zeros((CELLS, 128), np.float32)
    for core in range(2):
        far_half = 1 - core
        for lat in range(2):
            for lon in range(2):
                which = core * 8 + lat * 2 + lon
                for at in range(CELLS):
                    window, half, pair, cell = at // 144, at % 144 // 72, at % 72 // 36, at % 36
                    level, row, column = cell // 18, cell % 18 // 6, cell % 6
                    column += (2 * window + pair) * 6 + lon * (6 - 12 * core)
                    across = column >= 24 or column < 0
                    edge_column = column - 24 if core == 0 else column + 24 - 16
                    along = lat == 1 and half == far_half
                    source = 1 - half if lat else half
                    edge = (level * 3 + row) * 8 + edge_column
                    if along and across:
                        take = AT_BOTH + edge
                    elif across:
                        take = AT_LON + source * EDGE + edge
                    else:
                        take = level * 144 + (source * 3 + row) * 24 + column
                    table[at, which] = take

                    level, row, column = at // 144, at % 144 // 24, at % 24
                    half, row = row // 3, row % 3
                    along = lat == 1 and half == core
                    source = 1 - half if lat else half
                    column -= lon * (6 - 12 * core)
                    across = column >= 24 or column < 0
                    column %= 24
                    window, pair = column // 12, column % 12 // 6
                    inside = source * 72 + pair * 36 + level * 18 + row * 6 + column % 6
                    if along and across:
                        take = AT_BOTH + inside - (0 if core else 96)
                    elif across:
                        take = AT_LON + source * EDGE + inside - source * 64 - (0 if core else 32)
                    else:
                        take = window * 144 + inside
                    table[at, which + 4] = take
    return table


def normed(values, gain, eps):
    mean = jnp.mean(values, axis=-1, keepdims=True)
    centred = values - mean
    var = jnp.mean(centred * centred, axis=-1, keepdims=True)
    return centred * lax.rsqrt(var + eps) * gain


def twice_gelu(u):
    inner = u * (0.7978845608028654 + 0.035677408136300125 * (u * u))
    return u + u * jnp.tanh(inner)


def dot(a, b):
    return jnp.dot(a, b, preferred_element_type=jnp.float32)


def kernel(
    lon_n, lat_n, lengths, depth_ref, latents, small_in, gains_in, table, w_qkv, w_out, w_up, w_down, sections,
    wq_a, wo_a, wu_a, wd_a, wq_b, wo_b, wu_b, wd_b, small, gains, fwd, bwd, x, src, packed, ret, stage, hand_out, hand_in, cross, ones,
    w_recv, w_send, p_recv, p_send, f_recv, f_send, b_recv, b_send, in_sem, h_recv, h_send,
    o_recv, o_send,
):
    seg = lax.axis_index("segment")
    lon = lax.axis_index("lon")
    lat = lax.axis_index("lat")
    chip = seg // 2
    core = lax.rem(seg, 2)
    mate_core = 1 - core
    north, south = lax.rem(lat + lat_n - 1, lat_n), lax.rem(lat + 1, lat_n)
    west, east = lax.rem(lon + lon_n - 1, lon_n), lax.rem(lon + 1, lon_n)

    def device(s, o, a):
        return {"segment": s, "lon": o, "lat": a}

    out_lat, home_lat = north + core * (south - north), south + core * (north - south)
    out_lon, home_lon = west + core * (east - west), east + core * (west - east)
    to_n, to_s = device(seg, lon, out_lat), device(seg, lon, home_lat)
    to_w, to_e = device(seg, out_lon, lat), device(seg, home_lon, lat)
    to_nw, to_se = device(seg, out_lon, out_lat), device(seg, home_lon, home_lat)
    mate = device(chip * 2 + mate_core, lon, lat)
    other = device(lax.rem(seg + 2, 4), lon, lat)

    steps = lengths[0] + chip * (lengths[1] - lengths[0])
    depth = depth_ref[2 * chip]
    layers = depth + depth_ref[2 * chip + 1]

    first_weights = (wq_a, wo_a, wu_a, wd_a)
    later_weights = (wq_b, wo_b, wu_b, wd_b)
    held_weights = (w_qkv, w_out, w_up, w_down)

    def each_weight(i, k, act):
        if i == 1:
            act(held_weights[k].at[1], later_weights[k].at[2 * core])
            return

        @pl.when(core == 0)
        def _():
            act(held_weights[k].at[0], first_weights[k])

        @pl.when(core == 1)
        def _():
            act(held_weights[k].at[0], later_weights[k].at[1])

    def own_weights(i, k):
        slot = core * 2 + i
        each_weight(
            i, k,
            lambda held, kept: pltpu.make_async_copy(held, kept, w_recv.at[slot, k]).start(),
        )

    def lent_weights(i, k, act):
        slot = core * 2 + i
        each_weight(
            i, k,
            lambda held, kept: act(
                pltpu.make_async_remote_copy(
                    src_ref=held, dst_ref=kept, send_sem=w_send.at[i, k],
                    recv_sem=w_recv.at[slot, k], device_id=mate, device_id_type=MESH,
                )
            ),
        )

    def weights_here(slot, k):
        kept = first_weights[k] if slot == 0 else later_weights[k].at[slot - 1]
        pltpu.make_async_copy(held_weights[k].at[0], kept, w_recv.at[slot, k]).wait()

    tiny = ((small_in, small), (gains_in, gains))

    def own_params(k):
        held, kept = tiny[k]
        return pltpu.make_async_copy(held, kept.at[pl.ds(core * 2, 2)], p_recv.at[core, k])

    def lent_params(k):
        held, kept = tiny[k]
        return pltpu.make_async_remote_copy(
            src_ref=held, dst_ref=kept.at[pl.ds(core * 2, 2)], send_sem=p_send.at[k],
            recv_sem=p_recv.at[core, k], device_id=mate, device_id_type=MESH,
        )

    def edges(pieces, send, recv):
        return [
            pltpu.make_async_remote_copy(
                src_ref=source, dst_ref=target, send_sem=send.at[i], recv_sem=recv.at[i],
                device_id=to, device_id_type=MESH,
            )
            for i, (source, target, to) in enumerate(pieces)
        ]

    def rows_from(start, size):
        return pl.ds(pl.multiple_of(start, 16), size)

    def forth(b):
        return edges(
            (
                (src.at[b, rows_from(64 * core, REACH)], src.at[b, pl.ds(AT_LAT, REACH)], to_n),
                (
                    src.at[b, rows_from(HALF + 64 * core, REACH)],
                    src.at[b, pl.ds(AT_LAT + REACH, REACH)], to_n,
                ),
                (packed.at[b], src.at[b, pl.ds(AT_LON, 2 * EDGE)], to_w),
                (packed.at[b, rows_from(EDGE * core, EDGE)], src.at[b, pl.ds(AT_BOTH, EDGE)], to_nw),
            ),
            f_send.at[b], f_recv.at[b],
        )

    def back(b):
        return edges(
            (
                (ret.at[b, rows_from(64 - 64 * core, REACH)], ret.at[b, pl.ds(AT_LAT, REACH)], to_s),
                (
                    ret.at[b, rows_from(208 - 64 * core, REACH)],
                    ret.at[b, pl.ds(AT_LAT + REACH, REACH)], to_s,
                ),
                (ret.at[b, rows_from(176 - 176 * core, EDGE)], ret.at[b, pl.ds(AT_LON, EDGE)], to_e),
                (
                    ret.at[b, rows_from(240 - 176 * core, EDGE)],
                    ret.at[b, pl.ds(AT_LON + EDGE, EDGE)], to_e,
                ),
                (ret.at[b, rows_from(240 - 240 * core, EDGE)], ret.at[b, pl.ds(AT_BOTH, EDGE)], to_se),
            ),
            b_send.at[b], b_recv.at[b],
        )

    def edge_of(values, column):
        rows = [
            level * 144 + row * 24 + column
            for half in ((0, 1, 2), (3, 4, 5)) for level in (0, 1) for row in half
        ]
        return jnp.concatenate([values[r : r + 8] for r in rows], axis=0)

    def far_edge(values):
        return jnp.where(core == 0, edge_of(values, 0), edge_of(values, 16)).astype(jnp.bfloat16)

    def load_input(b):
        return pltpu.make_async_copy(
            latents.at[core + 2 * b], src.at[b, pl.ds(0, CELLS)], in_sem.at[b]
        )

    def hand_on(b):
        return pltpu.make_async_remote_copy(
            src_ref=hand_out.at[b], dst_ref=hand_in.at[b], send_sem=h_send.at[b],
            recv_sem=h_recv.at[b], device_id=other, device_id_type=MESH,
        )

    def keep_output(b, s):
        return pltpu.make_async_copy(
            stage.at[b, s], sections.at[core + 2 * b], o_recv.at[b, 0]
        )

    def give_output(b, s):
        return pltpu.make_async_remote_copy(
            src_ref=stage.at[b, s], dst_ref=sections.at[core + 2 * b], send_sem=o_send.at[b],
            recv_sem=o_recv.at[b, 1], device_id=mate, device_id_type=MESH,
        )

    barrier = pltpu.get_barrier_semaphore()
    for k in range(4):
        own_weights(0, k)
    for k in range(2):
        own_params(k).start()

    @pl.when(chip == 0)
    def _():
        for b in range(2):
            load_input(b).start()

    for to in (to_n, to_s, to_w, to_e, to_nw, to_se, mate, other):
        pl.semaphore_signal(barrier, inc=1, device_id=to, device_id_type=MESH)
    pl.semaphore_wait(barrier, 8)

    for k in range(2):
        lent_params(k).start()
    for k in range(4):
        lent_weights(0, k, lambda copy: copy.start())

    @pl.when(chip == 0)
    def _():
        for b in range(2):
            load_input(b).wait()
            entry = src[b, 0:CELLS].astype(jnp.float32)
            x[b] = entry
            packed[b] = far_edge(entry)
            for copy in forth(b):
                copy.start()

    @pl.when(chip == 1)
    def _():
        for b in range(2):
            hand_on(b).wait_recv()
            src[b, 0:CELLS] = hand_in[b]
            entry = hand_in[b].astype(jnp.float32)
            x[b] = entry
            packed[b] = far_edge(entry)
            for copy in forth(b):
                copy.start()

    for k, (held, kept) in enumerate(tiny):
        own_params(k).wait()
        pltpu.make_async_copy(
            held, kept.at[pl.ds(mate_core * 2, 2)], p_recv.at[mate_core, k]
        ).wait()

    rows = lax.broadcasted_iota(jnp.int32, (HALF, HALF), 0)
    cols = lax.broadcasted_iota(jnp.int32, (HALF, HALF), 1)
    split = (rows < PART) != (cols < PART)
    is_last = jnp.where(lat == (lat_n - 1) * (1 - core), 1.0, 0.0)
    cross[...] = jnp.where(split, -BIG, 0.0) * is_last
    r256 = lax.broadcasted_iota(jnp.int32, (256, 256), 0)
    c256 = lax.broadcasted_iota(jnp.int32, (256, 256), 1)
    ones[...] = jnp.where(r256 // 64 == c256 // 64, 1.0, 0.0).astype(jnp.bfloat16)

    place = lax.broadcasted_iota(jnp.int32, (CELLS, TAKEN), 1).astype(jnp.float32)

    def slot_of(step):
        return jnp.clip(step + jnp.where(step == 0, 0, 2 - depth), 0, SLOTS - 1)

    def choose(step, carry):
        f_lat = small[slot_of(step), 0:1, 0:1]
        f_lon = small[slot_of(step), 0:1, 1:2]
        picks = (
            (1.0 - f_lat) * (1.0 - f_lon), (1.0 - f_lat) * f_lon,
            f_lat * (1.0 - f_lon), f_lat * f_lon,
        )
        for first, kept in ((0, fwd), (4, bwd)):
            at = sum(
                jnp.where(
                    core == 0, table[:, first + i : first + i + 1],
                    table[:, first + i + 8 : first + i + 9],
                ) * picks[i]
                for i in range(4)
            )
            kept[step] = jnp.where(place == at, 1.0, 0.0).astype(jnp.bfloat16)
        return carry

    lax.fori_loop(0, steps, choose, 0)

    lane = lax.broadcasted_iota(jnp.int32, (1, 256), 1)
    masks = [jnp.where(lane // 64 == h, 1.0, 0.0).astype(jnp.bfloat16) for h in range(4)]
    first_of_pair = lax.broadcasted_iota(jnp.int32, (HALF, 128), 1) < 64

    def unit(block):
        total = dot((block * block).astype(jnp.bfloat16), ones[...])
        return (block * lax.rsqrt(total + 1e-06)).astype(jnp.bfloat16)

    reach_row = lax.broadcasted_iota(jnp.int32, (REACH, 1), 0)

    def replace_rows(buf, b, l, far):
        kept = (reach_row >= 8 * far) & (reach_row < PART + 8 * far)
        theirs = jnp.where(kept, small[l, 0:1, 0:1], 0.0)
        ours = (1.0 - theirs).astype(jnp.bfloat16)
        theirs = theirs.astype(jnp.bfloat16)
        for i in range(2):
            at = rows_from(i * HALF + 64 * far, REACH)
            came = buf[b, AT_LAT + i * REACH : AT_LAT + (i + 1) * REACH]
            buf[b, at] = buf[b, at] * ours + came * theirs

    def attend(b, step, l, weight):
        for copy in forth(b):
            copy.wait()
        replace_rows(src, b, l, core)
        cells = dot(fwd[step], src[b, 0:TAKEN]).astype(jnp.bfloat16)
        bias = small[l, 0:1, 0:1] * cross[...]
        done = [[], []]
        for g in range(2):
            lanes = [slice(p * 512 + g * 256, p * 512 + g * 256 + 256) for p in range(3)]
            q = unit(dot(cells, weight(0, lanes[0])))
            k = unit(dot(cells, weight(0, lanes[1])))
            v = dot(cells, weight(0, lanes[2])).astype(jnp.bfloat16)
            for w in range(2):
                part = slice(w * HALF, w * HALF + HALF)
                heads = jnp.concatenate([q[part] * masks[h] for h in range(4)], axis=0)
                scores = lax.dot_general(
                    heads, k[part], (((1,), (1,)), ((), ())), preferred_element_type=jnp.float32
                )
                expos, shares = [], []
                for h in range(4):
                    scale = small[l, 0:1, 2 + g * 4 + h : 3 + g * 4 + h]
                    score = scores[h * HALF : h * HALF + HALF] * scale + bias
                    expo = jnp.exp2(score - jnp.max(score, axis=-1, keepdims=True))
                    total = jnp.sum(expo, axis=-1, keepdims=True)
                    share = pl.reciprocal(total, approx=True)
                    shares.append(share * (2.0 - total * share))
                    expos.append(expo.astype(jnp.bfloat16))
                mixed = dot(jnp.concatenate(expos, axis=0), v[part])
                for p in range(2):
                    at = slice(p * 128, p * 128 + 128)
                    one = mixed[2 * p * HALF : (2 * p + 1) * HALF, at] * shares[2 * p]
                    two = mixed[(2 * p + 1) * HALF : (2 * p + 2) * HALF, at] * shares[2 * p + 1]
                    done[w].append(jnp.where(first_of_pair, one, two).astype(jnp.bfloat16))
        for w in range(2):
            ret[b, w * HALF : w * HALF + HALF] = jnp.concatenate(done[w], axis=1)
        for copy in back(b):
            copy.start()

    def feed(b, step, l, weight):
        for copy in back(b):
            copy.wait()
        replace_rows(ret, b, l, 1 - core)
        mixed = dot(bwd[step], ret[b, 0:TAKEN]).astype(jnp.bfloat16)
        state = x[b]
        first = state + normed(dot(mixed, weight(1)), gains[l, 0:1], 1e-05)
        firstb = first.astype(jnp.bfloat16)
        hidden = jnp.concatenate(
            [
                twice_gelu(dot(firstb, weight(2, slice(c, c + 256)))).astype(jnp.bfloat16)
                for c in range(0, 2048, 256)
            ],
            axis=1,
        )
        fresh = first + normed(dot(hidden, weight(3)), gains[l, 1:2], 4e-05)
        fresh = jnp.where(step < layers, fresh, state)
        x[b] = fresh

        @pl.when(step < steps - 1)
        def _():
            src[b, 0:CELLS] = fresh.astype(jnp.bfloat16)
            packed[b] = far_edge(fresh)
            for copy in forth(b):
                copy.start()

        def emit(s, value):
            stage[b, s] = value

            @pl.when(s == core)
            def _():
                keep_output(b, s).start()

            @pl.when(s != core)
            def _():
                give_output(b, s).start()

        @pl.when(step == 1)
        def _():
            emit(0, jnp.where(depth == 1, state, fresh))

        @pl.when(step == steps - 1)
        def _():
            emit(1, fresh)

            @pl.when(chip == 0)
            def _():
                hand_out[b] = fresh.astype(jnp.bfloat16)
                hand_on(b).start()

    def layer(step, l, weight):
        def one(b, c):
            attend(b, step, l, weight)
            return c

        def two(b, c):
            feed(b, step, l, weight)
            return c

        return one, two

    def weight_a(k, lanes=slice(None)):
        return first_weights[k][:, lanes]

    weights_here(0, 0)
    one, two = layer(0, 0, weight_a)
    lax.fori_loop(0, 2, one, 0)
    for k in range(1, 4):
        weights_here(0, k)
    for k in range(4):
        lent_weights(1, k, lambda copy: copy.start())
        own_weights(1, k)
    lax.fori_loop(0, 2, two, 0)

    for slot in range(1, SLOTS):
        for k in range(4):
            weights_here(slot, k)

    def later(step, carry):
        l = slot_of(step)

        def weight_b(k, lanes=slice(None)):
            return later_weights[k][jnp.maximum(l, 1) - 1, :, lanes]

        one, two = layer(step, l, weight_b)
        lax.fori_loop(0, 2, one, 0)
        lax.fori_loop(0, 2, two, 0)
        return carry

    lax.fori_loop(1, steps, later, 0)

    for i in range(2):
        for k in range(4):
            lent_weights(i, k, lambda copy: copy.wait_send())
    for k in range(2):
        lent_params(k).wait_send()

    @pl.when(chip == 0)
    def _():
        for b in range(2):
            hand_on(b).wait_send()

    for b in range(2):
        keep_output(b, core).wait()
        give_output(b, mate_core).wait()


def shards(latents, segment_depth, shift_flags, w_qkv, w_out, w_up, w_down, gains, logit_scale,
           lon_n, lat_n):
    micro, levels, clat, clon, width = latents.shape
    cells = latents.reshape(micro, CELLS, width)
    small = jnp.concatenate(
        [shift_flags.astype(jnp.float32), logit_scale * LOG2E, jnp.zeros((2, 118), jnp.float32)],
        axis=1,
    ).reshape(2, 1, 128)
    table = jnp.asarray(moves())
    hbm = pl.BlockSpec(memory_space=pl.ANY)
    bf16, f32 = jnp.bfloat16, jnp.float32
    dma = pltpu.SemaphoreType.DMA
    def run(which):
        lengths = LENGTHS[which]
        return pl.pallas_call(
            functools.partial(kernel, lon_n, lat_n, lengths),
            out_shape=jax.ShapeDtypeStruct((micro, CELLS, width), f32),
            in_specs=[
                pl.BlockSpec(memory_space=pltpu.SMEM), hbm, hbm, hbm,
                pl.BlockSpec(memory_space=pltpu.VMEM), hbm, hbm, hbm, hbm,
            ],
            out_specs=hbm,
            scratch_shapes=[
                pltpu.VMEM((width, 3 * width), bf16),
                pltpu.VMEM((width, width), bf16),
                pltpu.VMEM((width, 4 * width), bf16),
                pltpu.VMEM((4 * width, width), bf16),
                pltpu.VMEM((SLOTS - 1, width, 3 * width), bf16),
                pltpu.VMEM((SLOTS - 1, width, width), bf16),
                pltpu.VMEM((SLOTS - 1, width, 4 * width), bf16),
                pltpu.VMEM((SLOTS - 1, 4 * width, width), bf16),
                pltpu.VMEM((SLOTS, 1, 128), f32),
                pltpu.VMEM((SLOTS, 2, width), f32),
                pltpu.VMEM((SLOTS, CELLS, TAKEN), bf16),
                pltpu.VMEM((SLOTS, CELLS, TAKEN), bf16),
                pltpu.VMEM((2, CELLS, width), f32),
                pltpu.VMEM((2, WIDE, width), bf16),
                pltpu.VMEM((2, 2 * EDGE, width), bf16),
                pltpu.VMEM((2, WIDE, width), bf16),
                pltpu.VMEM((2, 2, CELLS, width), f32),
                pltpu.VMEM((2, CELLS, width), bf16),
                pltpu.VMEM((2, CELLS, width), bf16),
                pltpu.VMEM((HALF, HALF), f32),
                pltpu.VMEM((256, 256), bf16),
                dma((SLOTS, 4)), dma((2, 4)), dma((2, 2)), dma((2,)),
                dma((2, 4)), dma((2, 4)), dma((2, 5)), dma((2, 5)),
                dma((2,)), dma((2,)), dma((2,)), dma((2, 2)), dma((2,)),
            ],
            compiler_params=pltpu.CompilerParams(
                collective_id=which, has_side_effects=True, vmem_limit_bytes=60 * 1024 * 1024
            ),
            cost_estimate=pl.CostEstimate(
                flops=16 * 2 * 10**9, bytes_accessed=20 * 10**6, transcendentals=10**7
            ),
        )

    operands = (segment_depth, cells, small, gains, table, w_qkv, w_out, w_up, w_down)
    lengths = segment_depth[0:2].sum(), segment_depth[2:4].sum()
    out = lax.switch(
        lengths[0] // 4 + 2 * (lengths[1] // 4),
        [run(which) for which in range(len(LENGTHS))],
        *operands,
    )
    return out.reshape(1, micro, levels, clat, clon, width)


def solution(mesh):
    placed = (
        P(None, None, "lat", "lon", None),
        P(),
        P("segment", None),
        P("segment", None, None),
        P("segment", None, None),
        P("segment", None, None),
        P("segment", None, None),
        P("segment", None, None),
        P("segment", None),
    )
    return jax.shard_map(
        functools.partial(shards, lon_n=mesh.shape["lon"], lat_n=mesh.shape["lat"]),
        mesh=mesh,
        in_specs=placed,
        out_specs=P("segment", None, None, "lat", "lon", None),
        check_vma=False,
    )
```

```python
import functools

import jax
import jax.numpy as jnp
import numpy as np
from jax import lax
from jax.experimental import pallas as pl
from jax.experimental.pallas import tpu as pltpu
from jax.sharding import PartitionSpec as P

MESH = pl.DeviceIdType.MESH
HALF = 144
CELLS = 2 * HALF
PART = HALF // 2
REACH = 80
EDGE = 48
AT_LON = CELLS
AT_BOTH = AT_LON + 2 * EDGE
TAKEN = AT_BOTH + EDGE
AT_LAT = TAKEN
WIDE = AT_LAT + 2 * REACH
SLOTS = 4
LENGTHS = ((3, 3), (4, 3), (3, 4))
LOG2E = 1.4426950408889634
BIG = 1e30


def moves():
    table = np.zeros((CELLS, 128), np.float32)
    for core in range(2):
        far_half = 1 - core
        for lat in range(2):
            for lon in range(2):
                which = core * 8 + lat * 2 + lon
                for at in range(CELLS):
                    window = at // 144 if core else 1 - at // 144
                    half, pair, cell = at % 144 // 72, at % 72 // 36, at % 36
                    level, row, column = cell // 18, cell % 18 // 6, cell % 6
                    column += (2 * window + pair) * 6 + lon * (6 - 12 * core)
                    across = column >= 24 or column < 0
                    edge_column = column - 24 if core == 0 else column + 24 - 16
                    along = lat == 1 and half == far_half
                    source = 1 - half if lat else half
                    edge = (level * 3 + row) * 8 + edge_column
                    if along and across:
                        take = AT_BOTH + edge
                    elif across:
                        take = AT_LON + source * EDGE + edge
                    else:
                        take = level * 144 + (source * 3 + row) * 24 + column
                    table[at, which] = take

                    level, row, column = at // 144, at % 144 // 24, at % 24
                    half, row = row // 3, row % 3
                    along = lat == 1 and half == core
                    source = 1 - half if lat else half
                    column -= lon * (6 - 12 * core)
                    across = column >= 24 or column < 0
                    column %= 24
                    window, pair = column // 12, column % 12 // 6
                    inside = source * 72 + pair * 36 + level * 18 + row * 6 + column % 6
                    if along and across:
                        take = AT_BOTH + inside - (0 if core else 96)
                    elif across:
                        take = AT_LON + source * EDGE + inside - source * 64 - (0 if core else 32)
                    else:
                        take = (window if core else 1 - window) * 144 + inside
                    table[at, which + 4] = take
    return table


def normed(values, gain, eps):
    mean = jnp.mean(values, axis=-1, keepdims=True)
    centred = values - mean
    var = jnp.mean(centred * centred, axis=-1, keepdims=True)
    return centred * lax.rsqrt(var + eps) * gain


def twice_gelu(u):
    inner = u * (0.7978845608028654 + 0.035677408136300125 * (u * u))
    return u + u * jnp.tanh(inner)


def dot(a, b):
    return jnp.dot(a, b, preferred_element_type=jnp.float32)


def kernel(
    lon_n, lat_n, lengths, depth_ref, latents, small_in, gains_in, table, w_qkv, w_out, w_up, w_down, sections,
    wq_a, wo_a, wu_a, wd_a, wq_b, wo_b, wu_b, wd_b, small, gains, fwd, bwd, x, src, packed, ret, stage, hand_out, hand_in, cross, ones,
    w_recv, w_send, p_recv, p_send, f_recv, f_send, b_recv, b_send, in_sem, h_recv, h_send,
    o_recv, o_send,
):
    seg = lax.axis_index("segment")
    lon = lax.axis_index("lon")
    lat = lax.axis_index("lat")
    chip = seg // 2
    core = lax.rem(seg, 2)
    mate_core = 1 - core
    north, south = lax.rem(lat + lat_n - 1, lat_n), lax.rem(lat + 1, lat_n)
    west, east = lax.rem(lon + lon_n - 1, lon_n), lax.rem(lon + 1, lon_n)

    def device(s, o, a):
        return {"segment": s, "lon": o, "lat": a}

    out_lat, home_lat = north + core * (south - north), south + core * (north - south)
    out_lon, home_lon = west + core * (east - west), east + core * (west - east)
    to_n, to_s = device(seg, lon, out_lat), device(seg, lon, home_lat)
    to_w, to_e = device(seg, out_lon, lat), device(seg, home_lon, lat)
    to_nw, to_se = device(seg, out_lon, out_lat), device(seg, home_lon, home_lat)
    mate = device(chip * 2 + mate_core, lon, lat)
    other = device(lax.rem(seg + 2, 4), lon, lat)

    steps = lengths[0] + chip * (lengths[1] - lengths[0])
    depth = depth_ref[2 * chip]
    layers = depth + depth_ref[2 * chip + 1]

    first_weights = (wq_a, wo_a, wu_a, wd_a)
    later_weights = (wq_b, wo_b, wu_b, wd_b)
    held_weights = (w_qkv, w_out, w_up, w_down)

    def each_weight(i, k, act):
        if i == 1:
            act(held_weights[k].at[1], later_weights[k].at[2 * core])
            return

        @pl.when(core == 0)
        def _():
            act(held_weights[k].at[0], first_weights[k])

        @pl.when(core == 1)
        def _():
            act(held_weights[k].at[0], later_weights[k].at[1])

    def own_weights(i, k):
        slot = core * 2 + i
        each_weight(
            i, k,
            lambda held, kept: pltpu.make_async_copy(held, kept, w_recv.at[slot, k]).start(),
        )

    def lent_weights(i, k, act):
        slot = core * 2 + i
        each_weight(
            i, k,
            lambda held, kept: act(
                pltpu.make_async_remote_copy(
                    src_ref=held, dst_ref=kept, send_sem=w_send.at[i, k],
                    recv_sem=w_recv.at[slot, k], device_id=mate, device_id_type=MESH,
                )
            ),
        )

    def weights_here(slot, k):
        kept = first_weights[k] if slot == 0 else later_weights[k].at[slot - 1]
        pltpu.make_async_copy(held_weights[k].at[0], kept, w_recv.at[slot, k]).wait()

    tiny = ((small_in, small), (gains_in, gains))

    def own_params(k):
        held, kept = tiny[k]
        return pltpu.make_async_copy(held, kept.at[pl.ds(core * 2, 2)], p_recv.at[core, k])

    def lent_params(k):
        held, kept = tiny[k]
        return pltpu.make_async_remote_copy(
            src_ref=held, dst_ref=kept.at[pl.ds(core * 2, 2)], send_sem=p_send.at[k],
            recv_sem=p_recv.at[core, k], device_id=mate, device_id_type=MESH,
        )

    def edges(pieces, send, recv):
        return [
            pltpu.make_async_remote_copy(
                src_ref=source, dst_ref=target, send_sem=send.at[i], recv_sem=recv.at[i],
                device_id=to, device_id_type=MESH,
            )
            for i, (source, target, to) in enumerate(pieces)
        ]

    def rows_from(start, size):
        return pl.ds(pl.multiple_of(start, 16), size)

    def forth(b):
        return edges(
            (
                (packed.at[b, rows_from(EDGE * core, EDGE)], src.at[b, pl.ds(AT_BOTH, EDGE)], to_nw),
                (packed.at[b], src.at[b, pl.ds(AT_LON, 2 * EDGE)], to_w),
                (src.at[b, rows_from(64 * core, REACH)], src.at[b, pl.ds(AT_LAT, REACH)], to_n),
                (
                    src.at[b, rows_from(HALF + 64 * core, REACH)],
                    src.at[b, pl.ds(AT_LAT + REACH, REACH)], to_n,
                ),
            ),
            f_send.at[b], f_recv.at[b],
        )

    def back(b):
        return edges(
            (
                (ret.at[b, rows_from(96 - 96 * core, EDGE)], ret.at[b, pl.ds(AT_BOTH, EDGE)], to_se),
                (ret.at[b, rows_from(32 - 32 * core, EDGE)], ret.at[b, pl.ds(AT_LON, EDGE)], to_e),
                (
                    ret.at[b, rows_from(96 - 32 * core, EDGE)],
                    ret.at[b, pl.ds(AT_LON + EDGE, EDGE)], to_e,
                ),
                (ret.at[b, rows_from(64 - 64 * core, REACH)], ret.at[b, pl.ds(AT_LAT, REACH)], to_s),
                (
                    ret.at[b, rows_from(208 - 64 * core, REACH)],
                    ret.at[b, pl.ds(AT_LAT + REACH, REACH)], to_s,
                ),
            ),
            b_send.at[b], b_recv.at[b],
        )

    def edge_of(values, column):
        rows = [
            level * 144 + row * 24 + column
            for half in ((0, 1, 2), (3, 4, 5)) for level in (0, 1) for row in half
        ]
        return jnp.concatenate([values[r : r + 8] for r in rows], axis=0)

    def far_edge(values):
        return jnp.where(core == 0, edge_of(values, 0), edge_of(values, 16)).astype(jnp.bfloat16)

    def load_input(b):
        return pltpu.make_async_copy(
            latents.at[core + 2 * b], src.at[b, pl.ds(0, CELLS)], in_sem.at[b]
        )

    def hand_on(b):
        return pltpu.make_async_remote_copy(
            src_ref=hand_out.at[b], dst_ref=hand_in.at[b], send_sem=h_send.at[b],
            recv_sem=h_recv.at[b], device_id=other, device_id_type=MESH,
        )

    def keep_output(b, s):
        return pltpu.make_async_copy(
            stage.at[b, s], sections.at[core + 2 * b], o_recv.at[b, 0]
        )

    def give_output(b, s):
        return pltpu.make_async_remote_copy(
            src_ref=stage.at[b, s], dst_ref=sections.at[core + 2 * b], send_sem=o_send.at[b],
            recv_sem=o_recv.at[b, 1], device_id=mate, device_id_type=MESH,
        )

    barrier = pltpu.get_barrier_semaphore()
    for k in range(4):
        own_weights(0, k)
    for k in range(2):
        own_params(k).start()

    @pl.when(chip == 0)
    def _():
        for b in range(2):
            load_input(b).start()

    for to in (to_n, to_s, to_w, to_e, to_nw, to_se, mate, other):
        pl.semaphore_signal(barrier, inc=1, device_id=to, device_id_type=MESH)
    pl.semaphore_wait(barrier, 8)

    for k in range(2):
        lent_params(k).start()
    for k in range(4):
        lent_weights(0, k, lambda copy: copy.start())

    @pl.when(chip == 0)
    def _():
        for b in range(2):
            load_input(b).wait()
            entry = src[b, 0:CELLS].astype(jnp.float32)
            x[b] = entry
            packed[b] = far_edge(entry)
            for copy in forth(b):
                copy.start()

    @pl.when(chip == 1)
    def _():
        for b in range(2):
            hand_on(b).wait_recv()
            src[b, 0:CELLS] = hand_in[b]
            entry = hand_in[b].astype(jnp.float32)
            x[b] = entry
            packed[b] = far_edge(entry)
            for copy in forth(b):
                copy.start()

    for k, (held, kept) in enumerate(tiny):
        own_params(k).wait()
        pltpu.make_async_copy(
            held, kept.at[pl.ds(mate_core * 2, 2)], p_recv.at[mate_core, k]
        ).wait()

    rows = lax.broadcasted_iota(jnp.int32, (HALF, HALF), 0)
    cols = lax.broadcasted_iota(jnp.int32, (HALF, HALF), 1)
    split = (rows < PART) != (cols < PART)
    is_last = jnp.where(lat == (lat_n - 1) * (1 - core), 1.0, 0.0)
    cross[...] = jnp.where(split, -BIG, 0.0) * is_last
    r256 = lax.broadcasted_iota(jnp.int32, (256, 256), 0)
    c256 = lax.broadcasted_iota(jnp.int32, (256, 256), 1)
    ones[...] = jnp.where(r256 // 64 == c256 // 64, 1.0, 0.0).astype(jnp.bfloat16)

    place = lax.broadcasted_iota(jnp.int32, (CELLS, TAKEN), 1).astype(jnp.float32)

    def slot_of(step):
        return jnp.clip(step + jnp.where(step == 0, 0, 2 - depth), 0, SLOTS - 1)

    def choose(step, carry):
        f_lat = small[slot_of(step), 0:1, 0:1]
        f_lon = small[slot_of(step), 0:1, 1:2]
        picks = (
            (1.0 - f_lat) * (1.0 - f_lon), (1.0 - f_lat) * f_lon,
            f_lat * (1.0 - f_lon), f_lat * f_lon,
        )
        for first, kept in ((0, fwd), (4, bwd)):
            at = sum(
                jnp.where(
                    core == 0, table[:, first + i : first + i + 1],
                    table[:, first + i + 8 : first + i + 9],
                ) * picks[i]
                for i in range(4)
            )
            kept[step] = jnp.where(place == at, 1.0, 0.0).astype(jnp.bfloat16)
        return carry

    lax.fori_loop(0, steps, choose, 0)

    lane = lax.broadcasted_iota(jnp.int32, (1, 256), 1)
    masks = [jnp.where(lane // 64 == h, 1.0, 0.0).astype(jnp.bfloat16) for h in range(4)]
    first_of_pair = lax.broadcasted_iota(jnp.int32, (HALF, 128), 1) < 64

    def unit(block):
        total = dot((block * block).astype(jnp.bfloat16), ones[...])
        return (block * lax.rsqrt(total + 1e-06)).astype(jnp.bfloat16)

    reach_row = lax.broadcasted_iota(jnp.int32, (REACH, 1), 0)

    def replace_rows(buf, b, l, far):
        kept = (reach_row >= 8 * far) & (reach_row < PART + 8 * far)
        theirs = jnp.where(kept, small[l, 0:1, 0:1], 0.0)
        ours = (1.0 - theirs).astype(jnp.bfloat16)
        theirs = theirs.astype(jnp.bfloat16)
        for i in range(2):
            at = rows_from(i * HALF + 64 * far, REACH)
            came = buf[b, AT_LAT + i * REACH : AT_LAT + (i + 1) * REACH]
            buf[b, at] = buf[b, at] * ours + came * theirs

    def attend(b, step, l, weight):
        for copy in forth(b):
            copy.wait()
        replace_rows(src, b, l, core)
        cells = dot(fwd[step], src[b, 0:TAKEN]).astype(jnp.bfloat16)
        bias = small[l, 0:1, 0:1] * cross[...]
        quads = []
        for g in range(2):
            lanes = [slice(p * 512 + g * 256, p * 512 + g * 256 + 256) for p in range(3)]
            q = unit(dot(cells, weight(0, lanes[0])))
            k = unit(dot(cells, weight(0, lanes[1])))
            quads.append((q, k, dot(cells, weight(0, lanes[2])).astype(jnp.bfloat16)))
        copies = back(b)
        for w in range(2):
            part = slice(w * HALF, w * HALF + HALF)
            done = []
            for g, (q, k, v) in enumerate(quads):
                heads = jnp.concatenate([q[part] * masks[h] for h in range(4)], axis=0)
                scores = lax.dot_general(
                    heads, k[part], (((1,), (1,)), ((), ())), preferred_element_type=jnp.float32
                )
                expos, shares = [], []
                for h in range(4):
                    scale = small[l, 0:1, 2 + g * 4 + h : 3 + g * 4 + h]
                    score = scores[h * HALF : h * HALF + HALF] * scale + bias
                    expo = jnp.exp2(score - jnp.max(score, axis=-1, keepdims=True))
                    total = jnp.sum(expo, axis=-1, keepdims=True)
                    share = pl.reciprocal(total, approx=True)
                    shares.append(share * (2.0 - total * share))
                    expos.append(expo.astype(jnp.bfloat16))
                mixed = dot(jnp.concatenate(expos, axis=0), v[part])
                for p in range(2):
                    at = slice(p * 128, p * 128 + 128)
                    one = mixed[2 * p * HALF : (2 * p + 1) * HALF, at] * shares[2 * p]
                    two = mixed[(2 * p + 1) * HALF : (2 * p + 2) * HALF, at] * shares[2 * p + 1]
                    done.append(jnp.where(first_of_pair, one, two).astype(jnp.bfloat16))
            ret[b, part] = jnp.concatenate(done, axis=1)
            for copy in copies[:3] if w == 0 else copies[3:]:
                copy.start()

    def feed(b, step, l, weight):
        for copy in back(b):
            copy.wait()
        replace_rows(ret, b, l, 1 - core)
        mixed = dot(bwd[step], ret[b, 0:TAKEN]).astype(jnp.bfloat16)
        state = x[b]
        first = state + normed(dot(mixed, weight(1)), gains[l, 0:1], 1e-05)
        firstb = first.astype(jnp.bfloat16)
        hidden = jnp.concatenate(
            [
                twice_gelu(dot(firstb, weight(2, slice(c, c + 256)))).astype(jnp.bfloat16)
                for c in range(0, 2048, 256)
            ],
            axis=1,
        )
        fresh = first + normed(dot(hidden, weight(3)), gains[l, 1:2], 4e-05)
        fresh = jnp.where(step < layers, fresh, state)
        x[b] = fresh

        @pl.when(step < steps - 1)
        def _():
            src[b, 0:CELLS] = fresh.astype(jnp.bfloat16)
            packed[b] = far_edge(fresh)
            for copy in forth(b):
                copy.start()

        def emit(s, value):
            stage[b, s] = value

            @pl.when(s == core)
            def _():
                keep_output(b, s).start()

            @pl.when(s != core)
            def _():
                give_output(b, s).start()

        @pl.when(step == 1)
        def _():
            emit(0, jnp.where(depth == 1, state, fresh))

        @pl.when(step == steps - 1)
        def _():
            emit(1, fresh)

            @pl.when(chip == 0)
            def _():
                hand_out[b] = fresh.astype(jnp.bfloat16)
                hand_on(b).start()

    def layer(step, l, weight):
        def one(b, c):
            attend(b, step, l, weight)
            return c

        def two(b, c):
            feed(b, step, l, weight)
            return c

        return one, two

    def weight_a(k, lanes=slice(None)):
        return first_weights[k][:, lanes]

    weights_here(0, 0)
    one, two = layer(0, 0, weight_a)
    lax.fori_loop(0, 2, one, 0)
    for k in range(1, 4):
        weights_here(0, k)
    for k in range(4):
        lent_weights(1, k, lambda copy: copy.start())
        own_weights(1, k)
    lax.fori_loop(0, 2, two, 0)

    for slot in range(1, SLOTS):
        for k in range(4):
            weights_here(slot, k)

    def later(step, carry):
        l = slot_of(step)

        def weight_b(k, lanes=slice(None)):
            return later_weights[k][jnp.maximum(l, 1) - 1, :, lanes]

        one, two = layer(step, l, weight_b)
        lax.fori_loop(0, 2, one, 0)
        lax.fori_loop(0, 2, two, 0)
        return carry

    lax.fori_loop(1, steps, later, 0)

    for i in range(2):
        for k in range(4):
            lent_weights(i, k, lambda copy: copy.wait_send())
    for k in range(2):
        lent_params(k).wait_send()

    @pl.when(chip == 0)
    def _():
        for b in range(2):
            hand_on(b).wait_send()

    for b in range(2):
        keep_output(b, core).wait()
        give_output(b, mate_core).wait()


def shards(latents, segment_depth, shift_flags, w_qkv, w_out, w_up, w_down, gains, logit_scale,
           lon_n, lat_n):
    micro, levels, clat, clon, width = latents.shape
    cells = latents.reshape(micro, CELLS, width)
    small = jnp.concatenate(
        [shift_flags.astype(jnp.float32), logit_scale * LOG2E, jnp.zeros((2, 118), jnp.float32)],
        axis=1,
    ).reshape(2, 1, 128)
    table = jnp.asarray(moves())
    hbm = pl.BlockSpec(memory_space=pl.ANY)
    bf16, f32 = jnp.bfloat16, jnp.float32
    dma = pltpu.SemaphoreType.DMA
    def run(which):
        lengths = LENGTHS[which]
        return pl.pallas_call(
            functools.partial(kernel, lon_n, lat_n, lengths),
            out_shape=jax.ShapeDtypeStruct((micro, CELLS, width), f32),
            in_specs=[
                pl.BlockSpec(memory_space=pltpu.SMEM), hbm, hbm, hbm,
                pl.BlockSpec(memory_space=pltpu.VMEM), hbm, hbm, hbm, hbm,
            ],
            out_specs=hbm,
            scratch_shapes=[
                pltpu.VMEM((width, 3 * width), bf16),
                pltpu.VMEM((width, width), bf16),
                pltpu.VMEM((width, 4 * width), bf16),
                pltpu.VMEM((4 * width, width), bf16),
                pltpu.VMEM((SLOTS - 1, width, 3 * width), bf16),
                pltpu.VMEM((SLOTS - 1, width, width), bf16),
                pltpu.VMEM((SLOTS - 1, width, 4 * width), bf16),
                pltpu.VMEM((SLOTS - 1, 4 * width, width), bf16),
                pltpu.VMEM((SLOTS, 1, 128), f32),
                pltpu.VMEM((SLOTS, 2, width), f32),
                pltpu.VMEM((SLOTS, CELLS, TAKEN), bf16),
                pltpu.VMEM((SLOTS, CELLS, TAKEN), bf16),
                pltpu.VMEM((2, CELLS, width), f32),
                pltpu.VMEM((2, WIDE, width), bf16),
                pltpu.VMEM((2, 2 * EDGE, width), bf16),
                pltpu.VMEM((2, WIDE, width), bf16),
                pltpu.VMEM((2, 2, CELLS, width), f32),
                pltpu.VMEM((2, CELLS, width), bf16),
                pltpu.VMEM((2, CELLS, width), bf16),
                pltpu.VMEM((HALF, HALF), f32),
                pltpu.VMEM((256, 256), bf16),
                dma((SLOTS, 4)), dma((2, 4)), dma((2, 2)), dma((2,)),
                dma((2, 4)), dma((2, 4)), dma((2, 5)), dma((2, 5)),
                dma((2,)), dma((2,)), dma((2,)), dma((2, 2)), dma((2,)),
            ],
            compiler_params=pltpu.CompilerParams(
                collective_id=which, has_side_effects=True, vmem_limit_bytes=60 * 1024 * 1024
            ),
            cost_estimate=pl.CostEstimate(
                flops=16 * 2 * 10**9, bytes_accessed=20 * 10**6, transcendentals=10**7
            ),
        )

    operands = (segment_depth, cells, small, gains, table, w_qkv, w_out, w_up, w_down)
    lengths = segment_depth[0:2].sum(), segment_depth[2:4].sum()
    out = lax.switch(
        lengths[0] // 4 + 2 * (lengths[1] // 4),
        [run(which) for which in range(len(LENGTHS))],
        *operands,
    )
    return out.reshape(1, micro, levels, clat, clon, width)


def solution(mesh):
    placed = (
        P(None, None, "lat", "lon", None),
        P(),
        P("segment", None),
        P("segment", None, None),
        P("segment", None, None),
        P("segment", None, None),
        P("segment", None, None),
        P("segment", None, None),
        P("segment", None),
    )
    return jax.shard_map(
        functools.partial(shards, lon_n=mesh.shape["lon"], lat_n=mesh.shape["lat"]),
        mesh=mesh,
        in_specs=placed,
        out_specs=P("segment", None, None, "lat", "lon", None),
        check_vma=False,
    )
```

```python
import functools

import jax
import jax.numpy as jnp
import numpy as np
from jax import lax
from jax.experimental import pallas as pl
from jax.experimental.pallas import tpu as pltpu
from jax.sharding import PartitionSpec as P

MESH = pl.DeviceIdType.MESH
HALF = 144
CELLS = 2 * HALF
PART = HALF // 2
REACH = 80
EDGE = 48
AT_LON = CELLS
AT_BOTH = AT_LON + 2 * EDGE
TAKEN = AT_BOTH + EDGE
AT_LAT = TAKEN
WIDE = AT_LAT + 2 * REACH
SLOTS = 4
LENGTHS = ((3, 3), (4, 3), (3, 4))
LOG2E = 1.4426950408889634
BIG = 1e30


def moves():
    table = np.zeros((CELLS, 128), np.float32)
    for core in range(2):
        far_half = 1 - core
        for lat in range(2):
            for lon in range(2):
                which = core * 8 + lat * 2 + lon
                for at in range(CELLS):
                    window = at // 144 if core else 1 - at // 144
                    half, pair, cell = at % 144 // 72, at % 72 // 36, at % 36
                    level, row, column = cell // 18, cell % 18 // 6, cell % 6
                    column += (2 * window + pair) * 6 + lon * (6 - 12 * core)
                    across = column >= 24 or column < 0
                    edge_column = column - 24 if core == 0 else column + 24 - 16
                    along = lat == 1 and half == far_half
                    source = 1 - half if lat else half
                    edge = (level * 3 + row) * 8 + edge_column
                    if along and across:
                        take = AT_BOTH + edge
                    elif across:
                        take = AT_LON + source * EDGE + edge
                    else:
                        take = level * 144 + (source * 3 + row) * 24 + column
                    table[at, which] = take

                    level, row, column = at // 144, at % 144 // 24, at % 24
                    half, row = row // 3, row % 3
                    along = lat == 1 and half == core
                    source = 1 - half if lat else half
                    column -= lon * (6 - 12 * core)
                    across = column >= 24 or column < 0
                    column %= 24
                    window, pair = column // 12, column % 12 // 6
                    inside = source * 72 + pair * 36 + level * 18 + row * 6 + column % 6
                    if along and across:
                        take = AT_BOTH + inside - (0 if core else 96)
                    elif across:
                        take = AT_LON + source * EDGE + inside - source * 64 - (0 if core else 32)
                    else:
                        take = (window if core else 1 - window) * 144 + inside
                    table[at, which + 4] = take
    return table


def normed(values, gain, eps):
    mean = jnp.mean(values, axis=-1, keepdims=True)
    centred = values - mean
    var = jnp.mean(centred * centred, axis=-1, keepdims=True)
    return centred * lax.rsqrt(var + eps) * gain


def twice_gelu(u):
    inner = u * (0.7978845608028654 + 0.035677408136300125 * (u * u))
    return u + u * jnp.tanh(inner)


def dot(a, b):
    return jnp.dot(a, b, preferred_element_type=jnp.float32)


def kernel(
    lon_n, lat_n, lengths, depth_ref, latents, small_in, gains_in, table, w_qkv, w_out, w_up, w_down, sections,
    wq_a, wo_a, wu_a, wd_a, wq_b, wo_b, wu_b, wd_b, small, gains, fwd, bwd, x, src, packed, ret, stage, hand_out, hand_in, cross, ones,
    w_recv, w_send, p_recv, p_send, f_recv, f_send, b_recv, b_send, in_sem, h_recv, h_send,
    o_recv, o_send,
):
    seg = lax.axis_index("segment")
    lon = lax.axis_index("lon")
    lat = lax.axis_index("lat")
    chip = seg // 2
    core = lax.rem(seg, 2)
    mate_core = 1 - core
    north, south = lax.rem(lat + lat_n - 1, lat_n), lax.rem(lat + 1, lat_n)
    west, east = lax.rem(lon + lon_n - 1, lon_n), lax.rem(lon + 1, lon_n)

    def device(s, o, a):
        return {"segment": s, "lon": o, "lat": a}

    out_lat, home_lat = north + core * (south - north), south + core * (north - south)
    out_lon, home_lon = west + core * (east - west), east + core * (west - east)
    to_n, to_s = device(seg, lon, out_lat), device(seg, lon, home_lat)
    to_w, to_e = device(seg, out_lon, lat), device(seg, home_lon, lat)
    to_nw, to_se = device(seg, out_lon, out_lat), device(seg, home_lon, home_lat)
    mate = device(chip * 2 + mate_core, lon, lat)
    other = device(lax.rem(seg + 2, 4), lon, lat)

    steps = lengths[0] + chip * (lengths[1] - lengths[0])
    depth = depth_ref[2 * chip]
    layers = depth + depth_ref[2 * chip + 1]

    first_weights = (wq_a, wo_a, wu_a, wd_a)
    later_weights = (wq_b, wo_b, wu_b, wd_b)
    held_weights = (w_qkv, w_out, w_up, w_down)

    def each_weight(i, k, act):
        if i == 1:
            act(held_weights[k].at[1], later_weights[k].at[2 * core])
            return

        @pl.when(core == 0)
        def _():
            act(held_weights[k].at[0], first_weights[k])

        @pl.when(core == 1)
        def _():
            act(held_weights[k].at[0], later_weights[k].at[1])

    def own_weights(i, k):
        slot = core * 2 + i
        each_weight(
            i, k,
            lambda held, kept: pltpu.make_async_copy(held, kept, w_recv.at[slot, k]).start(),
        )

    def lent_weights(i, k, act):
        slot = core * 2 + i
        each_weight(
            i, k,
            lambda held, kept: act(
                pltpu.make_async_remote_copy(
                    src_ref=held, dst_ref=kept, send_sem=w_send.at[i, k],
                    recv_sem=w_recv.at[slot, k], device_id=mate, device_id_type=MESH,
                )
            ),
        )

    def weights_here(slot, k):
        kept = first_weights[k] if slot == 0 else later_weights[k].at[slot - 1]
        pltpu.make_async_copy(held_weights[k].at[0], kept, w_recv.at[slot, k]).wait()

    tiny = ((small_in, small), (gains_in, gains))

    def own_params(k):
        held, kept = tiny[k]
        return pltpu.make_async_copy(held, kept.at[pl.ds(core * 2, 2)], p_recv.at[core, k])

    def lent_params(k):
        held, kept = tiny[k]
        return pltpu.make_async_remote_copy(
            src_ref=held, dst_ref=kept.at[pl.ds(core * 2, 2)], send_sem=p_send.at[k],
            recv_sem=p_recv.at[core, k], device_id=mate, device_id_type=MESH,
        )

    def edges(pieces, send, recv):
        return [
            pltpu.make_async_remote_copy(
                src_ref=source, dst_ref=target, send_sem=send.at[i], recv_sem=recv.at[i],
                device_id=to, device_id_type=MESH,
            )
            for i, (source, target, to) in enumerate(pieces)
        ]

    def rows_from(start, size):
        return pl.ds(pl.multiple_of(start, 16), size)

    def forth(b):
        return edges(
            (
                (packed.at[b, rows_from(EDGE * core, EDGE)], src.at[b, pl.ds(AT_BOTH, EDGE)], to_nw),
                (packed.at[b], src.at[b, pl.ds(AT_LON, 2 * EDGE)], to_w),
                (src.at[b, rows_from(64 * core, REACH)], src.at[b, pl.ds(AT_LAT, REACH)], to_n),
                (
                    src.at[b, rows_from(HALF + 64 * core, REACH)],
                    src.at[b, pl.ds(AT_LAT + REACH, REACH)], to_n,
                ),
            ),
            f_send.at[b], f_recv.at[b],
        )

    def back(b):
        return edges(
            (
                (ret.at[b, rows_from(96 - 96 * core, EDGE)], ret.at[b, pl.ds(AT_BOTH, EDGE)], to_se),
                (ret.at[b, rows_from(32 - 32 * core, EDGE)], ret.at[b, pl.ds(AT_LON, EDGE)], to_e),
                (
                    ret.at[b, rows_from(96 - 32 * core, EDGE)],
                    ret.at[b, pl.ds(AT_LON + EDGE, EDGE)], to_e,
                ),
                (ret.at[b, rows_from(64 - 64 * core, REACH)], ret.at[b, pl.ds(AT_LAT, REACH)], to_s),
                (
                    ret.at[b, rows_from(208 - 64 * core, REACH)],
                    ret.at[b, pl.ds(AT_LAT + REACH, REACH)], to_s,
                ),
            ),
            b_send.at[b], b_recv.at[b],
        )

    def edge_of(values, column):
        rows = [
            level * 144 + row * 24 + column
            for half in ((0, 1, 2), (3, 4, 5)) for level in (0, 1) for row in half
        ]
        return jnp.concatenate([values[r : r + 8] for r in rows], axis=0)

    def far_edge(values):
        return jnp.where(core == 0, edge_of(values, 0), edge_of(values, 16)).astype(jnp.bfloat16)

    def load_input(b):
        return pltpu.make_async_copy(
            latents.at[core + 2 * b], src.at[b, pl.ds(0, CELLS)], in_sem.at[b]
        )

    def hand_on(b):
        return pltpu.make_async_remote_copy(
            src_ref=hand_out.at[b], dst_ref=hand_in.at[b], send_sem=h_send.at[b],
            recv_sem=h_recv.at[b], device_id=other, device_id_type=MESH,
        )

    def keep_output(b, s):
        return pltpu.make_async_copy(
            stage.at[b, s], sections.at[core + 2 * b], o_recv.at[b, 0]
        )

    def give_output(b, s):
        return pltpu.make_async_remote_copy(
            src_ref=stage.at[b, s], dst_ref=sections.at[core + 2 * b], send_sem=o_send.at[b],
            recv_sem=o_recv.at[b, 1], device_id=mate, device_id_type=MESH,
        )

    barrier = pltpu.get_barrier_semaphore()
    for k in range(4):
        own_weights(0, k)
    for k in range(2):
        own_params(k).start()

    @pl.when(chip == 0)
    def _():
        for b in range(2):
            load_input(b).start()

    for to in (to_n, to_s, to_w, to_e, to_nw, to_se, mate, other):
        pl.semaphore_signal(barrier, inc=1, device_id=to, device_id_type=MESH)
    pl.semaphore_wait(barrier, 8)

    for k in range(2):
        lent_params(k).start()
    for k in range(4):
        lent_weights(0, k, lambda copy: copy.start())

    @pl.when(chip == 0)
    def _():
        for b in range(2):
            load_input(b).wait()
            entry = src[b, 0:CELLS].astype(jnp.float32)
            x[b] = entry
            packed[b] = far_edge(entry)
            for copy in forth(b):
                copy.start()

    @pl.when(chip == 1)
    def _():
        for b in range(2):
            hand_on(b).wait_recv()
            src[b, 0:CELLS] = hand_in[b]
            entry = hand_in[b].astype(jnp.float32)
            x[b] = entry
            packed[b] = far_edge(entry)
            for copy in forth(b):
                copy.start()

    for k, (held, kept) in enumerate(tiny):
        own_params(k).wait()
        pltpu.make_async_copy(
            held, kept.at[pl.ds(mate_core * 2, 2)], p_recv.at[mate_core, k]
        ).wait()

    rows = lax.broadcasted_iota(jnp.int32, (HALF, HALF), 0)
    cols = lax.broadcasted_iota(jnp.int32, (HALF, HALF), 1)
    split = (rows < PART) != (cols < PART)
    is_last = jnp.where(lat == (lat_n - 1) * (1 - core), 1.0, 0.0)
    cross[...] = jnp.where(split, -BIG, 0.0) * is_last
    r256 = lax.broadcasted_iota(jnp.int32, (256, 256), 0)
    c256 = lax.broadcasted_iota(jnp.int32, (256, 256), 1)
    ones[...] = jnp.where(r256 // 64 == c256 // 64, 1.0, 0.0).astype(jnp.bfloat16)

    place = lax.broadcasted_iota(jnp.int32, (CELLS, TAKEN), 1).astype(jnp.float32)

    def slot_of(step):
        return jnp.clip(step + jnp.where(step == 0, 0, 2 - depth), 0, SLOTS - 1)

    def choose(step, carry):
        f_lat = small[slot_of(step), 0:1, 0:1]
        f_lon = small[slot_of(step), 0:1, 1:2]
        picks = (
            (1.0 - f_lat) * (1.0 - f_lon), (1.0 - f_lat) * f_lon,
            f_lat * (1.0 - f_lon), f_lat * f_lon,
        )
        for first, kept in ((0, fwd), (4, bwd)):
            at = sum(
                jnp.where(
                    core == 0, table[:, first + i : first + i + 1],
                    table[:, first + i + 8 : first + i + 9],
                ) * picks[i]
                for i in range(4)
            )
            kept[step] = jnp.where(place == at, 1.0, 0.0).astype(jnp.bfloat16)
        return carry

    lax.fori_loop(0, steps, choose, 0)

    lane = lax.broadcasted_iota(jnp.int32, (1, 256), 1)
    masks = [jnp.where(lane // 64 == h, 1.0, 0.0).astype(jnp.bfloat16) for h in range(4)]
    first_of_pair = lax.broadcasted_iota(jnp.int32, (HALF, 128), 1) < 64

    def unit(block):
        total = dot((block * block).astype(jnp.bfloat16), ones[...])
        return (block * lax.rsqrt(total + 1e-06)).astype(jnp.bfloat16)

    reach_row = lax.broadcasted_iota(jnp.int32, (REACH, 1), 0)

    def replace_rows(buf, b, l, far):
        kept = (reach_row >= 8 * far) & (reach_row < PART + 8 * far)
        theirs = jnp.where(kept, small[l, 0:1, 0:1], 0.0)
        ours = (1.0 - theirs).astype(jnp.bfloat16)
        theirs = theirs.astype(jnp.bfloat16)
        for i in range(2):
            at = rows_from(i * HALF + 64 * far, REACH)
            came = buf[b, AT_LAT + i * REACH : AT_LAT + (i + 1) * REACH]
            buf[b, at] = buf[b, at] * ours + came * theirs

    def attend(b, step, l, weight):
        bias = small[l, 0:1, 0:1] * cross[...]

        def project(cells):
            quads = []
            for g in range(2):
                lanes = [slice(p * 512 + g * 256, p * 512 + g * 256 + 256) for p in range(3)]
                q = unit(dot(cells, weight(0, lanes[0])))
                k = unit(dot(cells, weight(0, lanes[1])))
                quads.append((q, k, dot(cells, weight(0, lanes[2])).astype(jnp.bfloat16)))
            return quads

        arrivals = forth(b)
        for copy in arrivals[2:]:
            copy.wait()
        replace_rows(src, b, l, core)
        near = project(dot(fwd[step, HALF:, 0:CELLS], src[b, 0:CELLS]).astype(jnp.bfloat16))
        for copy in arrivals[:2]:
            copy.wait()
        far = project(dot(fwd[step, 0:HALF], src[b, 0:TAKEN]).astype(jnp.bfloat16))
        copies = back(b)
        for w, quads in enumerate((far, near)):
            part = slice(w * HALF, w * HALF + HALF)
            done = []
            for g, (q, k, v) in enumerate(quads):
                heads = jnp.concatenate([q * masks[h] for h in range(4)], axis=0)
                scores = lax.dot_general(
                    heads, k, (((1,), (1,)), ((), ())), preferred_element_type=jnp.float32
                )
                expos, shares = [], []
                for h in range(4):
                    scale = small[l, 0:1, 2 + g * 4 + h : 3 + g * 4 + h]
                    score = scores[h * HALF : h * HALF + HALF] * scale + bias
                    expo = jnp.exp2(score - jnp.max(score, axis=-1, keepdims=True))
                    total = jnp.sum(expo, axis=-1, keepdims=True)
                    share = pl.reciprocal(total, approx=True)
                    shares.append(share * (2.0 - total * share))
                    expos.append(expo.astype(jnp.bfloat16))
                mixed = dot(jnp.concatenate(expos, axis=0), v)
                for p in range(2):
                    at = slice(p * 128, p * 128 + 128)
                    one = mixed[2 * p * HALF : (2 * p + 1) * HALF, at] * shares[2 * p]
                    two = mixed[(2 * p + 1) * HALF : (2 * p + 2) * HALF, at] * shares[2 * p + 1]
                    done.append(jnp.where(first_of_pair, one, two).astype(jnp.bfloat16))
            ret[b, part] = jnp.concatenate(done, axis=1)
            for copy in copies[:3] if w == 0 else copies[3:]:
                copy.start()

    def feed(b, step, l, weight):
        for copy in back(b):
            copy.wait()
        replace_rows(ret, b, l, 1 - core)
        mixed = dot(bwd[step], ret[b, 0:TAKEN]).astype(jnp.bfloat16)
        state = x[b]
        first = state + normed(dot(mixed, weight(1)), gains[l, 0:1], 1e-05)
        firstb = first.astype(jnp.bfloat16)
        hidden = jnp.concatenate(
            [
                twice_gelu(dot(firstb, weight(2, slice(c, c + 256)))).astype(jnp.bfloat16)
                for c in range(0, 2048, 256)
            ],
            axis=1,
        )
        fresh = first + normed(dot(hidden, weight(3)), gains[l, 1:2], 4e-05)
        fresh = jnp.where(step < layers, fresh, state)
        x[b] = fresh

        @pl.when(step < steps - 1)
        def _():
            copies = forth(b)
            packed[b] = far_edge(fresh)
            for copy in copies[:2]:
                copy.start()
            src[b, 0:CELLS] = fresh.astype(jnp.bfloat16)
            for copy in copies[2:]:
                copy.start()

        def emit(s, value):
            stage[b, s] = value

            @pl.when(s == core)
            def _():
                keep_output(b, s).start()

            @pl.when(s != core)
            def _():
                give_output(b, s).start()

        @pl.when(step == 1)
        def _():
            emit(0, jnp.where(depth == 1, state, fresh))

        @pl.when(step == steps - 1)
        def _():
            emit(1, fresh)

            @pl.when(chip == 0)
            def _():
                hand_out[b] = fresh.astype(jnp.bfloat16)
                hand_on(b).start()

    def layer(step, l, weight):
        def one(b, c):
            attend(b, step, l, weight)
            return c

        def two(b, c):
            feed(b, step, l, weight)
            return c

        return one, two

    def weight_a(k, lanes=slice(None)):
        return first_weights[k][:, lanes]

    weights_here(0, 0)
    one, two = layer(0, 0, weight_a)
    lax.fori_loop(0, 2, one, 0)
    for k in range(1, 4):
        weights_here(0, k)
    for k in range(4):
        lent_weights(1, k, lambda copy: copy.start())
        own_weights(1, k)
    lax.fori_loop(0, 2, two, 0)

    for slot in range(1, SLOTS):
        for k in range(4):
            weights_here(slot, k)

    def later(step, carry):
        l = slot_of(step)

        def weight_b(k, lanes=slice(None)):
            return later_weights[k][jnp.maximum(l, 1) - 1, :, lanes]

        one, two = layer(step, l, weight_b)
        lax.fori_loop(0, 2, one, 0)
        lax.fori_loop(0, 2, two, 0)
        return carry

    lax.fori_loop(1, steps, later, 0)

    for i in range(2):
        for k in range(4):
            lent_weights(i, k, lambda copy: copy.wait_send())
    for k in range(2):
        lent_params(k).wait_send()

    @pl.when(chip == 0)
    def _():
        for b in range(2):
            hand_on(b).wait_send()

    for b in range(2):
        keep_output(b, core).wait()
        give_output(b, mate_core).wait()


def shards(latents, segment_depth, shift_flags, w_qkv, w_out, w_up, w_down, gains, logit_scale,
           lon_n, lat_n):
    micro, levels, clat, clon, width = latents.shape
    cells = latents.reshape(micro, CELLS, width)
    small = jnp.concatenate(
        [shift_flags.astype(jnp.float32), logit_scale * LOG2E, jnp.zeros((2, 118), jnp.float32)],
        axis=1,
    ).reshape(2, 1, 128)
    table = jnp.asarray(moves())
    hbm = pl.BlockSpec(memory_space=pl.ANY)
    bf16, f32 = jnp.bfloat16, jnp.float32
    dma = pltpu.SemaphoreType.DMA
    def run(which):
        lengths = LENGTHS[which]
        return pl.pallas_call(
            functools.partial(kernel, lon_n, lat_n, lengths),
            out_shape=jax.ShapeDtypeStruct((micro, CELLS, width), f32),
            in_specs=[
                pl.BlockSpec(memory_space=pltpu.SMEM), hbm, hbm, hbm,
                pl.BlockSpec(memory_space=pltpu.VMEM), hbm, hbm, hbm, hbm,
            ],
            out_specs=hbm,
            scratch_shapes=[
                pltpu.VMEM((width, 3 * width), bf16),
                pltpu.VMEM((width, width), bf16),
                pltpu.VMEM((width, 4 * width), bf16),
                pltpu.VMEM((4 * width, width), bf16),
                pltpu.VMEM((SLOTS - 1, width, 3 * width), bf16),
                pltpu.VMEM((SLOTS - 1, width, width), bf16),
                pltpu.VMEM((SLOTS - 1, width, 4 * width), bf16),
                pltpu.VMEM((SLOTS - 1, 4 * width, width), bf16),
                pltpu.VMEM((SLOTS, 1, 128), f32),
                pltpu.VMEM((SLOTS, 2, width), f32),
                pltpu.VMEM((SLOTS, CELLS, TAKEN), bf16),
                pltpu.VMEM((SLOTS, CELLS, TAKEN), bf16),
                pltpu.VMEM((2, CELLS, width), f32),
                pltpu.VMEM((2, WIDE, width), bf16),
                pltpu.VMEM((2, 2 * EDGE, width), bf16),
                pltpu.VMEM((2, WIDE, width), bf16),
                pltpu.VMEM((2, 2, CELLS, width), f32),
                pltpu.VMEM((2, CELLS, width), bf16),
                pltpu.VMEM((2, CELLS, width), bf16),
                pltpu.VMEM((HALF, HALF), f32),
                pltpu.VMEM((256, 256), bf16),
                dma((SLOTS, 4)), dma((2, 4)), dma((2, 2)), dma((2,)),
                dma((2, 4)), dma((2, 4)), dma((2, 5)), dma((2, 5)),
                dma((2,)), dma((2,)), dma((2,)), dma((2, 2)), dma((2,)),
            ],
            compiler_params=pltpu.CompilerParams(
                collective_id=which, has_side_effects=True, vmem_limit_bytes=60 * 1024 * 1024
            ),
            cost_estimate=pl.CostEstimate(
                flops=16 * 2 * 10**9, bytes_accessed=20 * 10**6, transcendentals=10**7
            ),
        )

    operands = (segment_depth, cells, small, gains, table, w_qkv, w_out, w_up, w_down)
    lengths = segment_depth[0:2].sum(), segment_depth[2:4].sum()
    out = lax.switch(
        lengths[0] // 4 + 2 * (lengths[1] // 4),
        [run(which) for which in range(len(LENGTHS))],
        *operands,
    )
    return out.reshape(1, micro, levels, clat, clon, width)


def solution(mesh):
    placed = (
        P(None, None, "lat", "lon", None),
        P(),
        P("segment", None),
        P("segment", None, None),
        P("segment", None, None),
        P("segment", None, None),
        P("segment", None, None),
        P("segment", None, None),
        P("segment", None),
    )
    return jax.shard_map(
        functools.partial(shards, lon_n=mesh.shape["lon"], lat_n=mesh.shape["lat"]),
        mesh=mesh,
        in_specs=placed,
        out_specs=P("segment", None, None, "lat", "lon", None),
        check_vma=False,
    )
```

```python
import functools

import jax
import jax.numpy as jnp
import numpy as np
from jax import lax
from jax.experimental import pallas as pl
from jax.experimental.pallas import tpu as pltpu
from jax.sharding import PartitionSpec as P

MESH = pl.DeviceIdType.MESH
HALF = 144
CELLS = 2 * HALF
PART = HALF // 2
REACH = 80
EDGE = 48
AT_LON = CELLS
AT_BOTH = AT_LON + 2 * EDGE
TAKEN = AT_BOTH + EDGE
AT_LAT = TAKEN
WIDE = AT_LAT + 2 * REACH
SLOTS = 4
LENGTHS = ((3, 3), (4, 3), (3, 4))
LOG2E = 1.4426950408889634
BIG = 1e30


def moves():
    table = np.zeros((CELLS, 128), np.float32)
    for core in range(2):
        far_half = 1 - core
        for lat in range(2):
            for lon in range(2):
                which = core * 8 + lat * 2 + lon
                for at in range(CELLS):
                    window = at // 144 if core else 1 - at // 144
                    half, pair, cell = at % 144 // 72, at % 72 // 36, at % 36
                    level, row, column = cell // 18, cell % 18 // 6, cell % 6
                    column += (2 * window + pair) * 6 + lon * (6 - 12 * core)
                    across = column >= 24 or column < 0
                    edge_column = column - 24 if core == 0 else column + 24 - 16
                    along = lat == 1 and half == far_half
                    source = 1 - half if lat else half
                    edge = (level * 3 + row) * 8 + edge_column
                    if along and across:
                        take = AT_BOTH + edge
                    elif across:
                        take = AT_LON + source * EDGE + edge
                    else:
                        take = level * 144 + (source * 3 + row) * 24 + column
                    table[at, which] = take

                    level, row, column = at // 144, at % 144 // 24, at % 24
                    half, row = row // 3, row % 3
                    along = lat == 1 and half == core
                    source = 1 - half if lat else half
                    column -= lon * (6 - 12 * core)
                    across = column >= 24 or column < 0
                    column %= 24
                    window, pair = column // 12, column % 12 // 6
                    inside = source * 72 + pair * 36 + level * 18 + row * 6 + column % 6
                    if along and across:
                        take = AT_BOTH + inside - (0 if core else 96)
                    elif across:
                        take = AT_LON + source * EDGE + inside - source * 64 - (0 if core else 32)
                    else:
                        take = (window if core else 1 - window) * 144 + inside
                    table[at, which + 4] = take
    return table


def normed(values, gain, eps):
    mean = jnp.mean(values, axis=-1, keepdims=True)
    centred = values - mean
    var = jnp.mean(centred * centred, axis=-1, keepdims=True)
    return centred * lax.rsqrt(var + eps) * gain


def twice_gelu(u):
    inner = u * (0.7978845608028654 + 0.035677408136300125 * (u * u))
    return u + u * jnp.tanh(inner)


def dot(a, b):
    return jnp.dot(a, b, preferred_element_type=jnp.float32)


def kernel(
    lon_n, lat_n, lengths, depth_ref, latents, small_in, gains_in, table, w_qkv, w_out, w_up, w_down, sections,
    wq_a, wo_a, wu_a, wd_a, wq_b, wo_b, wu_b, wd_b, small, gains, fwd, bwd, x, src, packed, ret, stage, hand_out, hand_in, cross, ones,
    w_recv, w_send, p_recv, p_send, f_recv, f_send, b_recv, b_send, in_sem, h_recv, h_send,
    o_recv, o_send,
):
    seg = lax.axis_index("segment")
    lon = lax.axis_index("lon")
    lat = lax.axis_index("lat")
    chip = seg // 2
    core = lax.rem(seg, 2)
    mate_core = 1 - core
    north, south = lax.rem(lat + lat_n - 1, lat_n), lax.rem(lat + 1, lat_n)
    west, east = lax.rem(lon + lon_n - 1, lon_n), lax.rem(lon + 1, lon_n)

    def device(s, o, a):
        return {"segment": s, "lon": o, "lat": a}

    out_lat, home_lat = north + core * (south - north), south + core * (north - south)
    out_lon, home_lon = west + core * (east - west), east + core * (west - east)
    to_n, to_s = device(seg, lon, out_lat), device(seg, lon, home_lat)
    to_w, to_e = device(seg, out_lon, lat), device(seg, home_lon, lat)
    to_nw, to_se = device(seg, out_lon, out_lat), device(seg, home_lon, home_lat)
    mate = device(chip * 2 + mate_core, lon, lat)
    other = device(lax.rem(seg + 2, 4), lon, lat)

    steps = lengths[0] + chip * (lengths[1] - lengths[0])
    depth = depth_ref[2 * chip]
    layers = depth + depth_ref[2 * chip + 1]

    first_weights = (wq_a, wo_a, wu_a, wd_a)
    later_weights = (wq_b, wo_b, wu_b, wd_b)
    held_weights = (w_qkv, w_out, w_up, w_down)

    def each_weight(i, k, act):
        if i == 1:
            act(held_weights[k].at[1], later_weights[k].at[2 * core])
            return

        @pl.when(core == 0)
        def _():
            act(held_weights[k].at[0], first_weights[k])

        @pl.when(core == 1)
        def _():
            act(held_weights[k].at[0], later_weights[k].at[1])

    def own_weights(i, k):
        slot = core * 2 + i
        each_weight(
            i, k,
            lambda held, kept: pltpu.make_async_copy(held, kept, w_recv.at[slot, k]).start(),
        )

    def lent_weights(i, k, act):
        slot = core * 2 + i
        each_weight(
            i, k,
            lambda held, kept: act(
                pltpu.make_async_remote_copy(
                    src_ref=held, dst_ref=kept, send_sem=w_send.at[i, k],
                    recv_sem=w_recv.at[slot, k], device_id=mate, device_id_type=MESH,
                )
            ),
        )

    def weights_here(slot, k):
        kept = first_weights[k] if slot == 0 else later_weights[k].at[slot - 1]
        pltpu.make_async_copy(held_weights[k].at[0], kept, w_recv.at[slot, k]).wait()

    tiny = ((small_in, small), (gains_in, gains))

    def own_params(k):
        held, kept = tiny[k]
        return pltpu.make_async_copy(held, kept.at[pl.ds(core * 2, 2)], p_recv.at[core, k])

    def lent_params(k):
        held, kept = tiny[k]
        return pltpu.make_async_remote_copy(
            src_ref=held, dst_ref=kept.at[pl.ds(core * 2, 2)], send_sem=p_send.at[k],
            recv_sem=p_recv.at[core, k], device_id=mate, device_id_type=MESH,
        )

    def edges(pieces, send, recv):
        return [
            pltpu.make_async_remote_copy(
                src_ref=source, dst_ref=target, send_sem=send.at[i], recv_sem=recv.at[i],
                device_id=to, device_id_type=MESH,
            )
            for i, (source, target, to) in enumerate(pieces)
        ]

    def rows_from(start, size):
        return pl.ds(pl.multiple_of(start, 16), size)

    def forth(b):
        return edges(
            (
                (packed.at[b, rows_from(EDGE * core, EDGE)], src.at[b, pl.ds(AT_BOTH, EDGE)], to_nw),
                (packed.at[b], src.at[b, pl.ds(AT_LON, 2 * EDGE)], to_w),
                (src.at[b, rows_from(64 * core, REACH)], src.at[b, pl.ds(AT_LAT, REACH)], to_n),
                (
                    src.at[b, rows_from(HALF + 64 * core, REACH)],
                    src.at[b, pl.ds(AT_LAT + REACH, REACH)], to_n,
                ),
            ),
            f_send.at[b], f_recv.at[b],
        )

    def back(b):
        return edges(
            (
                (ret.at[b, rows_from(96 - 96 * core, EDGE)], ret.at[b, pl.ds(AT_BOTH, EDGE)], to_se),
                (ret.at[b, rows_from(32 - 32 * core, EDGE)], ret.at[b, pl.ds(AT_LON, EDGE)], to_e),
                (
                    ret.at[b, rows_from(96 - 32 * core, EDGE)],
                    ret.at[b, pl.ds(AT_LON + EDGE, EDGE)], to_e,
                ),
                (ret.at[b, rows_from(64 - 64 * core, REACH)], ret.at[b, pl.ds(AT_LAT, REACH)], to_s),
                (
                    ret.at[b, rows_from(208 - 64 * core, REACH)],
                    ret.at[b, pl.ds(AT_LAT + REACH, REACH)], to_s,
                ),
            ),
            b_send.at[b], b_recv.at[b],
        )

    def edge_of(values, column):
        rows = [
            level * 144 + row * 24 + column
            for half in ((0, 1, 2), (3, 4, 5)) for level in (0, 1) for row in half
        ]
        return jnp.concatenate([values[r : r + 8] for r in rows], axis=0)

    def far_edge(values):
        return jnp.where(core == 0, edge_of(values, 0), edge_of(values, 16)).astype(jnp.bfloat16)

    def load_input(b):
        return pltpu.make_async_copy(
            latents.at[core + 2 * b], src.at[b, pl.ds(0, CELLS)], in_sem.at[b]
        )

    def hand_on(b):
        return pltpu.make_async_remote_copy(
            src_ref=hand_out.at[b], dst_ref=hand_in.at[b], send_sem=h_send.at[b],
            recv_sem=h_recv.at[b], device_id=other, device_id_type=MESH,
        )

    def keep_output(b, s):
        return pltpu.make_async_copy(
            stage.at[b, s], sections.at[core + 2 * b], o_recv.at[b, 0]
        )

    def give_output(b, s):
        return pltpu.make_async_remote_copy(
            src_ref=stage.at[b, s], dst_ref=sections.at[core + 2 * b], send_sem=o_send.at[b],
            recv_sem=o_recv.at[b, 1], device_id=mate, device_id_type=MESH,
        )

    barrier = pltpu.get_barrier_semaphore()
    for k in range(4):
        own_weights(0, k)
    for k in range(2):
        own_params(k).start()

    @pl.when(chip == 0)
    def _():
        for b in range(2):
            load_input(b).start()

    for to in (to_n, to_s, to_w, to_e, to_nw, to_se, mate, other):
        pl.semaphore_signal(barrier, inc=1, device_id=to, device_id_type=MESH)
    pl.semaphore_wait(barrier, 8)

    for k in range(2):
        lent_params(k).start()
    for k in range(4):
        lent_weights(0, k, lambda copy: copy.start())

    @pl.when(chip == 0)
    def _():
        for b in range(2):
            load_input(b).wait()
            entry = src[b, 0:CELLS].astype(jnp.float32)
            x[b] = entry
            packed[b] = far_edge(entry)
            for copy in forth(b):
                copy.start()

    @pl.when(chip == 1)
    def _():
        for b in range(2):
            hand_on(b).wait_recv()
            src[b, 0:CELLS] = hand_in[b]
            entry = hand_in[b].astype(jnp.float32)
            x[b] = entry
            packed[b] = far_edge(entry)
            for copy in forth(b):
                copy.start()

    for k, (held, kept) in enumerate(tiny):
        own_params(k).wait()
        pltpu.make_async_copy(
            held, kept.at[pl.ds(mate_core * 2, 2)], p_recv.at[mate_core, k]
        ).wait()

    rows = lax.broadcasted_iota(jnp.int32, (HALF, HALF), 0)
    cols = lax.broadcasted_iota(jnp.int32, (HALF, HALF), 1)
    split = (rows < PART) != (cols < PART)
    is_last = jnp.where(lat == (lat_n - 1) * (1 - core), 1.0, 0.0)
    cross[...] = jnp.where(split, -BIG, 0.0) * is_last
    r256 = lax.broadcasted_iota(jnp.int32, (256, 256), 0)
    c256 = lax.broadcasted_iota(jnp.int32, (256, 256), 1)
    ones[...] = jnp.where(r256 // 64 == c256 // 64, 1.0, 0.0).astype(jnp.bfloat16)

    place = lax.broadcasted_iota(jnp.int32, (CELLS, TAKEN), 1).astype(jnp.float32)

    def slot_of(step):
        return jnp.clip(step + jnp.where(step == 0, 0, 2 - depth), 0, SLOTS - 1)

    def choose(step, carry):
        f_lat = small[slot_of(step), 0:1, 0:1]
        f_lon = small[slot_of(step), 0:1, 1:2]
        picks = (
            (1.0 - f_lat) * (1.0 - f_lon), (1.0 - f_lat) * f_lon,
            f_lat * (1.0 - f_lon), f_lat * f_lon,
        )
        for first, kept in ((0, fwd), (4, bwd)):
            at = sum(
                jnp.where(
                    core == 0, table[:, first + i : first + i + 1],
                    table[:, first + i + 8 : first + i + 9],
                ) * picks[i]
                for i in range(4)
            )
            kept[step] = jnp.where(place == at, 1.0, 0.0).astype(jnp.bfloat16)
        return carry

    lax.fori_loop(0, steps, choose, 0)

    lane = lax.broadcasted_iota(jnp.int32, (1, 256), 1)
    masks = [jnp.where(lane // 64 == h, 1.0, 0.0).astype(jnp.bfloat16) for h in range(4)]
    first_of_pair = lax.broadcasted_iota(jnp.int32, (HALF, 128), 1) < 64

    def unit(block):
        total = dot((block * block).astype(jnp.bfloat16), ones[...])
        return (block * lax.rsqrt(total + 1e-06)).astype(jnp.bfloat16)

    reach_row = lax.broadcasted_iota(jnp.int32, (REACH, 1), 0)

    def replace_rows(buf, b, l, far):
        kept = (reach_row >= 8 * far) & (reach_row < PART + 8 * far)
        theirs = jnp.where(kept, small[l, 0:1, 0:1], 0.0)
        ours = (1.0 - theirs).astype(jnp.bfloat16)
        theirs = theirs.astype(jnp.bfloat16)
        for i in range(2):
            at = rows_from(i * HALF + 64 * far, REACH)
            came = buf[b, AT_LAT + i * REACH : AT_LAT + (i + 1) * REACH]
            buf[b, at] = buf[b, at] * ours + came * theirs

    def attend(b, step, l, weight):
        bias = small[l, 0:1, 0:1] * cross[...]

        def project(cells):
            quads = []
            for g in range(2):
                lanes = [slice(p * 512 + g * 256, p * 512 + g * 256 + 256) for p in range(3)]
                q = unit(dot(cells, weight(0, lanes[0])))
                k = unit(dot(cells, weight(0, lanes[1])))
                quads.append((q, k, dot(cells, weight(0, lanes[2])).astype(jnp.bfloat16)))
            return quads

        arrivals = forth(b)
        for copy in arrivals[2:]:
            copy.wait()
        replace_rows(src, b, l, core)
        near = project(dot(fwd[step, HALF:, 0:CELLS], src[b, 0:CELLS]).astype(jnp.bfloat16))
        for copy in arrivals[:2]:
            copy.wait()
        far = project(dot(fwd[step, 0:HALF], src[b, 0:TAKEN]).astype(jnp.bfloat16))
        copies = back(b)
        for w, quads in enumerate((far, near)):
            part = slice(w * HALF, w * HALF + HALF)
            done = []
            for g, (q, k, v) in enumerate(quads):
                heads = jnp.concatenate([q * masks[h] for h in range(4)], axis=0)
                scores = lax.dot_general(
                    heads, k, (((1,), (1,)), ((), ())), preferred_element_type=jnp.float32
                )
                expos, shares = [], []
                for h in range(4):
                    scale = small[l, 0:1, 2 + g * 4 + h : 3 + g * 4 + h]
                    score = scores[h * HALF : h * HALF + HALF] * scale + bias
                    expo = jnp.exp2(score - jnp.max(score, axis=-1, keepdims=True))
                    total = jnp.sum(expo, axis=-1, keepdims=True)
                    share = pl.reciprocal(total, approx=True)
                    shares.append(share * (2.0 - total * share))
                    expos.append(expo.astype(jnp.bfloat16))
                mixed = dot(jnp.concatenate(expos, axis=0), v)
                for p in range(2):
                    at = slice(p * 128, p * 128 + 128)
                    one = mixed[2 * p * HALF : (2 * p + 1) * HALF, at] * shares[2 * p]
                    two = mixed[(2 * p + 1) * HALF : (2 * p + 2) * HALF, at] * shares[2 * p + 1]
                    done.append(jnp.where(first_of_pair, one, two).astype(jnp.bfloat16))
            ret[b, part] = jnp.concatenate(done, axis=1)
            for copy in copies[:3] if w == 0 else copies[3:]:
                copy.start()

    def feed(b, step, l, weight):
        arrivals = back(b)
        for copy in arrivals[3:]:
            copy.wait()
        for copy in arrivals[:3]:
            copy.wait_send()
        replace_rows(ret, b, l, 1 - core)
        near = dot(bwd[step, :, 0:256], ret[b, 0:256])
        for copy in arrivals[:3]:
            copy.wait_recv()
        mixed = (near + dot(bwd[step, :, 256:TAKEN], ret[b, 256:TAKEN])).astype(jnp.bfloat16)
        state = x[b]
        first = state + normed(dot(mixed, weight(1)), gains[l, 0:1], 1e-05)
        firstb = first.astype(jnp.bfloat16)
        hidden = jnp.concatenate(
            [
                twice_gelu(dot(firstb, weight(2, slice(c, c + 256)))).astype(jnp.bfloat16)
                for c in range(0, 2048, 256)
            ],
            axis=1,
        )
        fresh = first + normed(dot(hidden, weight(3)), gains[l, 1:2], 4e-05)
        fresh = jnp.where(step < layers, fresh, state)
        x[b] = fresh

        @pl.when(step < steps - 1)
        def _():
            copies = forth(b)
            packed[b] = far_edge(fresh)
            for copy in copies[:2]:
                copy.start()
            src[b, 0:CELLS] = fresh.astype(jnp.bfloat16)
            for copy in copies[2:]:
                copy.start()

        def emit(s, value):
            stage[b, s] = value

            @pl.when(s == core)
            def _():
                keep_output(b, s).start()

            @pl.when(s != core)
            def _():
                give_output(b, s).start()

        @pl.when(step == 1)
        def _():
            emit(0, jnp.where(depth == 1, state, fresh))

        @pl.when(step == steps - 1)
        def _():
            emit(1, fresh)

            @pl.when(chip == 0)
            def _():
                hand_out[b] = fresh.astype(jnp.bfloat16)
                hand_on(b).start()

    def layer(step, l, weight):
        def one(b, c):
            attend(b, step, l, weight)
            return c

        def two(b, c):
            feed(b, step, l, weight)
            return c

        return one, two

    def weight_a(k, lanes=slice(None)):
        return first_weights[k][:, lanes]

    weights_here(0, 0)
    one, two = layer(0, 0, weight_a)
    lax.fori_loop(0, 2, one, 0)
    for k in range(1, 4):
        weights_here(0, k)
    for k in range(4):
        lent_weights(1, k, lambda copy: copy.start())
        own_weights(1, k)
    lax.fori_loop(0, 2, two, 0)

    for slot in range(1, SLOTS):
        for k in range(4):
            weights_here(slot, k)

    def later(step, carry):
        l = slot_of(step)

        def weight_b(k, lanes=slice(None)):
            return later_weights[k][jnp.maximum(l, 1) - 1, :, lanes]

        one, two = layer(step, l, weight_b)
        lax.fori_loop(0, 2, one, 0)
        lax.fori_loop(0, 2, two, 0)
        return carry

    lax.fori_loop(1, steps, later, 0)

    for i in range(2):
        for k in range(4):
            lent_weights(i, k, lambda copy: copy.wait_send())
    for k in range(2):
        lent_params(k).wait_send()

    @pl.when(chip == 0)
    def _():
        for b in range(2):
            hand_on(b).wait_send()

    for b in range(2):
        keep_output(b, core).wait()
        give_output(b, mate_core).wait()


def shards(latents, segment_depth, shift_flags, w_qkv, w_out, w_up, w_down, gains, logit_scale,
           lon_n, lat_n):
    micro, levels, clat, clon, width = latents.shape
    cells = latents.reshape(micro, CELLS, width)
    small = jnp.concatenate(
        [shift_flags.astype(jnp.float32), logit_scale * LOG2E, jnp.zeros((2, 118), jnp.float32)],
        axis=1,
    ).reshape(2, 1, 128)
    table = jnp.asarray(moves())
    hbm = pl.BlockSpec(memory_space=pl.ANY)
    bf16, f32 = jnp.bfloat16, jnp.float32
    dma = pltpu.SemaphoreType.DMA
    def run(which):
        lengths = LENGTHS[which]
        return pl.pallas_call(
            functools.partial(kernel, lon_n, lat_n, lengths),
            out_shape=jax.ShapeDtypeStruct((micro, CELLS, width), f32),
            in_specs=[
                pl.BlockSpec(memory_space=pltpu.SMEM), hbm, hbm, hbm,
                pl.BlockSpec(memory_space=pltpu.VMEM), hbm, hbm, hbm, hbm,
            ],
            out_specs=hbm,
            scratch_shapes=[
                pltpu.VMEM((width, 3 * width), bf16),
                pltpu.VMEM((width, width), bf16),
                pltpu.VMEM((width, 4 * width), bf16),
                pltpu.VMEM((4 * width, width), bf16),
                pltpu.VMEM((SLOTS - 1, width, 3 * width), bf16),
                pltpu.VMEM((SLOTS - 1, width, width), bf16),
                pltpu.VMEM((SLOTS - 1, width, 4 * width), bf16),
                pltpu.VMEM((SLOTS - 1, 4 * width, width), bf16),
                pltpu.VMEM((SLOTS, 1, 128), f32),
                pltpu.VMEM((SLOTS, 2, width), f32),
                pltpu.VMEM((SLOTS, CELLS, TAKEN), bf16),
                pltpu.VMEM((SLOTS, CELLS, TAKEN), bf16),
                pltpu.VMEM((2, CELLS, width), f32),
                pltpu.VMEM((2, WIDE, width), bf16),
                pltpu.VMEM((2, 2 * EDGE, width), bf16),
                pltpu.VMEM((2, WIDE, width), bf16),
                pltpu.VMEM((2, 2, CELLS, width), f32),
                pltpu.VMEM((2, CELLS, width), bf16),
                pltpu.VMEM((2, CELLS, width), bf16),
                pltpu.VMEM((HALF, HALF), f32),
                pltpu.VMEM((256, 256), bf16),
                dma((SLOTS, 4)), dma((2, 4)), dma((2, 2)), dma((2,)),
                dma((2, 4)), dma((2, 4)), dma((2, 5)), dma((2, 5)),
                dma((2,)), dma((2,)), dma((2,)), dma((2, 2)), dma((2,)),
            ],
            compiler_params=pltpu.CompilerParams(
                collective_id=which, has_side_effects=True, vmem_limit_bytes=60 * 1024 * 1024
            ),
            cost_estimate=pl.CostEstimate(
                flops=16 * 2 * 10**9, bytes_accessed=20 * 10**6, transcendentals=10**7
            ),
        )

    operands = (segment_depth, cells, small, gains, table, w_qkv, w_out, w_up, w_down)
    lengths = segment_depth[0:2].sum(), segment_depth[2:4].sum()
    out = lax.switch(
        lengths[0] // 4 + 2 * (lengths[1] // 4),
        [run(which) for which in range(len(LENGTHS))],
        *operands,
    )
    return out.reshape(1, micro, levels, clat, clon, width)


def solution(mesh):
    placed = (
        P(None, None, "lat", "lon", None),
        P(),
        P("segment", None),
        P("segment", None, None),
        P("segment", None, None),
        P("segment", None, None),
        P("segment", None, None),
        P("segment", None, None),
        P("segment", None),
    )
    return jax.shard_map(
        functools.partial(shards, lon_n=mesh.shape["lon"], lat_n=mesh.shape["lat"]),
        mesh=mesh,
        in_specs=placed,
        out_specs=P("segment", None, None, "lat", "lon", None),
        check_vma=False,
    )
```
